32 devices in a mesh: seq: 8 (over z, core), fsdp: 4 (over y, x).
Axes of the slice: x: 2, y: 2, z: 4, core: 2. Of those that a mesh axis runs over, the one named last changes fastest.
Arguments:
- tokens: bfloat16 [4, 1024, 1536], P('fsdp', 'seq'), may hold values from -6 to 6
- cotangent: bfloat16 [4, 1024, 1536], P('fsdp', 'seq'), may hold values from -6 to 6
- norm_gain: bfloat16 [2, 1536], P(None, ('seq', 'fsdp')), may hold values from 0.5 to 1.5
- in_weight: bfloat16 [2, 1536, 6448], P(None, ('seq', 'fsdp')), may hold values from -0.15625 to 0.15625
- conv_kernel: bfloat16 [2, 4, 3328], P(None, None, ('seq', 'fsdp')), may hold values from -3 to 3
- conv_shift: bfloat16 [2, 3328], P(None, ('seq', 'fsdp')), may hold values from -0.5 to 0.5
- dt_bias: float32 [2, 48], P(None, 'seq'), may hold values from -8 to -2.5
- a_log: float32 [2, 48], P(None, 'seq'), may hold values from 0 to 2.5
- skip_gain: float32 [2, 48], P(None, 'seq'), may hold values from 0.5 to 1.5
- gate_gain: bfloat16 [2, 3072], P(None, ('seq', 'fsdp')), may hold values from 0.5 to 1.5
- out_weight: bfloat16 [2, 3072, 1536], P(None, ('seq', 'fsdp')), may hold values from -0.109375 to 0.109375
Outputs:
- out: bfloat16 [4, 1024, 1536], P('fsdp', 'seq')
- grad_tokens: float32 [4, 1024, 1536], P('fsdp', 'seq')
- grad_norm_gain: float32 [2, 1536], P(None, ('seq', 'fsdp'))
- grad_in_weight: float32 [2, 1536, 6448], P(None, ('seq', 'fsdp'))
- grad_conv_kernel: float32 [2, 4, 3328], P(None, None, ('seq', 'fsdp'))
- grad_conv_shift: float32 [2, 3328], P(None, ('seq', 'fsdp'))
- grad_dt_bias: float32 [2, 48], P(None, 'seq')
- grad_a_log: float32 [2, 48], P(None, 'seq')
- grad_skip_gain: float32 [2, 48], P(None, 'seq')
- grad_gate_gain: float32 [2, 3072], P(None, ('seq', 'fsdp'))
- grad_out_weight: float32 [2, 3072, 1536], P(None, ('seq', 'fsdp'))
The draws below stay inside these ranges and needn't reach their ends.
All inputs are finite; a program needn't handle non-finite values.
Results may differ from the reference program's by a relative error of at most 0.02.
Values may be sent and summed in bfloat16 or wider, within the bound.
No kernel may reach another device: no remote copies, remote signals or barrier semaphores. Data moves between devices by JAX's collectives and lax.ppermute only.
A program may use at most 384 MiB of HBM per device.

```python
import jax
import jax.numpy as jnp
from jax import lax

D = 1536
HEADS = 48
HD = 64
NSTATE = 128
CONV = 4
STRETCH = 256
LAYERS = 2
DI = 3072
CONVDIM = 3328
PROJ = 6448
LENGTH = 1024
SEQS = 4


def levels(key, extent, cuts, least, high):
    gain, own = 1.0, jax.random.fold_in(key, 6)
    for axis_at, blocks in cuts:
        heights = jnp.exp(jax.random.uniform(jax.random.fold_in(own, axis_at), (blocks,), jnp.float32, least / len(cuts), high / len(cuts)))
        gain = gain * jnp.repeat(heights, extent[axis_at] // blocks).reshape([-1 if axis == axis_at else 1 for axis in range(len(extent))])
    return gain


def bell_draw(own_key, extent, spread, limit, split=(), kind=jnp.bfloat16):
    level = levels(own_key, extent, split, -0.22, 0.18) if split else 1.0
    drawn = jax.random.normal(own_key, extent, jnp.float32) * spread * level
    return jnp.minimum(jnp.maximum(drawn, -limit), limit).astype(kind)


def setup_inputs(seed: int = 0) -> dict:
    splits = jax.random.split(jax.random.key(seed), 12)
    return {
        "tokens": bell_draw(splits[0], (SEQS, LENGTH, D), 1.0, 6.0, ((0, 4), (1, 8))),
        "cotangent": bell_draw(splits[1], (SEQS, LENGTH, D), 1.0, 6.0, ((0, 4), (1, 8))),
        "norm_gain": jnp.clip(1.0 + 0.1 * jax.random.normal(splits[2], (LAYERS, D), jnp.float32), 0.5, 1.5).astype(jnp.bfloat16),
        "in_weight": bell_draw(splits[3], (LAYERS, D, PROJ), D ** -0.5, 0.15625, ((1, 32),)),
        "conv_kernel": bell_draw(splits[4], (LAYERS, CONV, CONVDIM), CONV ** -0.5, 3.0, ((2, 32),)),
        "conv_shift": jnp.clip(jax.random.uniform(splits[5], (LAYERS, CONVDIM), jnp.float32, -0.5, 0.5) * levels(splits[5], (LAYERS, CONVDIM), ((1, 32),), -0.4, 0.0), -0.5, 0.5).astype(jnp.bfloat16),
        "dt_bias": jnp.clip(-8.0 + 5.5 * jax.random.uniform(splits[6], (LAYERS, HEADS), jnp.float32) ** levels(splits[6], (LAYERS, HEADS), ((1, 8),), -0.2, 0.2), -8.0, -2.5),
        "a_log": jnp.clip(2.5 * jax.random.uniform(splits[7], (LAYERS, HEADS), jnp.float32) ** levels(splits[7], (LAYERS, HEADS), ((1, 8),), -0.2, 0.2), 0.0, 2.5),
        "skip_gain": jnp.clip(0.5 + 1.0 * jax.random.uniform(splits[8], (LAYERS, HEADS), jnp.float32) ** levels(splits[8], (LAYERS, HEADS), ((1, 8),), -0.2, 0.2), 0.5, 1.5),
        "gate_gain": jnp.clip(1.0 + 0.1 * jax.random.normal(splits[9], (LAYERS, DI), jnp.float32), 0.5, 1.5).astype(jnp.bfloat16),
        "out_weight": bell_draw(splits[10], (LAYERS, DI, D), DI ** -0.5, 0.109375, ((1, 32),)),
    }


eps = 1e-05

@jax.custom_vjp
def low(v):
    return lax.optimization_barrier(v.astype(jnp.bfloat16)).astype(jnp.float32)

@jax.custom_vjp
def low_back(v):
    return v

def low_keep(v):
    return (low(v), None)

def low_pass(kept, grad):
    return (grad,)

def back_keep(v):
    return (v, None)

def back_low(kept, grad):
    return (low(grad),)
low.defvjp(low_keep, low_pass)
low_back.defvjp(back_keep, back_low)

def matmul(left, right):
    return jnp.dot(left, right, precision=lax.Precision.HIGHEST, preferred_element_type=jnp.float32)

def product(form, left, right):
    return jnp.einsum(form, left, right, precision=lax.Precision.HIGHEST, preferred_element_type=jnp.float32)

def rms_scale(values, gain_row):
    return values * lax.rsqrt(lax.optimization_barrier(jnp.mean(values * values, axis=-1, keepdims=True)) + eps) * gain_row

def causal_conv(values, kernel, offset):
    width_conv = kernel.shape[0]
    padded = jnp.concatenate([jnp.zeros((width_conv - 1, values.shape[1]), jnp.float32), values], axis=0)
    result = offset
    for lag_at in range(width_conv):
        result = result + kernel[lag_at] * padded[lag_at:lag_at + values.shape[0]]
    return result

def stretch_step(state_in, pieces):
    inputs, step_sizes, log_decay, b_in, c_in = pieces
    block_len = inputs.shape[0]
    cumulative = jnp.cumsum(log_decay, axis=0)
    row_ids = lax.broadcasted_iota(jnp.int32, (block_len, block_len), 0)
    col_ids = lax.broadcasted_iota(jnp.int32, (block_len, block_len), 1)
    lower_mask = (row_ids >= col_ids)[:, :, None]
    gap_log = cumulative[:, None, :] - cumulative[None, :, :]
    weights = jnp.where(lower_mask, jnp.exp(jnp.where(lower_mask, gap_log, 0.0)), 0.0)
    scores = matmul(c_in, b_in.T)
    mixed_in = scores[:, :, None] * weights * step_sizes[None, :, :]
    within = product('ijh,jhp->ihp', mixed_in, inputs)
    carried = jnp.exp(cumulative)[:, :, None] * product('in,hpn->ihp', c_in, state_in)
    to_end = jnp.exp(cumulative[-1][None, :] - cumulative) * step_sizes
    fresh_state = product('jhp,jn->hpn', inputs * to_end[:, :, None], b_in)
    state_next = state_in * jnp.exp(cumulative[-1])[:, None, None] + fresh_state
    return (state_next, within + carried)

def state_space(head_in, step_sizes, log_decay, b_in, c_in):
    length, head_count, head_dim = head_in.shape
    stretch_count = length // STRETCH
    pieces = (head_in.reshape(stretch_count, STRETCH, head_count, head_dim), step_sizes.reshape(stretch_count, STRETCH, head_count), log_decay.reshape(stretch_count, STRETCH, head_count), b_in.reshape(stretch_count, STRETCH, b_in.shape[1]), c_in.reshape(stretch_count, STRETCH, c_in.shape[1]))
    start_state = jnp.zeros((head_count, head_dim, b_in.shape[1]), jnp.float32)
    _, blocks = lax.scan(jax.checkpoint(stretch_step), start_state, pieces)
    return blocks.reshape(length, head_count, head_dim)

def layer_forward(residual, gain_in, in_weight, conv_kernel, conv_shift, dt_bias, a_log, skip_gain, gain_gate, out_weight):
    length = residual.shape[0]
    normed = low(rms_scale(residual, gain_in))
    projected = low(low_back(matmul(normed, in_weight)))
    gate_in = projected[:, :DI]
    conv_out = jax.nn.silu(causal_conv(projected[:, DI:DI + CONVDIM], conv_kernel, conv_shift))
    dt_raw = projected[:, DI + CONVDIM:]
    step_sizes = jax.nn.softplus(dt_raw + dt_bias)
    log_decay = -step_sizes * jnp.exp(a_log)
    head_in = conv_out[:, :DI].reshape(length, HEADS, HD)
    result = state_space(head_in, step_sizes, log_decay, conv_out[:, DI:DI + NSTATE], conv_out[:, DI + NSTATE:])
    result = result + skip_gain[:, None] * head_in
    gated_out = low(low_back(result.reshape(length, DI) * jax.nn.silu(gate_in)))
    scaled = low(rms_scale(gated_out, gain_gate))
    return residual + low_back(matmul(scaled, out_weight))

def forward(tokens, norm_gain, in_weight, conv_kernel, conv_shift, dt_bias, a_log, skip_gain, gate_gain, out_weight):

    def one_sequence(carried_in, sequence):
        residual = sequence
        for current in range(LAYERS):
            residual = layer_forward(residual, norm_gain[current], in_weight[current], conv_kernel[current], conv_shift[current], dt_bias[current], a_log[current], skip_gain[current], gate_gain[current], out_weight[current])
        return (carried_in, residual)
    _, result = lax.scan(jax.checkpoint(one_sequence), jnp.zeros((), jnp.float32), tokens)
    return result

def reference(tokens, cotangent, norm_gain, in_weight, conv_kernel, conv_shift, dt_bias, a_log, skip_gain, gate_gain, out_weight):
    result, pullback = jax.vjp(forward, tokens.astype(jnp.float32), norm_gain.astype(jnp.float32), in_weight.astype(jnp.float32), conv_kernel.astype(jnp.float32), conv_shift.astype(jnp.float32), dt_bias.astype(jnp.float32), a_log.astype(jnp.float32), skip_gain.astype(jnp.float32), gate_gain.astype(jnp.float32), out_weight.astype(jnp.float32))
    gradients = pullback(cotangent.astype(jnp.float32))
    return (result.astype(jnp.bfloat16), gradients[0], gradients[1], gradients[2], gradients[3], gradients[4], gradients[5], gradients[6], gradients[7], gradients[8], gradients[9])
```

```python
import functools

import jax
import jax.numpy as jnp
from jax import lax
from jax.experimental import pallas as pl
from jax.experimental.pallas import tpu as pltpu
from jax.sharding import Mesh
from jax.sharding import PartitionSpec as P

HD = 64
NSTATE = 128
STRETCH = 256
DI = 3072
CONV = 4
LANES = 128
BC = 2 * NSTATE

eps = 1e-05

EVERY = ("a", "b", "c", "p", "q")
SEQ = ("a", "b", "c")
FSDP = ("p", "q")
TEAM = ("q", "b", "c")
COPIES = ("p", "a")
SWAP = [(0, 0), (1, 2), (2, 1), (3, 3)]

F32 = jnp.float32
BF16 = jnp.bfloat16
EXACT = lax.Precision.HIGHEST


def mm(left, right):
    return jnp.dot(left, right, preferred_element_type=F32)


def mm_nt(left, right):
    return lax.dot_general(left, right, (((1,), (1,)), ((), ())), preferred_element_type=F32)


def mm_tn(left, right):
    return lax.dot_general(left, right, (((0,), (0,)), ((), ())), preferred_element_type=F32)


def mm_exact(left, right):
    return jnp.dot(left, right, precision=EXACT, preferred_element_type=F32)


def iota(shape, dim):
    return lax.broadcasted_iota(jnp.int32, shape, dim)


def head_spread(width):
    return (iota((LANES, width), 0) == iota((LANES, width), 1) // HD).astype(F32)


def head_fold(width):
    return (iota((width, LANES), 0) // HD == iota((width, LANES), 1)).astype(F32)


def steps_of(raw, head_rows):
    shifted = raw + head_rows[0:1]
    step = jnp.maximum(shifted, 0.0) + jnp.log1p(jnp.exp(-jnp.abs(shifted)))
    return shifted, step


def pairs(width):
    return [(at, min(at + LANES, width)) for at in range(0, width, LANES)]


def mix_forward_kernel(
    proj_ref, conv_ref, head_ref, skip_ref, gated_ref, y_ref, enter_ref, state_ref, ext_ref
):
    rows = proj_ref.shape[0]
    wide = gated_ref.shape[1]
    chans = wide + BC

    @pl.when(pl.program_id(0) == 0)
    def _():
        state_ref[...] = jnp.zeros_like(state_ref)
        ext_ref[0:8, :] = jnp.zeros((8, chans), F32)

    ext_ref[8 : 8 + rows, :] = proj_ref[:, wide : wide + chans].astype(F32)
    pre = conv_ref[CONV : CONV + 1, :] + conv_ref[0:1, :] * ext_ref[5 : 5 + rows, :]
    for lag in range(1, CONV):
        pre = pre + conv_ref[lag : lag + 1, :] * ext_ref[5 + lag : 5 + lag + rows, :]
    ext_ref[0:8, :] = ext_ref[rows : rows + 8, :]
    act = pre * jax.nn.sigmoid(pre)
    x = act[:, :wide]
    b_low = act[:, wide : wide + NSTATE].astype(BF16)
    c_low = act[:, wide + NSTATE :].astype(BF16)

    _, step = steps_of(proj_ref[:, wide + chans :].astype(F32), head_ref)
    decay = -step * head_ref[1:2, :]
    lower = iota((rows, rows), 0) >= iota((rows, rows), 1)
    cum = mm_exact(lower.astype(F32), decay)
    cum_t = jnp.transpose(cum)
    spread = head_spread(wide)
    cum_wide = mm_exact(cum, spread)
    step_wide = mm_exact(step, spread)
    total = cum_wide[rows - 1 : rows, :]

    scores = mm_nt(c_low, b_low)
    weighted = x * step_wide
    weighted_low = weighted.astype(BF16)
    within = []
    for start, end in pairs(wide):
        both = weighted_low[:, start:end]
        parts = []
        for head in range(start // HD, end // HD):
            gap = cum[:, head : head + 1] - cum_t[head : head + 1, :]
            mixed = jnp.where(lower, jnp.exp(gap), 0.0) * scores
            parts.append(mm(mixed.astype(BF16), both))
        if len(parts) == 2:
            first = iota((rows, end - start), 1) < HD
            within.append(jnp.where(first, parts[0], parts[1]))
        else:
            within.append(parts[0])
    within = jnp.concatenate(within, axis=1)
    state = state_ref[...]
    enter_ref[0] = state
    carried = jnp.exp(cum_wide) * mm(c_low, state.astype(BF16))
    y = within + carried + skip_ref[0:1, :] * x
    gate = proj_ref[:, :wide].astype(F32)
    gated_ref[...] = (y * (gate * jax.nn.sigmoid(gate))).astype(BF16)
    y_ref[...] = y.astype(BF16)
    ending = (weighted * jnp.exp(total - cum_wide)).astype(BF16)
    state_ref[...] = state * jnp.exp(total) + mm_tn(b_low, ending)


def mix_forward(proj, conv_rows, head_rows, wide_rows):
    length, width = proj.shape
    wide = wide_rows.shape[1]
    count = length // STRETCH
    whole = lambda shape: pl.BlockSpec(shape, lambda i: (0,) * len(shape))
    part = lambda cols: pl.BlockSpec((STRETCH, cols), lambda i: (i, 0))
    return pl.pallas_call(
        mix_forward_kernel,
        grid=(count,),
        in_specs=[
            part(width),
            whole(conv_rows.shape),
            whole(head_rows.shape),
            whole(wide_rows.shape),
        ],
        out_specs=[
            part(wide),
            part(wide),
            pl.BlockSpec((1, NSTATE, wide), lambda i: (i, 0, 0)),
        ],
        out_shape=[
            jax.ShapeDtypeStruct((length, wide), BF16),
            jax.ShapeDtypeStruct((length, wide), BF16),
            jax.ShapeDtypeStruct((count, NSTATE, wide), F32),
        ],
        scratch_shapes=[
            pltpu.VMEM((NSTATE, wide), F32),
            pltpu.VMEM((STRETCH + 8, wide + BC), F32),
        ],
        compiler_params=pltpu.CompilerParams(
            dimension_semantics=("arbitrary",), vmem_limit_bytes=48 * 1024 * 1024
        ),
        cost_estimate=pl.CostEstimate(
            flops=length * 2 * STRETCH * wide * 4, bytes_accessed=length * 6000, transcendentals=0
        ),
        name="mix_forward",
    )(proj, conv_rows, head_rows, wide_rows)


def mix_backward_kernel(
    proj_ref,
    before_ref,
    y_ref,
    pulled_ref,
    kappa_ref,
    enter_ref,
    conv_ref,
    head_ref,
    wide_ref,
    out_ref,
    conv_grad_ref,
    head_grad_ref,
    skip_grad_ref,
    dstate_ref,
    ext_ref,
    gext_ref,
    rows_ref,
):
    rows = proj_ref.shape[0]
    wide = y_ref.shape[1]
    chans = wide + BC
    turn = pl.program_id(0)

    @pl.when(turn == 0)
    def _():
        dstate_ref[...] = jnp.zeros_like(dstate_ref)
        gext_ref[rows : rows + 8, :] = jnp.zeros((8, chans), F32)
        conv_grad_ref[...] = jnp.zeros_like(conv_grad_ref)
        head_grad_ref[...] = jnp.zeros_like(head_grad_ref)
        skip_grad_ref[...] = jnp.zeros_like(skip_grad_ref)
        rows_ref[...] = jnp.zeros_like(rows_ref)

    before = before_ref[8:16, wide : wide + chans].astype(F32)
    ext_ref[0:8, :] = jnp.where(turn == pl.num_programs(0) - 1, 0.0, before)
    ext_ref[8 : 8 + rows, :] = proj_ref[:, wide : wide + chans].astype(F32)
    pre = conv_ref[CONV : CONV + 1, :] + conv_ref[0:1, :] * ext_ref[5 : 5 + rows, :]
    for lag in range(1, CONV):
        pre = pre + conv_ref[lag : lag + 1, :] * ext_ref[5 + lag : 5 + lag + rows, :]
    sig = jax.nn.sigmoid(pre)
    act = pre * sig
    slope = sig * (1.0 + pre * (1.0 - sig))
    x = act[:, :wide]
    x_low = x.astype(BF16)
    b_low = act[:, wide : wide + NSTATE].astype(BF16)
    c_low = act[:, wide + NSTATE :].astype(BF16)

    shifted, step = steps_of(proj_ref[:, wide + chans :].astype(F32), head_ref)
    rate = head_ref[1:2, :]
    decay = -step * rate
    lower = iota((rows, rows), 0) >= iota((rows, rows), 1)
    upper = iota((rows, rows), 0) <= iota((rows, rows), 1)
    cum = mm_exact(lower.astype(F32), decay)
    cum_t = jnp.transpose(cum)
    spread = head_spread(wide)
    fold = head_fold(wide)
    cum_wide = mm_exact(cum, spread)
    step_wide = mm_exact(step, spread)
    total = cum_wide[rows - 1 : rows, :]
    grown = jnp.exp(cum_wide)
    to_end = jnp.exp(total - cum_wide)

    gate = proj_ref[:, :wide].astype(F32)
    y = y_ref[...].astype(F32)
    gate_sig = jax.nn.sigmoid(gate)
    gate_act = gate * gate_sig
    gain = wide_ref[1:2, :]
    g_gated = gain * pulled_ref[...].astype(F32) - (y * gate_act) * kappa_ref[...]
    dy = g_gated * gate_act
    out_ref[:, :wide] = (g_gated * y * (gate_sig * (1.0 + gate * (1.0 - gate_sig)))).astype(BF16)
    dy_low = dy.astype(BF16)
    skip_grad_ref[0:1, :] += jnp.sum(x * dy, axis=0, keepdims=True)

    scores_t = mm_nt(b_low, c_low)
    lane = iota((rows, LANES), 1)
    d_scores = jnp.zeros((rows, rows), F32)
    column = jnp.zeros((rows, LANES), F32)
    inner = []
    for start, end in pairs(wide):
        both_dy = dy_low[:, start:end]
        both_x = x_low[:, start:end]
        side = iota((rows, end - start), 1) // HD
        parts = []
        for head in range(start // HD, end // HD):
            gap = cum_t[head : head + 1, :] - cum[:, head : head + 1]
            fade = jnp.where(upper, jnp.exp(gap), 0.0)
            own = jnp.where(side == head - start // HD, both_x, jnp.zeros_like(both_x))
            faded = fade * mm_nt(own, both_dy)
            stepped = faded * step[:, head : head + 1]
            d_scores = d_scores + stepped
            parts.append(mm((scores_t * fade).astype(BF16), both_dy))
            column = jnp.where(
                lane == head, jnp.sum(scores_t * faded, axis=1, keepdims=True), column
            )
            rows_ref[head : head + 1, :] = jnp.sum(scores_t * stepped, axis=0, keepdims=True)
        if len(parts) == 2:
            inner.append(jnp.where(side == 0, parts[0], parts[1]))
        else:
            inner.append(parts[0])
    inner = jnp.concatenate(inner, axis=1)

    enter = enter_ref[0]
    enter_low = enter.astype(BF16)
    dstate = dstate_ref[...]
    dstate_low = dstate.astype(BF16)
    outer = to_end * mm(b_low, dstate_low)
    g_x = step_wide * (inner + outer) + wide_ref[0:1, :] * dy
    dy_grown = dy * grown
    dy_grown_low = dy_grown.astype(BF16)
    carried_sum = mm_exact(dy_grown * mm(c_low, enter_low), fold)
    outer_sum = mm_exact(x * outer, fold)
    state_sum = mm_exact(
        jnp.broadcast_to(jnp.sum(enter * dstate, axis=0, keepdims=True), (8, wide)), fold
    )[0:1, :]
    step_outer = step * outer_sum
    g_cum = jnp.transpose(rows_ref[...]) + carried_sum - step * column - step_outer
    g_total = (
        jnp.sum(step_outer, axis=0, keepdims=True)
        + jnp.exp(cum[rows - 1 : rows, :]) * state_sum
    )
    g_decay = mm_exact(upper.astype(F32), g_cum) + g_total
    scaled_decay = rate * g_decay
    g_raw = (column + outer_sum - scaled_decay) * jax.nn.sigmoid(shifted)
    head_grad_ref[0:1, :] += jnp.sum(g_raw, axis=0, keepdims=True)
    head_grad_ref[1:2, :] -= jnp.sum(step * scaled_decay, axis=0, keepdims=True)
    out_ref[:, wide + chans :] = g_raw.astype(BF16)

    d_low = d_scores.astype(BF16)
    ending = (x * (step_wide * to_end)).astype(BF16)
    g_b = mm(d_low, c_low) + mm_nt(ending, dstate_low)
    g_c = mm_tn(d_low, b_low) + mm_nt(dy_grown_low, enter_low)
    dstate_ref[...] = dstate * jnp.exp(total) + mm_tn(c_low, dy_grown_low)

    gext_ref[0:rows, :wide] = g_x * slope[:, :wide]
    gext_ref[0:rows, wide : wide + NSTATE] = g_b * slope[:, wide : wide + NSTATE]
    gext_ref[0:rows, wide + NSTATE :] = g_c * slope[:, wide + NSTATE :]
    g_pre = gext_ref[0:rows, :]
    g_in = conv_ref[CONV - 1 : CONV, :] * g_pre
    for lag in range(CONV - 1):
        g_in = g_in + conv_ref[lag : lag + 1, :] * gext_ref[3 - lag : 3 - lag + rows, :]
    out_ref[:, wide : wide + chans] = g_in.astype(BF16)
    for lag in range(CONV):
        conv_grad_ref[lag : lag + 1, :] += jnp.sum(
            ext_ref[5 + lag : 5 + lag + rows, :] * g_pre, axis=0, keepdims=True
        )
    conv_grad_ref[CONV : CONV + 1, :] += jnp.sum(g_pre, axis=0, keepdims=True)
    gext_ref[rows : rows + 8, :] = gext_ref[0:8, :]


def mix_backward(proj, y, pulled, kappa, enter, conv_rows, head_rows, wide_rows):
    length, width = proj.shape
    wide = wide_rows.shape[1]
    count = length // STRETCH
    whole = lambda shape: pl.BlockSpec(shape, lambda i: (0,) * len(shape))
    part = lambda cols: pl.BlockSpec((STRETCH, cols), lambda i: (count - 1 - i, 0))
    before = pl.BlockSpec(
        (16, width), lambda i: (jnp.maximum((count - 1 - i) * (STRETCH // 16) - 1, 0), 0)
    )
    return pl.pallas_call(
        mix_backward_kernel,
        grid=(count,),
        in_specs=[
            part(width),
            before,
            part(wide),
            part(wide),
            part(1),
            pl.BlockSpec((1, NSTATE, wide), lambda i: (count - 1 - i, 0, 0)),
            whole(conv_rows.shape),
            whole(head_rows.shape),
            whole(wide_rows.shape),
        ],
        out_specs=[
            part(width),
            whole((8, wide + BC)),
            whole((8, LANES)),
            whole((8, wide)),
        ],
        out_shape=[
            jax.ShapeDtypeStruct((length, width), BF16),
            jax.ShapeDtypeStruct((8, wide + BC), F32),
            jax.ShapeDtypeStruct((8, LANES), F32),
            jax.ShapeDtypeStruct((8, wide), F32),
        ],
        scratch_shapes=[
            pltpu.VMEM((NSTATE, wide), F32),
            pltpu.VMEM((STRETCH + 8, wide + BC), F32),
            pltpu.VMEM((STRETCH + 8, wide + BC), F32),
            pltpu.VMEM((LANES, STRETCH), F32),
        ],
        compiler_params=pltpu.CompilerParams(
            dimension_semantics=("arbitrary",), vmem_limit_bytes=48 * 1024 * 1024
        ),
        cost_estimate=pl.CostEstimate(
            flops=length * 2 * STRETCH * wide * 8, bytes_accessed=length * 9000, transcendentals=0
        ),
        name="mix_backward",
    )(proj, proj, y, pulled, kappa, enter, conv_rows, head_rows, wide_rows)


def team_gather(rows):
    return lax.all_gather(rows, TEAM, axis=0, tiled=True)


def team_scatter(rows):
    return lax.psum_scatter(rows, TEAM, scatter_dimension=0, tiled=True)


def swap(values):
    return lax.ppermute(values, ("a", "q"), SWAP)


def rms(values):
    return lax.rsqrt(jnp.mean(values * values, axis=-1, keepdims=True) + eps)


def local(
    tokens,
    cotangent,
    norm_gain,
    in_weight,
    conv_kernel,
    conv_shift,
    dt_bias,
    a_log,
    skip_gain,
    gate_gain,
    out_weight,
):
    layers, depth, columns = in_weight.shape
    heads = dt_bias.shape[1]
    wide = heads * HD
    chans = wide + BC
    team = lax.axis_size(TEAM)
    sizes = tuple(lax.axis_size(name) for name in EVERY)
    model = in_weight.shape[1] * team * lax.axis_size(COPIES)
    rank = lax.axis_index(TEAM)
    tail = columns - 2 * DI

    small = jnp.concatenate(
        [
            norm_gain,
            conv_kernel.reshape(layers, -1),
            conv_shift,
            gate_gain,
        ],
        axis=1,
    )
    small = lax.all_gather(small, EVERY, axis=0)
    n_norm, n_conv, n_gate = norm_gain.shape[1], conv_shift.shape[1], gate_gain.shape[1]
    cuts = [n_norm, n_norm + CONV * n_conv, n_norm + (CONV + 1) * n_conv]
    head_all = swap(jnp.stack([dt_bias, a_log, skip_gain]))

    def parameters(layer):
        mine = small[:, layer]
        norm = mine[:, : cuts[0]].reshape(-1).astype(F32)
        kernel = mine[:, cuts[0] : cuts[1]].reshape(-1, CONV, n_conv)
        kernel = kernel.transpose(1, 0, 2).reshape(CONV, -1).astype(F32)
        shift = mine[:, cuts[1] : cuts[2]].reshape(1, -1).astype(F32)
        gate = mine[:, cuts[2] :].reshape(1, -1).astype(F32)
        rows = jnp.concatenate([kernel, shift, jnp.zeros((3, kernel.shape[1]), F32)], axis=0)
        conv_rows = jnp.concatenate(
            [lax.dynamic_slice_in_dim(rows, rank * wide, wide, 1), rows[:, DI:]], axis=1
        )
        head_rows = jnp.zeros((8, LANES), F32)
        head_rows = head_rows.at[0, :heads].set(head_all[0, layer])
        head_rows = head_rows.at[1, :heads].set(jnp.exp(head_all[1, layer]))
        wide_rows = jnp.concatenate(
            [
                jnp.repeat(head_all[2, layer], HD)[None],
                lax.dynamic_slice_in_dim(gate, rank * wide, wide, 1),
                jnp.zeros((6, wide), F32),
            ],
            axis=0,
        )
        return norm, conv_rows, head_rows, wide_rows

    def in_columns(layer):
        mine = in_weight[layer]
        parts = mine[:, : 2 * DI].reshape(depth, 2, team, wide).transpose(2, 0, 1, 3)
        parts = parts.reshape(team, depth, 2 * wide)
        parts = lax.all_to_all(parts, TEAM, split_axis=0, concat_axis=0)
        parts = lax.all_gather(parts, COPIES, axis=0)
        parts = parts.reshape(sizes[3], 2, 2, *sizes[1:3], depth, 2 * wide)
        parts = parts.transpose(1, 3, 4, 0, 2, 5, 6).reshape(model, 2 * wide)
        rest = lax.all_gather(mine[:, 2 * DI :], EVERY, axis=0, tiled=True)
        steps = lax.dynamic_slice_in_dim(rest, BC + rank * heads, heads, 1)
        steps = jnp.pad(steps, ((0, 0), (0, LANES - heads)))
        return jnp.concatenate([parts, rest[:, :BC], steps], axis=1)

    def out_rows(layer):
        return lax.all_gather(swap(out_weight[layer]), COPIES, axis=0, tiled=True)

    residual = swap(tokens[0]).astype(F32)
    records = []
    for layer in range(layers):
        params = parameters(layer)
        norm, conv_rows, head_rows, wide_rows = params
        weight_in, weight_out = in_columns(layer), out_rows(layer)
        rho = rms(residual)
        normed = team_gather((residual * rho * norm).astype(BF16))
        proj = mm(normed, weight_in).astype(BF16)
        gated, y, enter = mix_forward(proj, conv_rows, head_rows, wide_rows)
        gated_wide = gated.astype(F32)
        squares = jnp.sum(gated_wide * gated_wide, axis=1, keepdims=True)
        branch = mm((gated_wide * wide_rows[1:2]).astype(BF16), weight_out)
        sent = jnp.concatenate([branch, jnp.broadcast_to(squares, (gated.shape[0], LANES))], axis=1)
        got = team_scatter(sent.astype(BF16)).astype(F32)
        branch = got[:, :model]
        gate_rho = lax.rsqrt(got[:, model : model + 1] / DI + eps)
        records.append(
            (residual, rho, normed, proj, gated, y, enter, branch, gate_rho, weight_in, weight_out, params)
        )
        residual = residual + gate_rho * branch

    out = swap(residual.astype(BF16))
    grad = swap(cotangent[0]).astype(F32)
    in_grads, out_grads, vectors, head_grads = [], [], [], []
    for layer in reversed(range(layers)):
        (before, rho, normed, proj, gated, y, enter, branch, gate_rho, weight_in, weight_out, params) = records[layer]
        norm, conv_rows, head_rows, wide_rows = params
        pulled = grad * gate_rho
        kappa = gate_rho * gate_rho * jnp.sum(pulled * branch, axis=1, keepdims=True) / DI
        sent = jnp.concatenate([pulled, jnp.broadcast_to(kappa, (pulled.shape[0], LANES))], axis=1)
        got = team_gather(sent.astype(BF16))
        g_branch = got[:, :model]
        kappa = got[:, model : model + 1].astype(F32)
        g_scaled = mm_nt(g_branch, weight_out)
        outer = mm_tn(gated, g_branch)
        g_gate_gain = jnp.sum(outer * weight_out.astype(F32), axis=1)
        g_out = (outer * wide_rows[1][:, None]).astype(BF16)
        g_proj, g_conv, g_heads, g_skip = mix_backward(
            proj, y, g_scaled, kappa, enter, conv_rows, head_rows, wide_rows
        )
        g_normed = team_scatter(mm_nt(g_proj, weight_in).astype(BF16)).astype(F32)
        g_in = mm_tn(normed, g_proj).astype(BF16)

        g_out = swap(lax.psum_scatter(g_out, COPIES, scatter_dimension=0, tiled=True))
        out_grads.insert(0, g_out.astype(F32))
        parts = g_in[:, : 2 * wide].reshape(*sizes[:4], 2, depth, 2 * wide)
        parts = parts.transpose(3, 0, 4, 1, 2, 5, 6).reshape(-1, team, depth, 2 * wide)
        parts = lax.psum_scatter(parts, COPIES, scatter_dimension=0)
        parts = lax.all_to_all(parts, TEAM, split_axis=0, concat_axis=0)
        parts = parts.reshape(team, depth, 2, wide).transpose(1, 2, 0, 3).reshape(depth, 2 * DI)
        rest = jnp.zeros((model, tail - BC), BF16)
        rest = lax.dynamic_update_slice_in_dim(
            rest, g_in[:, 2 * wide + BC : 2 * wide + BC + heads], rank * heads, 1
        )
        rest = jnp.concatenate([g_in[:, 2 * wide : 2 * wide + BC], rest], axis=1)
        rest = lax.psum_scatter(rest, EVERY, scatter_dimension=0, tiled=True)
        in_grads.insert(0, jnp.concatenate([parts, rest], axis=1).astype(F32))

        weighed = g_normed * norm
        mean = jnp.mean(weighed * before, axis=1, keepdims=True)
        grad = grad + rho * weighed - before * (rho * rho * rho * mean)
        g_norm = jnp.sum(g_normed * before * rho, axis=0)
        g_conv_all = jnp.concatenate(
            [
                lax.dynamic_update_slice_in_dim(
                    jnp.zeros((CONV + 1, DI), F32), g_conv[: CONV + 1, :wide], rank * wide, 1
                ),
                g_conv[: CONV + 1, wide:],
            ],
            axis=1,
        )
        g_gate_all = lax.dynamic_update_slice_in_dim(
            jnp.zeros((DI,), F32), g_gate_gain, rank * wide, 0
        )
        vectors.insert(0, (g_norm, g_conv_all, g_gate_all))
        head_grads.insert(
            0,
            jnp.stack(
                [
                    g_heads[0, :heads],
                    g_heads[1, :heads],
                    jnp.sum(g_skip[0].reshape(heads, HD), axis=1),
                ]
            ),
        )

    norm_all = jnp.stack([entry[0] for entry in vectors])
    conv_all = jnp.stack([entry[1] for entry in vectors])
    gate_all = jnp.stack([entry[2] for entry in vectors])
    norm_all, conv_all, gate_all = lax.psum((norm_all, conv_all, gate_all), EVERY)
    place = lax.axis_index(EVERY)
    norm_all = lax.dynamic_slice_in_dim(norm_all, place * n_norm, n_norm, 1)
    conv_all = lax.dynamic_slice_in_dim(conv_all, place * n_conv, n_conv, 2)
    gate_all = lax.dynamic_slice_in_dim(gate_all, place * n_gate, n_gate, 1)
    head_all = swap(lax.psum(jnp.stack(head_grads), COPIES))
    grad_tokens = swap(grad)
    return (
        out[None],
        grad_tokens[None],
        norm_all,
        jnp.stack(in_grads),
        conv_all[:, :CONV],
        conv_all[:, CONV],
        head_all[:, 0],
        head_all[:, 1],
        head_all[:, 2],
        gate_all,
        jnp.stack(out_grads),
    )


def solution(mesh):
    seq, fsdp = mesh.shape["seq"], mesh.shape["fsdp"]
    fine = Mesh(mesh.devices.reshape(2, seq // 4, 2, fsdp // 2, 2), EVERY)
    acts = P(FSDP, SEQ, None)
    flat = P(None, SEQ + FSDP)
    rows = P(None, SEQ + FSDP, None)
    taps = P(None, None, SEQ + FSDP)
    head = P(None, SEQ)
    return jax.shard_map(
        local,
        mesh=fine,
        in_specs=(acts, acts, flat, rows, taps, flat, head, head, head, flat, rows),
        out_specs=(acts, acts, flat, rows, taps, flat, head, head, head, flat, rows),
        check_vma=False,
    )
```

```python
import functools

import jax
import jax.numpy as jnp
from jax import lax
from jax.experimental import pallas as pl
from jax.experimental.pallas import tpu as pltpu
from jax.sharding import Mesh
from jax.sharding import PartitionSpec as P

HD = 64
NSTATE = 128
STRETCH = 256
DI = 3072
CONV = 4
LANES = 128
BC = 2 * NSTATE

eps = 1e-05

F32 = jnp.float32
BF16 = jnp.bfloat16
EXACT = lax.Precision.HIGHEST
CAP = 48 * 1024 * 1024


def mm(left, right):
    return jnp.dot(left, right, preferred_element_type=F32)


def mm_nt(left, right):
    return lax.dot_general(left, right, (((1,), (1,)), ((), ())), preferred_element_type=F32)


def mm_tn(left, right):
    return lax.dot_general(left, right, (((0,), (0,)), ((), ())), preferred_element_type=F32)


def mm_exact(left, right):
    return jnp.dot(left, right, precision=EXACT, preferred_element_type=F32)


def iota(shape, dim):
    return lax.broadcasted_iota(jnp.int32, shape, dim)


def head_spread(width):
    return (iota((LANES, width), 0) == iota((LANES, width), 1) // HD).astype(F32)


def head_fold(width):
    return (iota((width, LANES), 0) // HD == iota((width, LANES), 1)).astype(F32)


def own_steps(raw, turned):
    return pltpu.roll(raw.astype(F32), turned, 1)


def steps_of(raw, head_rows):
    shifted = raw + head_rows[0:1]
    step = jnp.maximum(shifted, 0.0) + jnp.log1p(jnp.exp(-jnp.abs(shifted)))
    return shifted, step


def take(ref, core):
    half = ref.shape[0] // 2
    first = ref[pl.ds(pl.multiple_of(core * half, half), half), :]
    second = ref[pl.ds(pl.multiple_of((1 - core) * half, half), half), :]
    return jnp.concatenate([first, second], axis=0)


def put(ref, core, values, start, end):
    half = ref.shape[0] // 2
    ref[pl.ds(pl.multiple_of(core * half, half), half), start:end] = values[:half]
    ref[pl.ds(pl.multiple_of((1 - core) * half, half), half), start:end] = values[half:]


def pairs(width):
    return [(at, min(at + LANES, width)) for at in range(0, width, LANES)]


def mix_forward_kernel(
    place_ref, proj_ref, conv_ref, head_ref, skip_ref, *refs, with_sums
):
    gated_ref, y_ref, enter_ref = refs[with_sums : with_sums + 3]
    state_ref, ext_ref = refs[-2:]
    core, turned = place_ref[0] & 1, place_ref[1]
    rows = proj_ref.shape[0]
    wide = gated_ref.shape[1]
    chans = wide + BC

    @pl.when(pl.program_id(0) == 0)
    def _():
        state_ref[...] = jnp.zeros_like(state_ref)
        ext_ref[0:8, :] = jnp.zeros((8, chans), F32)

    proj = take(proj_ref, core)
    ext_ref[8 : 8 + rows, :] = proj[:, wide : wide + chans].astype(F32)
    pre = conv_ref[CONV : CONV + 1, :] + conv_ref[0:1, :] * ext_ref[5 : 5 + rows, :]
    for lag in range(1, CONV):
        pre = pre + conv_ref[lag : lag + 1, :] * ext_ref[5 + lag : 5 + lag + rows, :]
    ext_ref[0:8, :] = ext_ref[rows : rows + 8, :]
    act = pre * jax.nn.sigmoid(pre)
    x = act[:, :wide]
    b_low = act[:, wide : wide + NSTATE].astype(BF16)
    c_low = act[:, wide + NSTATE :].astype(BF16)

    _, step = steps_of(own_steps(proj[:, wide + chans :], turned), head_ref)
    decay = -step * head_ref[1:2, :]
    lower = iota((rows, rows), 0) >= iota((rows, rows), 1)
    cum = mm_exact(lower.astype(F32), decay)
    cum_t = jnp.transpose(cum)
    spread = head_spread(wide)
    cum_wide = mm_exact(cum, spread)
    step_wide = mm_exact(step, spread)
    total = cum_wide[rows - 1 : rows, :]

    scores = mm_nt(c_low, b_low)
    weighted = x * step_wide
    weighted_low = weighted.astype(BF16)
    within = []
    for start, end in pairs(wide):
        both = weighted_low[:, start:end]
        parts = []
        for head in range(start // HD, end // HD):
            gap = cum[:, head : head + 1] - cum_t[head : head + 1, :]
            mixed = jnp.where(lower, jnp.exp(gap), 0.0) * scores
            parts.append(mm(mixed.astype(BF16), both))
        if len(parts) == 2:
            first = iota((rows, end - start), 1) < HD
            within.append(jnp.where(first, parts[0], parts[1]))
        else:
            within.append(parts[0])
    within = jnp.concatenate(within, axis=1)
    state = state_ref[...]
    enter_ref[0] = state
    carried = jnp.exp(cum_wide) * mm(c_low, state.astype(BF16))
    y = within + carried + skip_ref[0:1, :] * x
    gate = proj[:, :wide].astype(F32)
    gated = (y * (gate * jax.nn.sigmoid(gate))).astype(BF16)
    put(gated_ref, core, gated, 0, wide)
    if with_sums:
        gated = gated.astype(F32)
        ones = jnp.ones((8, wide), BF16)
        product = gated * take(refs[0], core).astype(F32)
        squares = mm_nt(ones, (gated * gated).astype(BF16))
        product = mm_nt(ones, product.astype(BF16))
        refs[4][...] = jnp.where(iota((8, rows), 0) == 0, squares, product)
    put(y_ref, core, y.astype(BF16), 0, wide)
    ending = (weighted * jnp.exp(total - cum_wide)).astype(BF16)
    state_ref[...] = state * jnp.exp(total) + mm_tn(b_low, ending)


def mix_forward(place, proj, conv_rows, head_rows, wide_rows, pulled=None):
    with_sums = pulled is not None
    length, width = proj.shape
    wide = wide_rows.shape[1]
    count = length // STRETCH
    whole = lambda shape: pl.BlockSpec(shape, lambda i, at: (0,) * len(shape))
    part = lambda cols: pl.BlockSpec((STRETCH, cols), lambda i, at: (i ^ (at[0] >> 1), 0))
    return pl.pallas_call(
        functools.partial(mix_forward_kernel, with_sums=with_sums),
        grid_spec=pltpu.PrefetchScalarGridSpec(
            num_scalar_prefetch=1,
            grid=(count,),
            in_specs=[
                part(width),
                whole(conv_rows.shape),
                whole(head_rows.shape),
                whole(wide_rows.shape),
            ]
            + [part(wide)] * with_sums,
            out_specs=[
                part(wide),
                part(wide),
                pl.BlockSpec((1, NSTATE, wide), lambda i, at: (i, 0, 0)),
            ]
            + [pl.BlockSpec((8, STRETCH), lambda i, at: (0, i))] * with_sums,
            scratch_shapes=[
                pltpu.VMEM((NSTATE, wide), F32),
                pltpu.VMEM((STRETCH + 8, wide + BC), F32),
            ],
        ),
        out_shape=[
            jax.ShapeDtypeStruct((length, wide), BF16),
            jax.ShapeDtypeStruct((length, wide), BF16),
            jax.ShapeDtypeStruct((count, NSTATE, wide), F32),
        ]
        + [jax.ShapeDtypeStruct((8, length), F32)] * with_sums,
        compiler_params=pltpu.CompilerParams(
            dimension_semantics=("arbitrary",), vmem_limit_bytes=CAP
        ),
        cost_estimate=pl.CostEstimate(
            flops=length * wide * 30000, bytes_accessed=length * 6000, transcendentals=0
        ),
        name="mix_forward",
    )(place, proj, conv_rows, head_rows, wide_rows, *[pulled] * with_sums)


def mix_backward_kernel(
    place_ref,
    proj_ref,
    before_ref,
    y_ref,
    pulled_ref,
    kappa_ref,
    enter_ref,
    conv_ref,
    head_ref,
    wide_ref,
    *refs,
    as_rows,
):
    out_ref, conv_grad_ref, head_grad_ref, skip_grad_ref = refs[:4]
    dstate_ref, ext_ref, gext_ref, rows_ref = refs[-4:]
    core, turned = place_ref[0] & 1, place_ref[1]
    rows = proj_ref.shape[0]
    wide = y_ref.shape[1]
    chans = wide + BC
    turn = pl.program_id(0)

    @pl.when(turn == 0)
    def _():
        dstate_ref[...] = jnp.zeros_like(dstate_ref)
        gext_ref[rows : rows + 8, :] = jnp.zeros((8, chans), F32)
        conv_grad_ref[...] = jnp.zeros_like(conv_grad_ref)
        head_grad_ref[...] = jnp.zeros_like(head_grad_ref)
        skip_grad_ref[...] = jnp.zeros_like(skip_grad_ref)
        rows_ref[...] = jnp.zeros_like(rows_ref)

    before = before_ref[8:16, wide : wide + chans].astype(F32)
    ext_ref[0:8, :] = jnp.where(turn == pl.num_programs(0) - 1, 0.0, before)
    proj = take(proj_ref, core)
    ext_ref[8 : 8 + rows, :] = proj[:, wide : wide + chans].astype(F32)
    pre = conv_ref[CONV : CONV + 1, :] + conv_ref[0:1, :] * ext_ref[5 : 5 + rows, :]
    for lag in range(1, CONV):
        pre = pre + conv_ref[lag : lag + 1, :] * ext_ref[5 + lag : 5 + lag + rows, :]
    sig = jax.nn.sigmoid(pre)
    act = pre * sig
    slope = sig * (1.0 + pre * (1.0 - sig))
    x = act[:, :wide]
    x_low = x.astype(BF16)
    b_low = act[:, wide : wide + NSTATE].astype(BF16)
    c_low = act[:, wide + NSTATE :].astype(BF16)

    shifted, step = steps_of(own_steps(proj[:, wide + chans :], turned), head_ref)
    rate = head_ref[1:2, :]
    decay = -step * rate
    lower = iota((rows, rows), 0) >= iota((rows, rows), 1)
    upper = iota((rows, rows), 0) <= iota((rows, rows), 1)
    cum = mm_exact(lower.astype(F32), decay)
    cum_t = jnp.transpose(cum)
    spread = head_spread(wide)
    fold = head_fold(wide)
    cum_wide = mm_exact(cum, spread)
    step_wide = mm_exact(step, spread)
    total = cum_wide[rows - 1 : rows, :]
    grown = jnp.exp(cum_wide)
    to_end = jnp.exp(total - cum_wide)

    gate = proj[:, :wide].astype(F32)
    y = take(y_ref, core).astype(F32)
    gate_sig = jax.nn.sigmoid(gate)
    gate_act = gate * gate_sig
    g_gated = take(pulled_ref, core).astype(F32)
    gated = y * gate_act
    if as_rows:
        sums = jnp.transpose(kappa_ref[...])
        rho = lax.rsqrt(sums[:, 0:1] / DI + eps)
        kappa = rho * rho * rho * sums[:, 1:2] / DI
        g_gated = rho * g_gated - gated * kappa
        put(refs[4], core, (gated * rho).astype(BF16), 0, wide)
    else:
        g_gated = g_gated - gated * take(kappa_ref, core)[:, 0:1].astype(F32)
    dy = g_gated * gate_act
    g_gate = g_gated * y * (gate_sig * (1.0 + gate * (1.0 - gate_sig)))
    put(out_ref, core, g_gate.astype(BF16), 0, wide)
    dy_low = dy.astype(BF16)
    skip_grad_ref[0:1, :] += jnp.sum(x * dy, axis=0, keepdims=True)

    scores_t = mm_nt(b_low, c_low)
    lane = iota((rows, LANES), 1)
    d_scores = jnp.zeros((rows, rows), F32)
    column = jnp.zeros((rows, LANES), F32)
    inner = []
    for start, end in pairs(wide):
        both_dy = dy_low[:, start:end]
        both_x = x_low[:, start:end]
        side = iota((rows, end - start), 1) // HD
        parts = []
        for head in range(start // HD, end // HD):
            gap = cum_t[head : head + 1, :] - cum[:, head : head + 1]
            fade = jnp.where(upper, jnp.exp(gap), 0.0)
            own = jnp.where(side == head - start // HD, both_x, jnp.zeros_like(both_x))
            faded = fade * mm_nt(own, both_dy)
            stepped = faded * step[:, head : head + 1]
            d_scores = d_scores + stepped
            parts.append(mm((scores_t * fade).astype(BF16), both_dy))
            column = jnp.where(
                lane == head, jnp.sum(scores_t * faded, axis=1, keepdims=True), column
            )
            rows_ref[head : head + 1, :] = jnp.sum(scores_t * stepped, axis=0, keepdims=True)
        if len(parts) == 2:
            inner.append(jnp.where(side == 0, parts[0], parts[1]))
        else:
            inner.append(parts[0])
    inner = jnp.concatenate(inner, axis=1)

    enter = enter_ref[0]
    enter_low = enter.astype(BF16)
    dstate = dstate_ref[...]
    dstate_low = dstate.astype(BF16)
    outer = to_end * mm(b_low, dstate_low)
    g_x = step_wide * (inner + outer) + wide_ref[0:1, :] * dy
    dy_grown = dy * grown
    dy_grown_low = dy_grown.astype(BF16)
    carried_sum = mm_exact(dy_grown * mm(c_low, enter_low), fold)
    outer_sum = mm_exact(x * outer, fold)
    state_sum = mm_exact(
        jnp.broadcast_to(jnp.sum(enter * dstate, axis=0, keepdims=True), (8, wide)), fold
    )[0:1, :]
    step_outer = step * outer_sum
    g_cum = jnp.transpose(rows_ref[...]) + carried_sum - step * column - step_outer
    g_total = (
        jnp.sum(step_outer, axis=0, keepdims=True)
        + jnp.exp(cum[rows - 1 : rows, :]) * state_sum
    )
    g_decay = mm_exact(upper.astype(F32), g_cum) + g_total
    scaled_decay = rate * g_decay
    g_raw = (column + outer_sum - scaled_decay) * jax.nn.sigmoid(shifted)
    head_grad_ref[0:1, :] += jnp.sum(g_raw, axis=0, keepdims=True)
    head_grad_ref[1:2, :] -= jnp.sum(step * scaled_decay, axis=0, keepdims=True)
    g_raw = pltpu.roll(g_raw, lax.rem(LANES - turned, LANES), 1)
    put(out_ref, core, g_raw.astype(BF16), wide + chans, wide + chans + LANES)

    d_low = d_scores.astype(BF16)
    ending = (x * (step_wide * to_end)).astype(BF16)
    g_b = mm(d_low, c_low) + mm_nt(ending, dstate_low)
    g_c = mm_tn(d_low, b_low) + mm_nt(dy_grown_low, enter_low)
    dstate_ref[...] = dstate * jnp.exp(total) + mm_tn(c_low, dy_grown_low)

    gext_ref[0:rows, :wide] = g_x * slope[:, :wide]
    gext_ref[0:rows, wide : wide + NSTATE] = g_b * slope[:, wide : wide + NSTATE]
    gext_ref[0:rows, wide + NSTATE :] = g_c * slope[:, wide + NSTATE :]
    g_pre = gext_ref[0:rows, :]
    g_in = conv_ref[CONV - 1 : CONV, :] * g_pre
    for lag in range(CONV - 1):
        g_in = g_in + conv_ref[lag : lag + 1, :] * gext_ref[3 - lag : 3 - lag + rows, :]
    put(out_ref, core, g_in.astype(BF16), wide, wide + chans)
    for lag in range(CONV):
        conv_grad_ref[lag : lag + 1, :] += jnp.sum(
            ext_ref[5 + lag : 5 + lag + rows, :] * g_pre, axis=0, keepdims=True
        )
    conv_grad_ref[CONV : CONV + 1, :] += jnp.sum(g_pre, axis=0, keepdims=True)
    gext_ref[rows : rows + 8, :] = gext_ref[0:8, :]


def mix_backward(place, proj, y, pulled, kappa, enter, conv_rows, head_rows, wide_rows, as_rows):
    length, width = proj.shape
    wide = wide_rows.shape[1]
    count = length // STRETCH
    whole = lambda shape: pl.BlockSpec(shape, lambda i, at: (0,) * len(shape))
    part = lambda cols: pl.BlockSpec((STRETCH, cols), lambda i, at: ((count - 1 - i) ^ (at[0] >> 1), 0))
    half = STRETCH // 2

    def last_rows(i, at):
        pair = jnp.maximum(count - 2 - i, 0) ^ (at[0] >> 1)
        block = 2 * pair + 1 - (at[0] & 1)
        return block * (half // 16) + half // 16 - 1, 0

    before = pl.BlockSpec((16, width), last_rows)
    turn = lambda i, at: (count - 1 - i) ^ (at[0] >> 1)
    if as_rows:
        scales = pl.BlockSpec((8, STRETCH), lambda i, at: (0, count - 1 - i))
    else:
        last = kappa.shape[1] // LANES - 1
        scales = pl.BlockSpec((STRETCH, LANES), lambda i, at: (turn(i, at), last))
    return pl.pallas_call(
        functools.partial(mix_backward_kernel, as_rows=as_rows),
        grid_spec=pltpu.PrefetchScalarGridSpec(
            num_scalar_prefetch=1,
            grid=(count,),
            in_specs=[
                part(width),
                before,
                part(wide),
                part(wide),
                scales,
                pl.BlockSpec((1, NSTATE, wide), lambda i, at: (count - 1 - i, 0, 0)),
                whole(conv_rows.shape),
                whole(head_rows.shape),
                whole(wide_rows.shape),
            ],
            out_specs=[
                part(width),
                whole((8, wide + BC)),
                whole((8, LANES)),
                whole((8, wide)),
            ]
            + [part(wide)] * as_rows,
            scratch_shapes=[
                pltpu.VMEM((NSTATE, wide), F32),
                pltpu.VMEM((STRETCH + 8, wide + BC), F32),
                pltpu.VMEM((STRETCH + 8, wide + BC), F32),
                pltpu.VMEM((LANES, STRETCH), F32),
            ],
        ),
        out_shape=[
            jax.ShapeDtypeStruct((length, width), BF16),
            jax.ShapeDtypeStruct((8, wide + BC), F32),
            jax.ShapeDtypeStruct((8, LANES), F32),
            jax.ShapeDtypeStruct((8, wide), F32),
        ]
        + [jax.ShapeDtypeStruct((length, wide), BF16)] * as_rows,
        compiler_params=pltpu.CompilerParams(
            dimension_semantics=("arbitrary",), vmem_limit_bytes=CAP
        ),
        cost_estimate=pl.CostEstimate(
            flops=length * wide * 66000, bytes_accessed=length * 9000, transcendentals=0
        ),
        name="mix_backward",
    )(place, proj, proj, y, pulled, kappa, enter, conv_rows, head_rows, wide_rows)


def add_low(*terms):
    total = terms[0].astype(F32)
    for term in terms[1:]:
        total = total + term.astype(F32)
    return total.astype(BF16)


def rms(values):
    return lax.rsqrt(jnp.mean(values * values, axis=-1, keepdims=True) + eps)


def after(values, *others):
    return lax.optimization_barrier((values, others))[0]


def flip(values, axis):
    return lax.ppermute(values, axis, [(0, 1), (1, 0)])


class Axes:
    def __init__(self, seq, fsdp):
        between = tuple(f"b{i}" for i in range((seq // 4).bit_length() - 1))
        before = tuple(f"p{i}" for i in range((fsdp // 2).bit_length() - 1))
        self.seq = ("a",) + between + ("c",)
        self.fsdp = before + ("q",)
        self.every = self.seq + self.fsdp
        self.links = ("a",) + between
        self.team = self.seq
        self.copies = self.fsdp

    def bits(self, names, at):
        value = 0
        for spot, name in enumerate(names):
            if at >> (len(names) - 1 - spot) & 1:
                value |= 1 << (len(self.every) - 1 - self.every.index(name))
        return value

    def at(self, me, r, k, relative):
        if relative:
            me = me ^ self.bits(self.copies, r)
        else:
            me = me & ~self.bits(self.copies, -1) | self.bits(self.copies, r)
        return me & ~self.bits(self.team, -1) | self.bits(self.team, k)


def all_vmem(count):
    return [pl.BlockSpec(memory_space=pltpu.VMEM)] * count


SMEM = pl.BlockSpec(memory_space=pltpu.SMEM)


def split_in(axes, weights, gain, spare, layer):
    team = 2 ** len(axes.team)
    depth, columns = weights.shape[1:]
    wide = DI // team
    parts = 2 + 3 * LANES // wide

    def kernel(weight_ref, gain_ref, spare_ref, out_ref):
        scale = gain_ref[...].astype(F32)
        tail = (weight_ref[0, :, 2 * DI :].astype(F32) * scale).astype(BF16)
        tail = jnp.concatenate([tail, spare_ref[...]], axis=1)
        for k in range(team):
            for part in range(2):
                base = (1 - part) * DI + k * wide
                cut = weight_ref[0, :, base : base + wide].astype(F32)
                out_ref[k, part] = (cut * scale).astype(BF16)
            for part in range(2, parts):
                out_ref[k, part] = tail[:, (part - 2) * wide : (part - 1) * wide]

    whole = lambda shape: pl.BlockSpec(shape, lambda i: (0,) * len(shape))
    return pl.pallas_call(
        kernel,
        grid=(1,),
        in_specs=[
            pl.BlockSpec((1, depth, columns), lambda i: (layer, 0, 0)),
            whole((depth, 1)),
            whole(spare.shape),
        ],
        out_specs=whole((team, parts, depth, wide)),
        out_shape=jax.ShapeDtypeStruct((team, parts, depth, wide), BF16),
        compiler_params=pltpu.CompilerParams(vmem_limit_bytes=CAP),
        name="split_in",
    )(weights, gain[:, None], spare)


def columns_of(part, wide):
    return (1 - part if part < 2 else part) * wide


def join_in(axes, place, lists, relative):
    copies, team = len(lists), 2 ** len(axes.team)
    parts = len(lists[0]) // team
    depth, wide = lists[0][0][0].shape[-2:]
    rows = copies * team * depth
    extra = min(depth, 32)
    if depth % 16:
        flat = jnp.stack([jnp.stack([array[index] for array, index in row]) for row in lists])
        flat = flat.reshape(copies * team, parts, depth, wide)
        flat = jnp.concatenate(
            [flat[:, 1], flat[:, 0]] + [flat[:, part] for part in range(2, parts)], axis=-1
        )
        at = [axes.at(place[2], r, k, relative) for r in range(copies) for k in range(team)]
        flat = jnp.zeros_like(flat).at[jnp.stack(at)].set(flat)
        return flat.reshape(rows, -1), flat[:, :extra, -LANES:]

    arrays = []
    for row in lists:
        for array, _ in row:
            if not any(array is known for known in arrays):
                arrays.append(array)
    which = lambda array: next(i for i, known in enumerate(arrays) if known is array)

    def kernel(place_ref, *refs):
        out_ref, spare_ref = refs[-2:]
        for r in range(copies):
            for k in range(team):
                spot = axes.at(place_ref[2], r, k, relative)
                at = pl.ds(pl.multiple_of(spot * depth, 16), depth)
                for part in range(parts):
                    array, index = lists[r][parts * k + part]
                    base = columns_of(part, wide)
                    out_ref[at, base : base + wide] = refs[which(array)][index]
                index = index if isinstance(index, tuple) else (index,)
                index += (slice(0, extra), slice(wide - LANES, wide))
                spare_ref[spot] = refs[which(array)][index]

    return pl.pallas_call(
        kernel,
        in_specs=[SMEM] + all_vmem(len(arrays)),
        out_specs=all_vmem(2),
        out_shape=[
            jax.ShapeDtypeStruct((rows, parts * wide), BF16),
            jax.ShapeDtypeStruct((copies * team, extra, LANES), BF16),
        ],
        compiler_params=pltpu.CompilerParams(vmem_limit_bytes=CAP),
        name="join_in",
    )(place, *arrays)


def cut_in(axes, place, grad, spare, depth, wide, relative):
    copies, team = 2 ** len(axes.copies), 2 ** len(axes.team)
    parts = grad.shape[1] // wide
    extra, room = spare.shape[1:]
    if depth % 16:
        flat = grad.reshape(copies * team, depth, -1).at[:, :extra, -room:].set(spare)
        at = [axes.at(place[2], r, k, relative) for r in range(copies) for k in range(team)]
        flat = jnp.take(flat, jnp.stack(at), axis=0)
        flat = [
            flat[:, :, columns_of(part, wide) : columns_of(part, wide) + wide]
            for part in range(parts)
        ]
        return jnp.stack(flat, axis=1).reshape(copies, team * parts, depth, wide)

    def kernel(place_ref, grad_ref, spare_ref, out_ref):
        for r in range(copies):
            for k in range(team):
                spot = axes.at(place_ref[2], r, k, relative)
                rows = pl.ds(pl.multiple_of(spot * depth, 16), depth)
                for part in range(parts):
                    base = columns_of(part, wide)
                    out_ref[r, parts * k + part] = grad_ref[rows, base : base + wide]
                out_ref[r, parts * k + parts - 1, 0:extra, wide - room :] = spare_ref[spot]

    return pl.pallas_call(
        kernel,
        in_specs=[SMEM] + all_vmem(2),
        out_specs=pl.BlockSpec(memory_space=pltpu.VMEM),
        out_shape=jax.ShapeDtypeStruct((copies, team * parts, depth, wide), BF16),
        compiler_params=pltpu.CompilerParams(vmem_limit_bytes=CAP),
        name="cut_in",
    )(place, grad, spare)


def finish_in(axes, grads, weight, gain):
    layers, depth, columns = weight.shape
    team = 2 ** len(axes.team)
    wide = DI // team
    parts = grads[0].shape[1]
    room = parts * wide - 2 * wide - (columns - 2 * DI)

    def kernel(weight_ref, gain_ref, *refs):
        grad_ref, sum_ref, spare_ref = refs[-3:]
        for layer in range(layers):
            blocks_ref = refs[layer]
            scale = gain_ref[layer].astype(F32)
            tails = []
            for part in range(2, parts):
                tail = blocks_ref[0, part].astype(F32)
                for k in range(1, team):
                    tail = tail + blocks_ref[k, part].astype(F32)
                tails.append(tail)
            tail = jnp.concatenate(tails, axis=1)
            spare_ref[layer] = tail[:, columns - 2 * DI :]
            tail = tail[:, : columns - 2 * DI]
            grad_ref[layer, :, 2 * DI :] = tail * scale
            total = jnp.sum(tail * weight_ref[layer, :, 2 * DI :].astype(F32), 1, keepdims=True)
            for k in range(team):
                for part in range(2):
                    values = blocks_ref[k, part].astype(F32)
                    base = (1 - part) * DI + k * wide
                    grad_ref[layer, :, base : base + wide] = values * scale
                    total = total + jnp.sum(
                        values * weight_ref[layer, :, base : base + wide].astype(F32),
                        1,
                        keepdims=True,
                    )
            sum_ref[layer] = jnp.broadcast_to(total, (depth, LANES))

    grads, sums, spares = pl.pallas_call(
        kernel,
        in_specs=all_vmem(2 + layers),
        out_specs=all_vmem(3),
        out_shape=[
            jax.ShapeDtypeStruct((layers, depth, columns), F32),
            jax.ShapeDtypeStruct((layers, depth, LANES), F32),
            jax.ShapeDtypeStruct((layers, depth, room), F32),
        ],
        compiler_params=pltpu.CompilerParams(vmem_limit_bytes=CAP),
        name="finish_in",
    )(weight, gain[..., None], *grads)
    return grads, sums[:, :, 0], spares


def copies_gather(axes, whole):
    slow, fast = axes.copies
    half = whole.shape[0] // 2
    one, two = flip(whole, fast), flip(whole, slow)
    corner = [flip(one[:half], slow), flip(two[half:], fast)]
    every = [(index,) for index in range(whole.shape[0])]
    lists = [[(array, at) for (at,) in every] for array in (whole, one, two)]
    return lists + [[(corner[at // half], at % half) for (at,) in every]]


def sum_start(axes, pieces):
    slow, fast = axes.copies
    half = pieces.shape[1] // 2
    corner = [flip(pieces[3, :half], slow), flip(pieces[3, half:], fast)]
    to_fast = jnp.concatenate([add_low(pieces[1, :half], corner[0]), pieces[1, half:]], axis=0)
    to_slow = jnp.concatenate([pieces[2, :half], add_low(pieces[2, half:], corner[1])], axis=0)
    return pieces[0], to_fast, to_slow


def sum_end(axes, parts):
    own, to_fast, to_slow = parts
    slow, fast = axes.copies
    return add_low(own, flip(to_fast, fast), flip(to_slow, slow))


def team_gather(axes, rows):
    if len(axes.links) != 2:
        whole = rows[None]
        for name in reversed(axes.links):
            whole = jnp.concatenate([whole, flip(whole, name)], axis=0)
        whole = jnp.stack([whole, flip(whole, "c")], axis=1)
        return [whole.reshape(-1, rows.shape[1])]
    far, near = axes.links
    half = rows.shape[0] // 2
    from_far, from_near = flip(rows, far), flip(rows, near)
    own = jnp.concatenate([rows, flip(rows, "c")], axis=0)
    corner = jnp.concatenate([flip(from_near[:half], far), flip(from_far[half:], near)], axis=0)
    sides = jnp.stack([from_near, from_far])
    sides = jnp.stack([sides, flip(sides, "c")], axis=1).reshape(-1, rows.shape[1])
    corner = jnp.concatenate([corner, flip(corner, "c")], axis=0)
    return [own, sides, corner]


def scatter_start(axes, product, rows):
    team = 2 ** len(axes.team)
    if len(axes.links) != 2:
        whole = product(0, team * rows).reshape(team // 2, 2, rows, -1)
        whole = add_low(whole[:, 0], flip(whole[:, 1], "c"))
        for name in axes.links[:-1]:
            half = whole.shape[0] // 2
            whole = add_low(whole[:half], flip(whole[half:], name))
        return whole[0], whole[1:]
    far, near = axes.links
    half = rows // 2
    corner = product(6 * rows, 8 * rows)
    corner = add_low(corner[:rows], flip(corner[rows:], "c"))
    sides = product(2 * rows, 6 * rows).reshape(2, 2, rows, -1)
    sides = add_low(sides[:, 0], flip(sides[:, 1], "c"))
    own = product(0, 2 * rows)
    own = add_low(own[:rows], flip(own[rows:], "c"))
    got_far, got_near = flip(corner[:half], far), flip(corner[half:], near)
    to_near = jnp.concatenate([add_low(sides[0, :half], got_far), sides[0, half:]], axis=0)
    to_far = jnp.concatenate([sides[1, :half], add_low(sides[1, half:], got_near)], axis=0)
    return own, to_near, to_far


def scatter_end(axes, parts):
    if len(axes.links) != 2:
        return parts[0].astype(F32) + flip(parts[1], axes.links[-1])[0].astype(F32)
    own, to_near, to_far = parts
    far, near = axes.links
    return own.astype(F32) + flip(to_near, near).astype(F32) + flip(to_far, far).astype(F32)


def team_scatter(axes, product, rows):
    return scatter_end(axes, scatter_start(axes, product, rows))


def local(
    axes,
    tokens,
    cotangent,
    norm_gain,
    in_weight,
    conv_kernel,
    conv_shift,
    dt_bias,
    a_log,
    skip_gain,
    gate_gain,
    out_weight,
):
    layers, depth, columns = in_weight.shape
    rows = tokens.shape[1]
    model = tokens.shape[2]
    heads = dt_bias.shape[1]
    wide = heads * HD
    team = 2 ** len(axes.team)
    copies = 2 ** len(axes.copies)
    me = lax.axis_index(axes.team)
    all_at = lax.axis_index(axes.every)
    place = jnp.stack([me, lax.rem(LANES - me * heads, LANES), all_at]).astype(jnp.int32)

    n_conv = conv_shift.shape[1]
    room = 3 * LANES - (columns - 2 * DI)
    cuts = [(at, min(at + room, n_conv)) for at in range(0, n_conv, room)]
    taps = CONV + 1
    conv = jnp.concatenate([conv_kernel, conv_shift[:, None]], axis=1).reshape(-1, n_conv)
    conv = [jnp.pad(conv[:, at:end], ((0, 0), (0, room - end + at))) for at, end in cuts]
    conv = jnp.concatenate(conv, axis=0)
    spare = jnp.pad(conv, ((0, depth - conv.shape[0]), (0, 0)))

    def team_swap(blocks):
        return lax.all_to_all(blocks, axes.team, split_axis=0, concat_axis=0)

    def in_blocks(layer, start):
        blocks = split_in(axes, in_weight, after(norm_gain[layer], start), spare, layer)
        return team_swap(blocks).reshape(-1, depth, wide)

    def in_columns(blocks, at_once):
        relative = at_once and len(axes.copies) == 2
        if relative:
            lists = copies_gather(axes, blocks)
        else:
            got = lax.all_gather(blocks, axes.copies)
            lists = [[(got, (r, k)) for k in range(blocks.shape[0])] for r in range(copies)]
        return join_in(axes, place, lists, relative)

    def out_rows(layer):
        mine = out_weight[layer].astype(F32) * gate_gain[layer].astype(F32)[:, None]
        return lax.all_gather(mine.astype(BF16), axes.copies, axis=0, tiled=True)

    blocks = in_blocks(0, tokens)
    parts = blocks.shape[0] // team
    weight_in, beside = in_columns(blocks, True)
    weight_out = out_rows(0)
    residual = after(tokens[0], blocks).astype(F32)

    conv = beside[:, : conv.shape[0], LANES - room :]
    conv = conv.reshape(-1, len(cuts), layers * taps, room).transpose(0, 2, 1, 3)
    conv = conv.reshape(-1, layers * taps, len(cuts) * room)[:, :, :n_conv]
    conv = conv.reshape(-1, layers, taps, n_conv)
    conv = conv.transpose(1, 2, 0, 3).reshape(layers, CONV + 1, -1).astype(F32)
    conv = jnp.pad(conv, ((0, 0), (0, 7 - CONV), (0, 0)))
    conv = jnp.concatenate(
        [lax.dynamic_slice_in_dim(conv, me * wide, wide, 2), conv[:, :, DI:]], axis=2
    )
    head = jnp.stack([dt_bias, a_log, skip_gain], axis=1)
    skip = jnp.pad(jnp.repeat(head[:, 2:], HD, axis=2), ((0, 0), (0, 7), (0, 0)))
    head = jnp.stack([head[:, 0], jnp.exp(head[:, 1])], axis=1)
    head = jnp.pad(head, ((0, 0), (0, 6), (0, LANES - heads)))

    records = []
    for layer in range(layers):
        rho = rms(residual)
        pieces = team_gather(axes, (residual * rho).astype(BF16))
        more = layer + 1 < layers
        if more:
            blocks = in_blocks(layer + 1, pieces[-1])
            cot_pieces = team_gather(axes, after(cotangent[0], blocks))
            g_scaled = None
        else:
            g_scaled = [mm_nt(piece, weight_out) for piece in cot_pieces]
            g_scaled = jnp.concatenate(g_scaled, axis=0).astype(BF16)
        proj = jnp.concatenate([mm(piece, weight_in).astype(BF16) for piece in pieces], axis=0)
        gated, y, enter, *sums = mix_forward(
            place, proj, conv[layer], head[layer], skip[layer], g_scaled
        )
        normed = jnp.concatenate(pieces, axis=0)
        records.append((residual, rho, normed, proj, gated, y, enter, weight_in, weight_out))
        if not more:
            break
        gated = after(gated, blocks, cot_pieces)

        def branch_rows(begin, end):
            cut = gated[begin:end]
            squares = jnp.sum(jnp.square(cut.astype(F32)), axis=1, keepdims=True)
            squares = jnp.broadcast_to(squares, (end - begin, LANES))
            return jnp.concatenate([mm(cut, weight_out), squares], axis=1).astype(BF16)

        got = team_scatter(axes, branch_rows, rows)
        branch = got[:, :model]
        gate_rho = lax.rsqrt(got[:, model : model + 1] / DI + eps)
        records[-1] += (branch, gate_rho)
        residual = residual + gate_rho * branch
        weight_in = in_columns(blocks, False)[0]
        weight_out = out_rows(layer + 1)

    in_grads, out_grads = [], []
    grad = cotangent[0].astype(F32)

    def spare_rows(g_conv, g_head, g_skip):
        g_conv = jnp.concatenate(
            [
                lax.dynamic_update_slice_in_dim(
                    jnp.zeros((taps, DI), F32), g_conv[:taps, :wide], me * wide, 1
                ),
                g_conv[:taps, wide:],
            ],
            axis=1,
        )
        g_conv = g_conv.reshape(taps, -1, n_conv).transpose(1, 0, 2)
        g_conv = [
            jnp.pad(g_conv[..., at:end], ((0, 0), (0, 0), (0, room - end + at)))
            for at, end in cuts
        ]
        g_head = jnp.stack(
            [g_head[0, :heads], g_head[1, :heads], jnp.sum(g_skip[0].reshape(heads, HD), 1)]
        )
        g_head = jnp.pad(g_head, ((0, 0), (0, room - heads)))
        sharers = team * copies // team
        owner = jnp.arange(team * copies) // sharers == me
        g_head = jnp.where(owner[:, None, None], g_head, 0.0)
        spare = jnp.concatenate(g_conv + [g_head], axis=1)
        more = -spare.shape[1] % 16 if depth % 16 == 0 else 0
        return jnp.pad(spare, ((0, 0), (0, more), (0, 0))).astype(BF16)

    for layer in reversed(range(layers)):
        last = layer == layers - 1
        if last:
            residual_in, rho, normed, proj, gated, y, enter, weight_in, weight_out = records[layer]
            pieces = cot_pieces
        else:
            (
                residual_in,
                rho,
                normed,
                proj,
                gated,
                y,
                enter,
                weight_in,
                weight_out,
                branch,
                gate_rho,
            ) = records[layer]
            pulled = grad * gate_rho
            kappa = gate_rho * gate_rho * jnp.sum(pulled * branch, axis=1, keepdims=True) / DI
            pulled = after(pulled, g_out, blocks)
            sent = jnp.concatenate([pulled, jnp.broadcast_to(kappa, (rows, LANES))], axis=1)
            pieces = team_gather(axes, sent.astype(BF16))
        got = jnp.concatenate(pieces, axis=0)
        if last:
            sums = sums[0]
            for name in axes.team:
                sums = sums + flip(sums, name)
            branch = scatter_start(
                axes, lambda begin, end: mm(gated[begin:end], weight_out).astype(BF16), rows
            )
            scales = after(sums, branch)
        else:
            g_scaled = [mm_nt(piece[:, :model], weight_out) for piece in pieces]
            g_scaled = jnp.concatenate(g_scaled, axis=0).astype(BF16)
            scales = after(got, summed)
        outs = mix_backward(
            place, proj, y, g_scaled, scales, enter, conv[layer], head[layer], skip[layer], last
        )
        g_proj, g_conv, g_head, g_skip = outs[:4]
        if last:
            branch = scatter_end(axes, branch)
            gate_rho = lax.dynamic_slice_in_dim(sums, me * rows, rows, 1)[0][:, None]
            out = (residual + lax.rsqrt(gate_rho / DI + eps) * branch).astype(BF16)
            g_proj = after(g_proj, branch)
        else:
            in_grads.insert(0, team_swap(summed.reshape(team, parts, depth, wide)))
            g_proj = after(g_proj, in_grads)
        g_in = mm_tn(normed, g_proj).astype(BF16)
        spare = spare_rows(g_conv, g_head, g_skip)
        quick = layer == 0 and len(axes.copies) == 2
        blocks = cut_in(axes, place, g_in, spare, depth, wide, quick)
        g_out = mm_tn(outs[4] if last else gated, after(got, g_proj)[:, :model]).astype(BF16)
        if layer == 0:
            g_proj = after(g_proj, blocks)
        weighed = scatter_start(
            axes, lambda begin, end: mm_nt(g_proj[begin:end], weight_in).astype(BF16), rows
        )
        if quick:
            summed = sum_end(axes, after(sum_start(axes, blocks), weighed))
        else:
            summed = lax.psum_scatter(blocks, axes.copies, scatter_dimension=0)
        weighed = scatter_end(axes, weighed)
        mean = jnp.mean(weighed * residual_in, axis=1, keepdims=True)
        grad = grad + rho * weighed - residual_in * (rho * rho * rho * mean)
        out_grads.insert(0, lax.psum_scatter(g_out, axes.copies, scatter_dimension=0, tiled=True))
    in_grads.insert(0, team_swap(after(summed, weighed).reshape(team, parts, depth, wide)))

    grad_in, grad_norm, spare = finish_in(axes, in_grads, in_weight, norm_gain)
    grad_out = jnp.stack(out_grads).astype(F32)
    grad_gate = jnp.sum(grad_out * out_weight.astype(F32), axis=2)
    grad_out = grad_out * gate_gain.astype(F32)[:, :, None]

    conv_grad = [
        spare[:, at * taps : (at + 1) * taps, : end - start] for at, (start, end) in enumerate(cuts)
    ]
    conv_grad = jnp.concatenate(conv_grad, axis=2)
    head_grad = spare[:, len(cuts) * taps : len(cuts) * taps + 3, :heads]
    return (
        out[None],
        grad[None],
        grad_norm,
        grad_in,
        conv_grad[:, :CONV],
        conv_grad[:, CONV],
        head_grad[:, 0],
        head_grad[:, 1],
        head_grad[:, 2],
        grad_gate,
        grad_out,
    )


def solution(mesh):
    axes = Axes(mesh.shape["seq"], mesh.shape["fsdp"])
    fine = Mesh(mesh.devices.reshape((2,) * len(axes.every)), axes.every)
    acts = P(axes.fsdp, axes.seq, None)
    flat = P(None, axes.every)
    rows = P(None, axes.every, None)
    taps = P(None, None, axes.every)
    head = P(None, axes.seq)
    return jax.shard_map(
        functools.partial(local, axes),
        mesh=fine,
        in_specs=(acts, acts, flat, rows, taps, flat, head, head, head, flat, rows),
        out_specs=(acts, acts, flat, rows, taps, flat, head, head, head, flat, rows),
        check_vma=False,
    )
```

```python
import functools

import jax
import jax.numpy as jnp
from jax import lax
from jax.experimental import pallas as pl
from jax.experimental.pallas import tpu as pltpu
from jax.sharding import Mesh
from jax.sharding import PartitionSpec as P

HD = 64
NSTATE = 128
STRETCH = 256
DI = 3072
CONV = 4
LANES = 128
BC = 2 * NSTATE

eps = 1e-05

F32 = jnp.float32
BF16 = jnp.bfloat16
EXACT = lax.Precision.HIGHEST
CAP = 48 * 1024 * 1024


def mm(left, right):
    return jnp.dot(left, right, preferred_element_type=F32)


def mm_nt(left, right):
    return lax.dot_general(left, right, (((1,), (1,)), ((), ())), preferred_element_type=F32)


def mm_tn(left, right):
    return lax.dot_general(left, right, (((0,), (0,)), ((), ())), preferred_element_type=F32)


def mm_exact(left, right):
    return jnp.dot(left, right, precision=EXACT, preferred_element_type=F32)


def mm_low(left, right):
    return mm(left.astype(BF16), right.astype(BF16))


def mm_thirds(ones, right):
    lane = iota(right.shape, 1)
    high = right.astype(BF16).astype(F32)
    left = right - high
    middle = left.astype(BF16).astype(F32)
    low = left - middle
    packed = jnp.where(lane < 64, pltpu.roll(middle, 32, 1), pltpu.roll(low, 64, 1))
    packed = jnp.where(lane < 32, high, jnp.where(lane < 96, packed, 0.0))
    total = mm_low(ones, packed)
    total = total + pltpu.roll(total, 96, 1) + pltpu.roll(total, 64, 1)
    return jnp.where(lane < 32, total, 0.0)


def iota(shape, dim):
    return lax.broadcasted_iota(jnp.int32, shape, dim)


def head_spread(width):
    return (iota((LANES, width), 0) == iota((LANES, width), 1) // HD).astype(F32)


def head_fold(width):
    return (iota((width, LANES), 0) // HD == iota((width, LANES), 1)).astype(F32)


def own_steps(raw, turned):
    return pltpu.roll(raw.astype(F32), turned, 1)


def steps_of(raw, head_rows):
    shifted = raw + head_rows[0:1]
    step = jnp.maximum(shifted, 0.0) + jnp.log1p(jnp.exp(-jnp.abs(shifted)))
    return shifted, step


def take(ref, core):
    half = ref.shape[0] // 2
    first = ref[pl.ds(pl.multiple_of(core * half, half), half), :]
    second = ref[pl.ds(pl.multiple_of((1 - core) * half, half), half), :]
    return jnp.concatenate([first, second], axis=0)


def put(ref, core, values, start, end):
    half = ref.shape[0] // 2
    ref[pl.ds(pl.multiple_of(core * half, half), half), start:end] = values[:half]
    ref[pl.ds(pl.multiple_of((1 - core) * half, half), half), start:end] = values[half:]


def pairs(width):
    return [(at, min(at + LANES, width)) for at in range(0, width, LANES)]


def mix_forward_kernel(
    place_ref, proj_ref, conv_ref, head_ref, skip_ref, *refs, with_sums
):
    gated_ref, y_ref, enter_ref = refs[with_sums : with_sums + 3]
    state_ref, ext_ref = refs[-2:]
    core, turned = place_ref[0] & 1, place_ref[1]
    rows = proj_ref.shape[0]
    wide = gated_ref.shape[1]
    chans = wide + BC

    @pl.when(pl.program_id(0) == 0)
    def _():
        state_ref[...] = jnp.zeros_like(state_ref)
        ext_ref[0:8, :] = jnp.zeros((8, chans), F32)

    proj = take(proj_ref, core)
    ext_ref[8 : 8 + rows, :] = proj[:, wide : wide + chans].astype(F32)
    pre = conv_ref[CONV : CONV + 1, :] + conv_ref[0:1, :] * ext_ref[5 : 5 + rows, :]
    for lag in range(1, CONV):
        pre = pre + conv_ref[lag : lag + 1, :] * ext_ref[5 + lag : 5 + lag + rows, :]
    ext_ref[0:8, :] = ext_ref[rows : rows + 8, :]
    act = pre * jax.nn.sigmoid(pre)
    x = act[:, :wide]
    b_low = act[:, wide : wide + NSTATE].astype(BF16)
    c_low = act[:, wide + NSTATE :].astype(BF16)

    _, step = steps_of(own_steps(proj[:, wide + chans :], turned), head_ref)
    decay = -step * head_ref[1:2, :]
    lower = iota((rows, rows), 0) >= iota((rows, rows), 1)
    cum = mm_thirds(lower.astype(F32), decay)
    cum_t = jnp.transpose(cum)
    spread = head_spread(wide)
    total = cum[rows - 1 : rows, :]
    step_wide = mm_low(step, spread)
    grown = mm_low(jnp.exp(cum), spread)
    ending_wide = mm_low(step * jnp.exp(total - cum), spread)
    kept = mm_exact(jnp.broadcast_to(jnp.exp(total), (8, LANES)), spread)[0:1, :]

    scores = mm_nt(c_low, b_low)
    weighted = x * step_wide
    weighted_low = weighted.astype(BF16)
    within = []
    for start, end in pairs(wide):
        both = weighted_low[:, start:end]
        parts = []
        for head in range(start // HD, end // HD):
            gap = cum[:, head : head + 1] - cum_t[head : head + 1, :]
            mixed = jnp.where(lower, jnp.exp(gap), 0.0) * scores
            parts.append(mm(mixed.astype(BF16), both))
        if len(parts) == 2:
            first = iota((rows, end - start), 1) < HD
            within.append(jnp.where(first, parts[0], parts[1]))
        else:
            within.append(parts[0])
    within = jnp.concatenate(within, axis=1)
    state = state_ref[...]
    enter_ref[0] = state
    carried = grown * mm(c_low, state.astype(BF16))
    y = within + carried + skip_ref[0:1, :] * x
    gate = proj[:, :wide].astype(F32)
    gated = (y * (gate * jax.nn.sigmoid(gate))).astype(BF16)
    if not with_sums:
        put(gated_ref, core, gated, 0, wide)
    else:
        gated_ref[...] = gated
        gated = gated.astype(F32)
        ones = jnp.ones((8, wide), BF16)
        product = gated * take(refs[0], core).astype(F32)
        squares = mm_nt(ones, (gated * gated).astype(BF16))
        product = mm_nt(ones, product.astype(BF16))
        refs[4][...] = jnp.where(iota((8, rows), 0) == 0, squares, product)
    put(y_ref, core, y.astype(BF16), 0, wide)
    state_ref[...] = state * kept + mm_tn(b_low, (x * ending_wide).astype(BF16))


def mix_forward(place, proj, conv_rows, head_rows, wide_rows, pulled=None):
    with_sums = pulled is not None
    length, width = proj.shape
    wide = wide_rows.shape[1]
    count = length // STRETCH
    whole = lambda shape: pl.BlockSpec(shape, lambda i, at: (0,) * len(shape))
    part = lambda cols: pl.BlockSpec((STRETCH, cols), lambda i, at: (i ^ (at[0] >> 1), 0))
    plain = pl.BlockSpec((STRETCH, wide), lambda i, at: (i, 0))
    return pl.pallas_call(
        functools.partial(mix_forward_kernel, with_sums=with_sums),
        grid_spec=pltpu.PrefetchScalarGridSpec(
            num_scalar_prefetch=1,
            grid=(count,),
            in_specs=[
                part(width),
                whole(conv_rows.shape),
                whole(head_rows.shape),
                whole(wide_rows.shape),
            ]
            + [part(wide)] * with_sums,
            out_specs=[
                plain if with_sums else part(wide),
                part(wide),
                pl.BlockSpec((1, NSTATE, wide), lambda i, at: (i, 0, 0)),
            ]
            + [pl.BlockSpec((8, STRETCH), lambda i, at: (0, i))] * with_sums,
            scratch_shapes=[
                pltpu.VMEM((NSTATE, wide), F32),
                pltpu.VMEM((STRETCH + 8, wide + BC), F32),
            ],
        ),
        out_shape=[
            jax.ShapeDtypeStruct((length, wide), BF16),
            jax.ShapeDtypeStruct((length, wide), BF16),
            jax.ShapeDtypeStruct((count, NSTATE, wide), F32),
        ]
        + [jax.ShapeDtypeStruct((8, length), F32)] * with_sums,
        compiler_params=pltpu.CompilerParams(
            dimension_semantics=("arbitrary",), vmem_limit_bytes=CAP
        ),
        cost_estimate=pl.CostEstimate(
            flops=length * wide * 18000, bytes_accessed=length * 6000, transcendentals=0
        ),
        name="mix_forward",
    )(place, proj, conv_rows, head_rows, wide_rows, *[pulled] * with_sums)


def mix_backward_kernel(
    place_ref,
    proj_ref,
    before_ref,
    y_ref,
    pulled_ref,
    kappa_ref,
    enter_ref,
    conv_ref,
    head_ref,
    wide_ref,
    *refs,
    as_rows,
):
    out_ref, conv_grad_ref, head_grad_ref, skip_grad_ref = refs[:4]
    dstate_ref, ext_ref, gext_ref, rows_ref = refs[-4:]
    core, turned = place_ref[0] & 1, place_ref[1]
    rows = proj_ref.shape[0]
    wide = y_ref.shape[1]
    chans = wide + BC
    turn = pl.program_id(0)

    @pl.when(turn == 0)
    def _():
        dstate_ref[...] = jnp.zeros_like(dstate_ref)
        gext_ref[rows : rows + 8, :] = jnp.zeros((8, chans), F32)
        conv_grad_ref[...] = jnp.zeros_like(conv_grad_ref)
        head_grad_ref[...] = jnp.zeros_like(head_grad_ref)
        skip_grad_ref[...] = jnp.zeros_like(skip_grad_ref)
        rows_ref[...] = jnp.zeros_like(rows_ref)

    before = before_ref[8:16, wide : wide + chans].astype(F32)
    ext_ref[0:8, :] = jnp.where(turn == pl.num_programs(0) - 1, 0.0, before)
    proj = take(proj_ref, core)
    ext_ref[8 : 8 + rows, :] = proj[:, wide : wide + chans].astype(F32)
    pre = conv_ref[CONV : CONV + 1, :] + conv_ref[0:1, :] * ext_ref[5 : 5 + rows, :]
    for lag in range(1, CONV):
        pre = pre + conv_ref[lag : lag + 1, :] * ext_ref[5 + lag : 5 + lag + rows, :]
    sig = jax.nn.sigmoid(pre)
    act = pre * sig
    slope = sig * (1.0 + pre * (1.0 - sig))
    x = act[:, :wide]
    x_low = x.astype(BF16)
    b_low = act[:, wide : wide + NSTATE].astype(BF16)
    c_low = act[:, wide + NSTATE :].astype(BF16)

    shifted, step = steps_of(own_steps(proj[:, wide + chans :], turned), head_ref)
    rate = head_ref[1:2, :]
    decay = -step * rate
    lower = iota((rows, rows), 0) >= iota((rows, rows), 1)
    upper = iota((rows, rows), 0) <= iota((rows, rows), 1)
    cum = mm_thirds(lower.astype(F32), decay)
    cum_t = jnp.transpose(cum)
    spread = head_spread(wide)
    fold = head_fold(wide)
    total = cum[rows - 1 : rows, :]
    step_wide = mm_low(step, spread)
    grown = mm_low(jnp.exp(cum), spread)
    to_end = mm_low(jnp.exp(total - cum), spread)
    kept = mm_exact(jnp.broadcast_to(jnp.exp(total), (8, LANES)), spread)[0:1, :]

    gate = proj[:, :wide].astype(F32)
    y = take(y_ref, core).astype(F32)
    gate_sig = jax.nn.sigmoid(gate)
    gate_act = gate * gate_sig
    gated = y * gate_act
    if as_rows:
        g_gated = take(pulled_ref, core).astype(F32)
        sums = jnp.transpose(kappa_ref[...])
        rho = lax.rsqrt(sums[:, 0:1] / DI + eps)
        kappa = rho * rho * rho * sums[:, 1:2] / DI
        g_gated = rho * g_gated - gated * kappa
        put(refs[4], core, (gated * rho).astype(BF16), 0, wide)
    else:
        g_gated = take(pulled_ref, core).astype(F32)
        g_gated = g_gated - gated * take(kappa_ref, core)[:, 0:1].astype(F32)
    dy = g_gated * gate_act
    g_gate = g_gated * y * (gate_sig * (1.0 + gate * (1.0 - gate_sig)))
    put(out_ref, core, g_gate.astype(BF16), 0, wide)
    dy_low = dy.astype(BF16)
    skip_grad_ref[0:1, :] += jnp.sum(x * dy, axis=0, keepdims=True)

    scores_t = mm_nt(b_low, c_low)
    lane = iota((rows, LANES), 1)
    d_scores = jnp.zeros((rows, rows), F32)
    column = jnp.zeros((rows, LANES), F32)
    inner = []
    for start, end in pairs(wide):
        both_dy = dy_low[:, start:end]
        both_x = x_low[:, start:end]
        side = iota((rows, end - start), 1) // HD
        parts = []
        for head in range(start // HD, end // HD):
            gap = cum_t[head : head + 1, :] - cum[:, head : head + 1]
            fade = jnp.where(upper, jnp.exp(gap), 0.0)
            own = jnp.where(side == head - start // HD, both_x, jnp.zeros_like(both_x))
            faded = fade * mm_nt(own, both_dy)
            stepped = faded * step[:, head : head + 1]
            d_scores = d_scores + stepped
            parts.append(mm((scores_t * fade).astype(BF16), both_dy))
            column = jnp.where(
                lane == head, jnp.sum(scores_t * faded, axis=1, keepdims=True), column
            )
            rows_ref[head : head + 1, :] = jnp.sum(scores_t * stepped, axis=0, keepdims=True)
        if len(parts) == 2:
            inner.append(jnp.where(side == 0, parts[0], parts[1]))
        else:
            inner.append(parts[0])
    inner = jnp.concatenate(inner, axis=1)

    enter = enter_ref[0]
    enter_low = enter.astype(BF16)
    dstate = dstate_ref[...]
    dstate_low = dstate.astype(BF16)
    outer = to_end * mm(b_low, dstate_low)
    g_x = step_wide * (inner + outer) + wide_ref[0:1, :] * dy
    dy_grown = dy * grown
    dy_grown_low = dy_grown.astype(BF16)
    carried_sum = mm_low(dy_grown * mm(c_low, enter_low), fold)
    outer_sum = mm_low(x * outer, fold)
    state_sum = mm_exact(
        jnp.broadcast_to(jnp.sum(enter * dstate, axis=0, keepdims=True), (8, wide)), fold
    )[0:1, :]
    step_outer = step * outer_sum
    g_cum = jnp.transpose(rows_ref[...]) + carried_sum - step * column - step_outer
    g_total = (
        jnp.sum(step_outer, axis=0, keepdims=True)
        + jnp.exp(total) * state_sum
    )
    g_decay = mm_thirds(upper.astype(F32), g_cum) + g_total
    scaled_decay = rate * g_decay
    g_raw = (column + outer_sum - scaled_decay) * jax.nn.sigmoid(shifted)
    head_grad_ref[0:1, :] += jnp.sum(g_raw, axis=0, keepdims=True)
    head_grad_ref[1:2, :] -= jnp.sum(step * scaled_decay, axis=0, keepdims=True)
    g_raw = pltpu.roll(g_raw, lax.rem(LANES - turned, LANES), 1)
    put(out_ref, core, g_raw.astype(BF16), wide + chans, wide + chans + LANES)

    d_low = d_scores.astype(BF16)
    ending = (x * (step_wide * to_end)).astype(BF16)
    g_b = mm(d_low, c_low) + mm_nt(ending, dstate_low)
    g_c = mm_tn(d_low, b_low) + mm_nt(dy_grown_low, enter_low)
    dstate_ref[...] = dstate * kept + mm_tn(c_low, dy_grown_low)

    gext_ref[0:rows, :wide] = g_x * slope[:, :wide]
    gext_ref[0:rows, wide : wide + NSTATE] = g_b * slope[:, wide : wide + NSTATE]
    gext_ref[0:rows, wide + NSTATE :] = g_c * slope[:, wide + NSTATE :]
    g_pre = gext_ref[0:rows, :]
    g_in = conv_ref[CONV - 1 : CONV, :] * g_pre
    for lag in range(CONV - 1):
        g_in = g_in + conv_ref[lag : lag + 1, :] * gext_ref[3 - lag : 3 - lag + rows, :]
    put(out_ref, core, g_in.astype(BF16), wide, wide + chans)
    for lag in range(CONV):
        conv_grad_ref[lag : lag + 1, :] += jnp.sum(
            ext_ref[5 + lag : 5 + lag + rows, :] * g_pre, axis=0, keepdims=True
        )
    conv_grad_ref[CONV : CONV + 1, :] += jnp.sum(g_pre, axis=0, keepdims=True)
    gext_ref[rows : rows + 8, :] = gext_ref[0:8, :]


def mix_backward(place, proj, y, pulled, kappa, enter, conv_rows, head_rows, wide_rows, as_rows):
    length, width = proj.shape
    wide = wide_rows.shape[1]
    count = length // STRETCH
    whole = lambda shape: pl.BlockSpec(shape, lambda i, at: (0,) * len(shape))
    part = lambda cols: pl.BlockSpec((STRETCH, cols), lambda i, at: ((count - 1 - i) ^ (at[0] >> 1), 0))
    half = STRETCH // 2

    def last_rows(i, at):
        pair = jnp.maximum(count - 2 - i, 0) ^ (at[0] >> 1)
        block = 2 * pair + 1 - (at[0] & 1)
        return block * (half // 16) + half // 16 - 1, 0

    before = pl.BlockSpec((16, width), last_rows)
    turn = lambda i, at: (count - 1 - i) ^ (at[0] >> 1)
    if as_rows:
        scales = pl.BlockSpec((8, STRETCH), lambda i, at: (0, count - 1 - i))
    else:
        last = kappa.shape[1] // LANES - 1
        scales = pl.BlockSpec((STRETCH, LANES), lambda i, at: (turn(i, at), last))
    return pl.pallas_call(
        functools.partial(mix_backward_kernel, as_rows=as_rows),
        grid_spec=pltpu.PrefetchScalarGridSpec(
            num_scalar_prefetch=1,
            grid=(count,),
            in_specs=[
                part(width),
                before,
                part(wide),
                part(wide),
                scales,
                pl.BlockSpec((1, NSTATE, wide), lambda i, at: (count - 1 - i, 0, 0)),
                whole(conv_rows.shape),
                whole(head_rows.shape),
                whole(wide_rows.shape),
            ],
            out_specs=[
                part(width),
                whole((8, wide + BC)),
                whole((8, LANES)),
                whole((8, wide)),
            ]
            + [part(wide)] * as_rows,
            scratch_shapes=[
                pltpu.VMEM((NSTATE, wide), F32),
                pltpu.VMEM((STRETCH + 8, wide + BC), F32),
                pltpu.VMEM((STRETCH + 8, wide + BC), F32),
                pltpu.VMEM((LANES, STRETCH), F32),
            ],
        ),
        out_shape=[
            jax.ShapeDtypeStruct((length, width), BF16),
            jax.ShapeDtypeStruct((8, wide + BC), F32),
            jax.ShapeDtypeStruct((8, LANES), F32),
            jax.ShapeDtypeStruct((8, wide), F32),
        ]
        + [jax.ShapeDtypeStruct((length, wide), BF16)] * as_rows,
        compiler_params=pltpu.CompilerParams(
            dimension_semantics=("arbitrary",), vmem_limit_bytes=CAP
        ),
        cost_estimate=pl.CostEstimate(
            flops=length * wide * 40000, bytes_accessed=length * 9000, transcendentals=0
        ),
        name="mix_backward",
    )(place, proj, proj, y, pulled, kappa, enter, conv_rows, head_rows, wide_rows)


def add_low(*terms):
    total = terms[0].astype(F32)
    for term in terms[1:]:
        total = total + term.astype(F32)
    return total.astype(BF16)


def rms(values):
    return lax.rsqrt(jnp.mean(values * values, axis=-1, keepdims=True) + eps)


def after(values, *others):
    return lax.optimization_barrier((values, others))[0]


def flip(values, axis):
    return lax.ppermute(values, axis, [(0, 1), (1, 0)])


def flip_both(values, names):
    return lax.ppermute(values, names, [(0, 3), (1, 2), (2, 1), (3, 0)])


class Axes:
    def __init__(self, seq, fsdp):
        between = tuple(f"b{i}" for i in range((seq // 4).bit_length() - 1))
        before = tuple(f"p{i}" for i in range((fsdp // 2).bit_length() - 1))
        self.seq = ("a",) + between + ("c",)
        self.fsdp = before + ("q",)
        self.every = self.seq + self.fsdp
        self.links = ("a",) + between
        self.team = self.seq
        self.copies = self.fsdp

    def bits(self, names, at):
        value = 0
        for spot, name in enumerate(names):
            if at >> (len(names) - 1 - spot) & 1:
                value |= 1 << (len(self.every) - 1 - self.every.index(name))
        return value

    def at(self, me, r, k, relative):
        if relative:
            me = me ^ self.bits(self.copies, r)
        else:
            me = me & ~self.bits(self.copies, -1) | self.bits(self.copies, r)
        return me & ~self.bits(self.team, -1) | self.bits(self.team, k)


def all_vmem(count):
    return [pl.BlockSpec(memory_space=pltpu.VMEM)] * count


SMEM = pl.BlockSpec(memory_space=pltpu.SMEM)


def split_in(axes, weights, gain, spare, layer):
    team = 2 ** len(axes.team)
    depth, columns = weights.shape[1:]
    wide = DI // team
    parts = 2 + 3 * LANES // wide

    def kernel(weight_ref, gain_ref, spare_ref, out_ref):
        scale = gain_ref[...].astype(F32)
        tail = (weight_ref[0, :, 2 * DI :].astype(F32) * scale).astype(BF16)
        tail = jnp.concatenate([tail, spare_ref[...]], axis=1)
        for k in range(team):
            for part in range(2):
                base = (1 - part) * DI + k * wide
                cut = weight_ref[0, :, base : base + wide].astype(F32)
                out_ref[k, part] = (cut * scale).astype(BF16)
            for part in range(2, parts):
                out_ref[k, part] = tail[:, (part - 2) * wide : (part - 1) * wide]

    whole = lambda shape: pl.BlockSpec(shape, lambda i: (0,) * len(shape))
    return pl.pallas_call(
        kernel,
        grid=(1,),
        in_specs=[
            pl.BlockSpec((1, depth, columns), lambda i: (layer, 0, 0)),
            whole((depth, 1)),
            whole(spare.shape),
        ],
        out_specs=whole((team, parts, depth, wide)),
        out_shape=jax.ShapeDtypeStruct((team, parts, depth, wide), BF16),
        compiler_params=pltpu.CompilerParams(vmem_limit_bytes=CAP),
        name="split_in",
    )(weights, gain[:, None], spare)


def columns_of(part, wide):
    return (1 - part if part < 2 else part) * wide


def join_in(axes, place, lists, relative):
    copies, team = len(lists), 2 ** len(axes.team)
    parts = len(lists[0]) // team
    depth, wide = lists[0][0][0].shape[-2:]
    rows = copies * team * depth
    extra = min(depth, 32)
    if depth % 16:
        flat = jnp.stack([jnp.stack([array[index] for array, index in row]) for row in lists])
        flat = flat.reshape(copies * team, parts, depth, wide)
        flat = jnp.concatenate(
            [flat[:, 1], flat[:, 0]] + [flat[:, part] for part in range(2, parts)], axis=-1
        )
        at = [axes.at(place[2], r, k, relative) for r in range(copies) for k in range(team)]
        flat = jnp.zeros_like(flat).at[jnp.stack(at)].set(flat)
        return flat.reshape(rows, -1), flat[:, :extra, -LANES:]

    arrays = []
    for row in lists:
        for array, _ in row:
            if not any(array is known for known in arrays):
                arrays.append(array)
    which = lambda array: next(i for i, known in enumerate(arrays) if known is array)

    def kernel(place_ref, *refs):
        out_ref, spare_ref = refs[-2:]
        for r in range(copies):
            for k in range(team):
                spot = axes.at(place_ref[2], r, k, relative)
                at = pl.ds(pl.multiple_of(spot * depth, 16), depth)
                for part in range(parts):
                    array, index = lists[r][parts * k + part]
                    base = columns_of(part, wide)
                    out_ref[at, base : base + wide] = refs[which(array)][index]
                index = index if isinstance(index, tuple) else (index,)
                index += (slice(0, extra), slice(wide - LANES, wide))
                spare_ref[spot] = refs[which(array)][index]

    return pl.pallas_call(
        kernel,
        in_specs=[SMEM] + all_vmem(len(arrays)),
        out_specs=all_vmem(2),
        out_shape=[
            jax.ShapeDtypeStruct((rows, parts * wide), BF16),
            jax.ShapeDtypeStruct((copies * team, extra, LANES), BF16),
        ],
        compiler_params=pltpu.CompilerParams(vmem_limit_bytes=CAP),
        name="join_in",
    )(place, *arrays)


def cut_in(axes, place, grad, spare, depth, wide, relative):
    copies, team = 2 ** len(axes.copies), 2 ** len(axes.team)
    parts = grad.shape[1] // wide
    extra, room = spare.shape[1:]
    if depth % 16:
        flat = grad.reshape(copies * team, depth, -1).at[:, :extra, -room:].set(spare)
        at = [axes.at(place[2], r, k, relative) for r in range(copies) for k in range(team)]
        flat = jnp.take(flat, jnp.stack(at), axis=0)
        flat = [
            flat[:, :, columns_of(part, wide) : columns_of(part, wide) + wide]
            for part in range(parts)
        ]
        return jnp.stack(flat, axis=1).reshape(copies, team * parts, depth, wide)

    def kernel(place_ref, grad_ref, spare_ref, out_ref):
        for r in range(copies):
            for k in range(team):
                spot = axes.at(place_ref[2], r, k, relative)
                rows = pl.ds(pl.multiple_of(spot * depth, 16), depth)
                for part in range(parts):
                    base = columns_of(part, wide)
                    out_ref[r, parts * k + part] = grad_ref[rows, base : base + wide]
                out_ref[r, parts * k + parts - 1, 0:extra, wide - room :] = spare_ref[spot]

    return pl.pallas_call(
        kernel,
        in_specs=[SMEM] + all_vmem(2),
        out_specs=pl.BlockSpec(memory_space=pltpu.VMEM),
        out_shape=jax.ShapeDtypeStruct((copies, team * parts, depth, wide), BF16),
        compiler_params=pltpu.CompilerParams(vmem_limit_bytes=CAP),
        name="cut_in",
    )(place, grad, spare)


def finish_in(axes, grads, weight, gain):
    layers, depth, columns = weight.shape
    team = 2 ** len(axes.team)
    wide = DI // team
    parts = grads[0].shape[1]
    room = parts * wide - 2 * wide - (columns - 2 * DI)

    def kernel(weight_ref, gain_ref, *refs):
        grad_ref, sum_ref, spare_ref = refs[-3:]
        for layer in range(layers):
            blocks_ref = refs[layer]
            scale = gain_ref[layer].astype(F32)
            tails = []
            for part in range(2, parts):
                tail = blocks_ref[0, part].astype(F32)
                for k in range(1, team):
                    tail = tail + blocks_ref[k, part].astype(F32)
                tails.append(tail)
            tail = jnp.concatenate(tails, axis=1)
            spare_ref[layer] = tail[:, columns - 2 * DI :]
            tail = tail[:, : columns - 2 * DI]
            grad_ref[layer, :, 2 * DI :] = tail * scale
            total = jnp.sum(tail * weight_ref[layer, :, 2 * DI :].astype(F32), 1, keepdims=True)
            for k in range(team):
                for part in range(2):
                    values = blocks_ref[k, part].astype(F32)
                    base = (1 - part) * DI + k * wide
                    grad_ref[layer, :, base : base + wide] = values * scale
                    total = total + jnp.sum(
                        values * weight_ref[layer, :, base : base + wide].astype(F32),
                        1,
                        keepdims=True,
                    )
            sum_ref[layer] = jnp.broadcast_to(total, (depth, LANES))

    grads, sums, spares = pl.pallas_call(
        kernel,
        in_specs=all_vmem(2 + layers),
        out_specs=all_vmem(3),
        out_shape=[
            jax.ShapeDtypeStruct((layers, depth, columns), F32),
            jax.ShapeDtypeStruct((layers, depth, LANES), F32),
            jax.ShapeDtypeStruct((layers, depth, room), F32),
        ],
        compiler_params=pltpu.CompilerParams(vmem_limit_bytes=CAP),
        name="finish_in",
    )(weight, gain[..., None], *grads)
    return grads, sums[:, :, 0], spares


def together(*values):
    return lax.optimization_barrier(values)


def copies_start(axes, whole):
    slow, fast = axes.copies
    return whole, flip(whole, fast), flip(whole, slow)


def copies_corner(axes, parts):
    slow, fast = axes.copies
    whole, one, two = parts
    half = whole.shape[0] // 2
    return flip(one[:half], slow), flip(two[half:], fast)


def copies_lists(parts, corner):
    count = parts[0].shape[0]
    half = count // 2
    lists = [[(array, at) for at in range(count)] for array in parts]
    return lists + [[(corner[at // half], at % half) for at in range(count)]]


def sum_corner(axes, pieces):
    slow, fast = axes.copies
    half = pieces.shape[1] // 2
    return flip(pieces[3, :half], slow), flip(pieces[3, half:], fast)


def sum_sides(axes, pieces, corner):
    slow, fast = axes.copies
    half = pieces.shape[1] // 2
    to_fast = jnp.concatenate([add_low(pieces[1, :half], corner[0]), pieces[1, half:]], axis=0)
    to_slow = jnp.concatenate([pieces[2, :half], add_low(pieces[2, half:], corner[1])], axis=0)
    return flip(to_fast, fast), flip(to_slow, slow)


def gather_start(axes, rows):
    if len(axes.links) != 2:
        return (rows,)
    far, near = axes.links
    return rows, flip(rows, "c"), flip(rows, far), flip(rows, near)


def gather_corner(axes, parts):
    if len(axes.links) != 2:
        return parts, []
    far, near = axes.links
    rows, other, from_far, from_near = parts
    half = rows.shape[0] // 2
    sides = jnp.stack([from_near, from_far])
    sides = jnp.stack([sides, flip(sides, "c")], axis=1).reshape(-1, rows.shape[1])
    corner = flip(from_near[:half], far), flip(from_far[half:], near)
    return corner, [jnp.concatenate([rows, other], axis=0), sides]


def gather_end(axes, corner):
    if len(axes.links) != 2:
        whole = corner[0][None]
        for name in reversed(axes.links):
            whole = jnp.concatenate([whole, flip(whole, name)], axis=0)
        whole = jnp.stack([whole, flip(whole, "c")], axis=1)
        return whole.reshape(-1, corner[0].shape[1])
    last = jnp.concatenate(corner, axis=0)
    return jnp.concatenate([last, flip(last, "c")], axis=0)


def core_sum(rows_of, first, last, rows):
    both = rows_of(first, last).reshape(-1, 2, rows, rows_of.columns)
    return add_low(both[:, 0], flip(both[:, 1], "c"))


def scatter_corner(axes, rows_of, rows):
    team = 2 ** len(axes.team)
    if len(axes.links) != 2:
        return (core_sum(rows_of, 0, team * rows, rows),)
    far, near = axes.links
    corner = core_sum(rows_of, 6 * rows, 8 * rows, rows)[0]
    half = rows // 2
    hops = flip(corner[:half], far), flip(corner[half:], near)
    sides = core_sum(rows_of, 2 * rows, 6 * rows, rows)
    return hops, sides, core_sum(rows_of, 0, 2 * rows, rows)[0]


def scatter_sides(axes, parts):
    if len(axes.links) != 2:
        whole = parts[0]
        for name in axes.links:
            half = whole.shape[0] // 2
            whole = add_low(whole[:half], flip(whole[half:], name))
        return (whole[0],)
    far, near = axes.links
    hops, sides, own = parts
    half = own.shape[0] // 2
    to_near = jnp.concatenate([add_low(sides[0, :half], hops[0]), sides[0, half:]], axis=0)
    to_far = jnp.concatenate([sides[1, :half], add_low(sides[1, half:], hops[1])], axis=0)
    return own, flip(to_near, near), flip(to_far, far)


def add_all(parts):
    total = parts[0].astype(F32)
    for part in parts[1:]:
        total = total + part.astype(F32)
    return total


class Rows:
    def __init__(self, make, columns):
        self.make, self.columns = make, columns

    def __call__(self, first, last):
        return self.make(first, last)


def local(
    axes,
    tokens,
    cotangent,
    norm_gain,
    in_weight,
    conv_kernel,
    conv_shift,
    dt_bias,
    a_log,
    skip_gain,
    gate_gain,
    out_weight,
):
    layers, depth, columns = in_weight.shape
    rows = tokens.shape[1]
    model = tokens.shape[2]
    heads = dt_bias.shape[1]
    wide = heads * HD
    team = 2 ** len(axes.team)
    copies = 2 ** len(axes.copies)
    me = lax.axis_index(axes.team)
    all_at = lax.axis_index(axes.every)
    place = jnp.stack([me, lax.rem(LANES - me * heads, LANES), all_at]).astype(jnp.int32)

    n_conv = conv_shift.shape[1]
    room = 3 * LANES - (columns - 2 * DI)
    cuts = [(at, min(at + room, n_conv)) for at in range(0, n_conv, room)]
    taps = CONV + 1
    conv = jnp.concatenate([conv_kernel, conv_shift[:, None]], axis=1).reshape(-1, n_conv)
    conv = [jnp.pad(conv[:, at:end], ((0, 0), (0, room - end + at))) for at, end in cuts]
    conv = jnp.concatenate(conv, axis=0)
    spare = jnp.pad(conv, ((0, depth - conv.shape[0]), (0, 0)))

    def team_swap(blocks):
        return lax.all_to_all(blocks, axes.team, split_axis=0, concat_axis=0)

    def in_blocks(layer, start):
        blocks = split_in(axes, in_weight, after(norm_gain[layer], start), spare, layer)
        return team_swap(blocks).reshape(-1, depth, wide)

    def in_columns(blocks):
        got = lax.all_gather(blocks, axes.copies)
        lists = [[(got, (r, k)) for k in range(blocks.shape[0])] for r in range(copies)]
        return join_in(axes, place, lists, False)

    def out_rows(layer, start):
        gain = after(gate_gain[layer], start)
        mine = out_weight[layer].astype(F32) * gain.astype(F32)[:, None]
        return lax.all_gather(mine.astype(BF16), axes.copies, axis=0, tiled=True)

    paired = len(axes.copies) == 2
    assert layers == 2

    weight_out_0 = out_rows(0, tokens)
    blocks = in_blocks(0, tokens)
    parts = blocks.shape[0] // team
    residual_0 = tokens[0].astype(F32)
    rho_0 = rms(residual_0)
    blocks, sent = together(blocks, (residual_0 * rho_0).astype(BF16))
    gathered = gather_start(axes, sent)
    if paired:
        copied, gathered = together(copies_start(axes, blocks), gathered)
    hops, pieces_0 = gather_corner(axes, gathered)
    cot = gather_start(axes, after(cotangent[0], gathered))
    if paired:
        corner = copies_corner(axes, copied)
        corner, hops, weight_out_0 = together(corner, hops, weight_out_0)
        weight_in_0, beside = join_in(axes, place, copies_lists(copied, corner), True)
    else:
        weight_in_0, beside = in_columns(blocks)
    last = gather_end(axes, hops)
    last, cot = together(last, cot)
    pieces_0 = pieces_0 + [last]
    proj_0 = [mm(piece, weight_in_0).astype(BF16) for piece in pieces_0]
    proj_0 = jnp.concatenate(proj_0, axis=0)

    conv = beside[:, : conv.shape[0], LANES - room :]
    conv = conv.reshape(-1, len(cuts), layers * taps, room).transpose(0, 2, 1, 3)
    conv = conv.reshape(-1, layers * taps, len(cuts) * room)[:, :, :n_conv]
    conv = conv.reshape(-1, layers, taps, n_conv)
    conv = conv.transpose(1, 2, 0, 3).reshape(layers, CONV + 1, -1).astype(F32)
    conv = jnp.pad(conv, ((0, 0), (0, 7 - CONV), (0, 0)))
    conv = jnp.concatenate(
        [lax.dynamic_slice_in_dim(conv, me * wide, wide, 2), conv[:, :, DI:]], axis=2
    )
    head = jnp.stack([dt_bias, a_log, skip_gain], axis=1)
    skip = jnp.pad(jnp.repeat(head[:, 2:], HD, axis=2), ((0, 0), (0, 7), (0, 0)))
    head = jnp.stack([head[:, 0], jnp.exp(head[:, 1])], axis=1)
    head = jnp.pad(head, ((0, 0), (0, 6), (0, LANES - heads)))

    blocks = in_blocks(1, last)
    gated_0, y_0, enter_0 = mix_forward(place, proj_0, conv[0], head[0], skip[0])
    cot_hops, cot = gather_corner(axes, cot)
    gated_0, blocks, cot_hops = together(gated_0, blocks, cot_hops)
    cot = cot + [gather_end(axes, cot_hops)]
    weight_out_1 = out_rows(1, gated_0)

    def branch_rows(begin, end):
        cut = gated_0[begin:end]
        squares = jnp.sum(jnp.square(cut.astype(F32)), axis=1, keepdims=True)
        squares = jnp.broadcast_to(squares, (end - begin, LANES))
        return jnp.concatenate([mm(cut, weight_out_0), squares], axis=1).astype(BF16)

    got = together(*scatter_corner(axes, Rows(branch_rows, model + LANES), rows))
    got = scatter_sides(axes, got)
    if paired:
        got, copied = together(got, copies_start(axes, blocks))
    got = add_all(got)
    branch_0 = got[:, :model]
    gate_rho_0 = lax.rsqrt(got[:, model : model + 1] / DI + eps)

    residual_1 = residual_0 + gate_rho_0 * branch_0
    rho_1 = rms(residual_1)
    gathered = gather_start(axes, (residual_1 * rho_1).astype(BF16))
    g_scaled = jnp.concatenate([mm_nt(piece, weight_out_1).astype(BF16) for piece in cot], axis=0)
    if paired:
        gathered, corner, g_scaled = together(gathered, copies_corner(axes, copied), g_scaled)
        weight_in_1 = join_in(axes, place, copies_lists(copied, corner), True)[0]
    else:
        weight_in_1 = in_columns(blocks)[0]
    hops, pieces_1 = gather_corner(axes, gathered)
    proj_1 = [mm(piece, weight_in_1).astype(BF16) for piece in pieces_1]
    hops, proj_1 = together(hops, proj_1)
    last = gather_end(axes, hops)
    pieces_1 = pieces_1 + [last]
    proj_1 = jnp.concatenate(proj_1 + [mm(last, weight_in_1).astype(BF16)], axis=0)
    gated_1, y_1, enter_1, sums = mix_forward(
        place, proj_1, conv[1], head[1], skip[1], g_scaled
    )

    sums = sums + flip(sums, "c")
    if len(axes.links) == 2:
        far, near = axes.links
        sums = sums + flip(sums, far) + flip(sums, near) + flip_both(sums, axes.links)
    else:
        for name in axes.links:
            sums = sums + flip(sums, name)
    branch_1 = mm(gated_1, weight_out_1).astype(BF16)
    sums, branch_1 = together(sums, branch_1)
    branch_1 = lax.psum_scatter(branch_1, axes.team, scatter_dimension=0, tiled=True)
    g_proj, g_conv, g_head, g_skip, scaled_1 = mix_backward(
        place, proj_1, y_1, g_scaled, sums, enter_1, conv[1], head[1], skip[1], True
    )
    got_1 = jnp.concatenate(after(cot, g_proj), axis=0)
    normed = jnp.concatenate(after(pieces_1, g_proj), axis=0)

    def spare_rows(g_conv, g_head, g_skip):
        g_conv = jnp.concatenate(
            [
                lax.dynamic_update_slice_in_dim(
                    jnp.zeros((taps, DI), F32), g_conv[:taps, :wide], me * wide, 1
                ),
                g_conv[:taps, wide:],
            ],
            axis=1,
        )
        g_conv = g_conv.reshape(taps, -1, n_conv).transpose(1, 0, 2)
        g_conv = [
            jnp.pad(g_conv[..., at:end], ((0, 0), (0, 0), (0, room - end + at)))
            for at, end in cuts
        ]
        g_head = jnp.stack(
            [g_head[0, :heads], g_head[1, :heads], jnp.sum(g_skip[0].reshape(heads, HD), 1)]
        )
        g_head = jnp.pad(g_head, ((0, 0), (0, room - heads)))
        sharers = team * copies // team
        owner = jnp.arange(team * copies) // sharers == me
        g_head = jnp.where(owner[:, None, None], g_head, 0.0)
        spare = jnp.concatenate(g_conv + [g_head], axis=1)
        more = -spare.shape[1] % 16 if depth % 16 == 0 else 0
        return jnp.pad(spare, ((0, 0), (0, more), (0, 0))).astype(BF16)

    def in_gradient(normed, g_proj, g_conv, g_head, g_skip, quick):
        g_in = mm_tn(normed, g_proj).astype(BF16)
        spare = spare_rows(g_conv, g_head, g_skip)
        return cut_in(axes, place, g_in, spare, depth, wide, quick)

    def copies_scatter(values):
        return lax.psum_scatter(values, axes.copies, scatter_dimension=0)

    def owned(summed):
        return team_swap(summed.reshape(team, parts, depth, wide))

    def weighed_rows(g_proj, weight_in):
        make = lambda begin, end: mm_nt(g_proj[begin:end], weight_in).astype(BF16)
        return Rows(make, model)

    weighed = scatter_corner(axes, weighed_rows(g_proj, weight_in_1), rows)
    weighed, branch_1 = together(weighed, branch_1)
    weighed = scatter_sides(axes, weighed)
    blocks = in_gradient(normed, after(g_proj, weighed[0]), g_conv, g_head, g_skip, False)
    weighed, blocks = together(weighed, blocks)
    summed = copies_scatter(blocks)
    squares = lax.dynamic_slice_in_dim(sums, me * rows, rows, 1)[0][:, None]
    out = (residual_1 + lax.rsqrt(squares / DI + eps) * branch_1.astype(F32)).astype(BF16)
    weighed = add_all(weighed)
    mean = jnp.mean(weighed * residual_1, axis=1, keepdims=True)
    grad = cotangent[0].astype(F32)
    grad = grad + rho_1 * weighed - residual_1 * (rho_1 * rho_1 * rho_1 * mean)

    pulled = grad * gate_rho_0
    kappa = gate_rho_0 * gate_rho_0 * jnp.sum(pulled * branch_0, axis=1, keepdims=True) / DI
    sent = jnp.concatenate([pulled, jnp.broadcast_to(kappa, (rows, LANES))], axis=1)
    gathered = gather_start(axes, sent.astype(BF16))
    g_out = mm_tn(scaled_1, got_1).astype(BF16)
    gathered, g_out = together(gathered, g_out)
    g_out_1 = lax.psum_scatter(g_out, axes.copies, scatter_dimension=0, tiled=True)
    hops, pieces = gather_corner(axes, gathered)
    g_scaled = [mm_nt(piece[:, :model], weight_out_0).astype(BF16) for piece in pieces]
    hops, g_scaled = together(hops, g_scaled)
    last = gather_end(axes, hops)
    pieces = pieces + [last]
    g_scaled = g_scaled + [mm_nt(last[:, :model], weight_out_0).astype(BF16)]
    g_scaled = jnp.concatenate(g_scaled, axis=0)
    kappa = jnp.concatenate([piece[:, model:] for piece in pieces], axis=0)
    g_proj, g_conv, g_head, g_skip = mix_backward(
        place, proj_0, y_0, g_scaled, after(kappa, summed), enter_0, conv[0], head[0], skip[0], False
    )
    g_proj, owned_1 = together(g_proj, owned(summed))
    normed = jnp.concatenate(after(pieces_0, g_proj), axis=0)
    got = jnp.concatenate([piece[:, :model] for piece in after(pieces, g_proj)], axis=0)
    blocks = in_gradient(normed, g_proj, g_conv, g_head, g_skip, paired)
    weighed = scatter_corner(axes, weighed_rows(after(g_proj, blocks), weight_in_0), rows)
    g_out = mm_tn(gated_0, got).astype(BF16)
    if paired:
        corner = sum_corner(axes, blocks)
        weighed, corner, g_out = together(weighed, corner, g_out)
        weighed = scatter_sides(axes, weighed)
        weighed, sides = together(weighed, sum_sides(axes, blocks, corner))
        summed = add_low(blocks[0], *sides)
    else:
        weighed = scatter_sides(axes, weighed)
        summed = copies_scatter(blocks)
    g_out_0 = lax.psum_scatter(g_out, axes.copies, scatter_dimension=0, tiled=True)
    owned_0 = owned(summed)
    weighed = add_all(weighed)
    mean = jnp.mean(weighed * residual_0, axis=1, keepdims=True)
    grad = grad + rho_0 * weighed - residual_0 * (rho_0 * rho_0 * rho_0 * mean)

    grad_in, grad_norm, spare = finish_in(axes, [owned_0, owned_1], in_weight, norm_gain)
    grad_out = jnp.stack([g_out_0, g_out_1]).astype(F32)
    grad_gate = jnp.sum(grad_out * out_weight.astype(F32), axis=2)
    grad_out = grad_out * gate_gain.astype(F32)[:, :, None]

    conv_grad = [
        spare[:, at * taps : (at + 1) * taps, : end - start] for at, (start, end) in enumerate(cuts)
    ]
    conv_grad = jnp.concatenate(conv_grad, axis=2)
    head_grad = spare[:, len(cuts) * taps : len(cuts) * taps + 3, :heads]
    return (
        out[None],
        grad[None],
        grad_norm,
        grad_in,
        conv_grad[:, :CONV],
        conv_grad[:, CONV],
        head_grad[:, 0],
        head_grad[:, 1],
        head_grad[:, 2],
        grad_gate,
        grad_out,
    )


def solution(mesh):
    axes = Axes(mesh.shape["seq"], mesh.shape["fsdp"])
    fine = Mesh(mesh.devices.reshape((2,) * len(axes.every)), axes.every)
    acts = P(axes.fsdp, axes.seq, None)
    flat = P(None, axes.every)
    rows = P(None, axes.every, None)
    taps = P(None, None, axes.every)
    head = P(None, axes.seq)
    return jax.shard_map(
        functools.partial(local, axes),
        mesh=fine,
        in_specs=(acts, acts, flat, rows, taps, flat, head, head, head, flat, rows),
        out_specs=(acts, acts, flat, rows, taps, flat, head, head, head, flat, rows),
        check_vma=False,
    )
```

```python
import functools

import jax
import jax.numpy as jnp
from jax import lax
from jax.experimental import pallas as pl
from jax.experimental.pallas import tpu as pltpu
from jax.sharding import Mesh
from jax.sharding import PartitionSpec as P

HD = 64
NSTATE = 128
STRETCH = 256
DI = 3072
CONV = 4
LANES = 128
BC = 2 * NSTATE

eps = 1e-05

F32 = jnp.float32
BF16 = jnp.bfloat16
EXACT = lax.Precision.HIGHEST
CAP = 48 * 1024 * 1024


def mm(left, right):
    return jnp.dot(left, right, preferred_element_type=F32)


def mm_nt(left, right):
    return lax.dot_general(left, right, (((1,), (1,)), ((), ())), preferred_element_type=F32)


def mm_tn(left, right):
    return lax.dot_general(left, right, (((0,), (0,)), ((), ())), preferred_element_type=F32)


def mm_exact(left, right):
    return jnp.dot(left, right, precision=EXACT, preferred_element_type=F32)


def mm_low(left, right):
    return mm(left.astype(BF16), right.astype(BF16))


def mm_thirds(ones, right):
    lane = iota(right.shape, 1)
    high = right.astype(BF16).astype(F32)
    left = right - high
    middle = left.astype(BF16).astype(F32)
    low = left - middle
    packed = jnp.where(lane < 64, pltpu.roll(middle, 32, 1), pltpu.roll(low, 64, 1))
    packed = jnp.where(lane < 32, high, jnp.where(lane < 96, packed, 0.0))
    total = mm_low(ones, packed)
    total = total + pltpu.roll(total, 96, 1) + pltpu.roll(total, 64, 1)
    return jnp.where(lane < 32, total, 0.0)


def iota(shape, dim):
    return lax.broadcasted_iota(jnp.int32, shape, dim)


def head_spread(width):
    return (iota((LANES, width), 0) == iota((LANES, width), 1) // HD).astype(F32)


def head_fold(width):
    return (iota((width, LANES), 0) // HD == iota((width, LANES), 1)).astype(F32)


def own_steps(raw, turned):
    return pltpu.roll(raw.astype(F32), turned, 1)


def steps_of(raw, head_rows):
    shifted = raw + head_rows[0:1]
    step = jnp.maximum(shifted, 0.0) + jnp.log1p(jnp.exp(-jnp.abs(shifted)))
    return shifted, step


def take(ref, core):
    half = ref.shape[0] // 2
    first = ref[pl.ds(pl.multiple_of(core * half, half), half), :]
    second = ref[pl.ds(pl.multiple_of((1 - core) * half, half), half), :]
    return jnp.concatenate([first, second], axis=0)


def put(ref, core, values, start, end):
    half = ref.shape[0] // 2
    ref[pl.ds(pl.multiple_of(core * half, half), half), start:end] = values[:half]
    ref[pl.ds(pl.multiple_of((1 - core) * half, half), half), start:end] = values[half:]


def pairs(width):
    return [(at, min(at + LANES, width)) for at in range(0, width, LANES)]


def mix_forward_kernel(
    place_ref, proj_ref, conv_ref, head_ref, skip_ref, *refs, with_sums
):
    gated_ref, y_ref, enter_ref = refs[with_sums : with_sums + 3]
    state_ref, ext_ref = refs[-2:]
    core, turned = place_ref[0] & 1, place_ref[1]
    rows = proj_ref.shape[0]
    wide = gated_ref.shape[1]
    chans = wide + BC

    @pl.when(pl.program_id(0) == 0)
    def _():
        state_ref[...] = jnp.zeros_like(state_ref)
        ext_ref[0:8, :] = jnp.zeros((8, chans), F32)

    proj = take(proj_ref, core)
    ext_ref[8 : 8 + rows, :] = proj[:, wide : wide + chans].astype(F32)
    pre = conv_ref[CONV : CONV + 1, :] + conv_ref[0:1, :] * ext_ref[5 : 5 + rows, :]
    for lag in range(1, CONV):
        pre = pre + conv_ref[lag : lag + 1, :] * ext_ref[5 + lag : 5 + lag + rows, :]
    ext_ref[0:8, :] = ext_ref[rows : rows + 8, :]
    act = pre * jax.nn.sigmoid(pre)
    x = act[:, :wide]
    b_low = act[:, wide : wide + NSTATE].astype(BF16)
    c_low = act[:, wide + NSTATE :].astype(BF16)

    _, step = steps_of(own_steps(proj[:, wide + chans :], turned), head_ref)
    decay = -step * head_ref[1:2, :]
    lower = iota((rows, rows), 0) >= iota((rows, rows), 1)
    cum = mm_thirds(lower.astype(F32), decay)
    cum_t = jnp.transpose(cum)
    spread = head_spread(wide)
    total = cum[rows - 1 : rows, :]
    step_wide = mm_low(step, spread)
    grown = mm_low(jnp.exp(cum), spread)
    ending_wide = mm_low(step * jnp.exp(total - cum), spread)
    kept = mm_exact(jnp.broadcast_to(jnp.exp(total), (8, LANES)), spread)[0:1, :]

    scores = mm_nt(c_low, b_low)
    weighted = x * step_wide
    weighted_low = weighted.astype(BF16)
    within = []
    for start, end in pairs(wide):
        both = weighted_low[:, start:end]
        parts = []
        for head in range(start // HD, end // HD):
            gap = cum[:, head : head + 1] - cum_t[head : head + 1, :]
            mixed = jnp.where(lower, jnp.exp(gap), 0.0) * scores
            parts.append(mm(mixed.astype(BF16), both))
        if len(parts) == 2:
            first = iota((rows, end - start), 1) < HD
            within.append(jnp.where(first, parts[0], parts[1]))
        else:
            within.append(parts[0])
    within = jnp.concatenate(within, axis=1)
    state = state_ref[...]
    enter_ref[0] = state
    carried = grown * mm(c_low, state.astype(BF16))
    y = within + carried + skip_ref[0:1, :] * x
    gate = proj[:, :wide].astype(F32)
    gated = (y * (gate * jax.nn.sigmoid(gate))).astype(BF16)
    put(gated_ref, core, gated, 0, wide)
    if with_sums:
        gated = gated.astype(F32)
        ones = jnp.ones((8, wide), BF16)
        product = gated * take(refs[0], core).astype(F32)
        squares = mm_nt(ones, (gated * gated).astype(BF16))
        product = mm_nt(ones, product.astype(BF16))
        refs[4][...] = jnp.where(iota((8, rows), 0) == 0, squares, product)
    put(y_ref, core, y.astype(BF16), 0, wide)
    state_ref[...] = state * kept + mm_tn(b_low, (x * ending_wide).astype(BF16))


def mix_forward(place, proj, conv_rows, head_rows, wide_rows, pulled=None):
    with_sums = pulled is not None
    length, width = proj.shape
    wide = wide_rows.shape[1]
    count = length // STRETCH
    whole = lambda shape: pl.BlockSpec(shape, lambda i, at: (0,) * len(shape))
    part = lambda cols: pl.BlockSpec((STRETCH, cols), lambda i, at: (i ^ (at[0] >> 1), 0))
    return pl.pallas_call(
        functools.partial(mix_forward_kernel, with_sums=with_sums),
        grid_spec=pltpu.PrefetchScalarGridSpec(
            num_scalar_prefetch=1,
            grid=(count,),
            in_specs=[
                part(width),
                whole(conv_rows.shape),
                whole(head_rows.shape),
                whole(wide_rows.shape),
            ]
            + [part(wide)] * with_sums,
            out_specs=[
                part(wide),
                part(wide),
                pl.BlockSpec((1, NSTATE, wide), lambda i, at: (i, 0, 0)),
            ]
            + [pl.BlockSpec((8, STRETCH), lambda i, at: (0, i))] * with_sums,
            scratch_shapes=[
                pltpu.VMEM((NSTATE, wide), F32),
                pltpu.VMEM((STRETCH + 8, wide + BC), F32),
            ],
        ),
        out_shape=[
            jax.ShapeDtypeStruct((length, wide), BF16),
            jax.ShapeDtypeStruct((length, wide), BF16),
            jax.ShapeDtypeStruct((count, NSTATE, wide), F32),
        ]
        + [jax.ShapeDtypeStruct((8, length), F32)] * with_sums,
        compiler_params=pltpu.CompilerParams(
            dimension_semantics=("arbitrary",), vmem_limit_bytes=CAP
        ),
        cost_estimate=pl.CostEstimate(
            flops=length * wide * 18000, bytes_accessed=length * 6000, transcendentals=0
        ),
        name="mix_forward",
    )(place, proj, conv_rows, head_rows, wide_rows, *[pulled] * with_sums)


def mix_backward_kernel(
    place_ref,
    proj_ref,
    before_ref,
    y_ref,
    pulled_ref,
    kappa_ref,
    enter_ref,
    conv_ref,
    head_ref,
    wide_ref,
    *refs,
    as_rows,
):
    out_ref, conv_grad_ref, head_grad_ref, skip_grad_ref = refs[:4]
    dstate_ref, ext_ref, gext_ref, rows_ref = refs[-4:]
    core, turned = place_ref[0] & 1, place_ref[1]
    rows = proj_ref.shape[0]
    wide = y_ref.shape[1]
    chans = wide + BC
    turn = pl.program_id(0)

    @pl.when(turn == 0)
    def _():
        dstate_ref[...] = jnp.zeros_like(dstate_ref)
        gext_ref[rows : rows + 8, :] = jnp.zeros((8, chans), F32)
        conv_grad_ref[...] = jnp.zeros_like(conv_grad_ref)
        head_grad_ref[...] = jnp.zeros_like(head_grad_ref)
        skip_grad_ref[...] = jnp.zeros_like(skip_grad_ref)
        rows_ref[...] = jnp.zeros_like(rows_ref)

    before = before_ref[8:16, wide : wide + chans].astype(F32)
    ext_ref[0:8, :] = jnp.where(turn == pl.num_programs(0) - 1, 0.0, before)
    proj = take(proj_ref, core)
    ext_ref[8 : 8 + rows, :] = proj[:, wide : wide + chans].astype(F32)
    pre = conv_ref[CONV : CONV + 1, :] + conv_ref[0:1, :] * ext_ref[5 : 5 + rows, :]
    for lag in range(1, CONV):
        pre = pre + conv_ref[lag : lag + 1, :] * ext_ref[5 + lag : 5 + lag + rows, :]
    sig = jax.nn.sigmoid(pre)
    act = pre * sig
    slope = sig * (1.0 + pre * (1.0 - sig))
    x = act[:, :wide]
    x_low = x.astype(BF16)
    b_low = act[:, wide : wide + NSTATE].astype(BF16)
    c_low = act[:, wide + NSTATE :].astype(BF16)

    shifted, step = steps_of(own_steps(proj[:, wide + chans :], turned), head_ref)
    rate = head_ref[1:2, :]
    decay = -step * rate
    lower = iota((rows, rows), 0) >= iota((rows, rows), 1)
    upper = iota((rows, rows), 0) <= iota((rows, rows), 1)
    cum = mm_thirds(lower.astype(F32), decay)
    cum_t = jnp.transpose(cum)
    spread = head_spread(wide)
    fold = head_fold(wide)
    total = cum[rows - 1 : rows, :]
    step_wide = mm_low(step, spread)
    grown = mm_low(jnp.exp(cum), spread)
    to_end = mm_low(jnp.exp(total - cum), spread)
    kept = mm_exact(jnp.broadcast_to(jnp.exp(total), (8, LANES)), spread)[0:1, :]

    gate = proj[:, :wide].astype(F32)
    y = take(y_ref, core).astype(F32)
    gate_sig = jax.nn.sigmoid(gate)
    gate_act = gate * gate_sig
    gated = y * gate_act
    if as_rows:
        g_gated = take(pulled_ref, core).astype(F32)
        sums = jnp.transpose(kappa_ref[...])
        rho = lax.rsqrt(sums[:, 0:1] / DI + eps)
        kappa = rho * rho * rho * sums[:, 1:2] / DI
        g_gated = rho * g_gated - gated * kappa
        put(refs[4], core, (gated * rho).astype(BF16), 0, wide)
        copies = []
    else:
        copies = [refs[4], refs[5]]
        g_gated = take(pulled_ref, core).astype(F32)
        g_gated = g_gated - gated * take(kappa_ref, core)[:, 0:1].astype(F32)
    dy = g_gated * gate_act
    g_gate = g_gated * y * (gate_sig * (1.0 + gate * (1.0 - gate_sig)))
    put(out_ref, core, g_gate.astype(BF16), 0, wide)
    for copy_ref in copies[:1]:
        put(copy_ref, core, g_gate.astype(BF16), 0, wide)
    dy_low = dy.astype(BF16)
    skip_grad_ref[0:1, :] += jnp.sum(x * dy, axis=0, keepdims=True)

    scores_t = mm_nt(b_low, c_low)
    lane = iota((rows, LANES), 1)
    d_scores = jnp.zeros((rows, rows), F32)
    column = jnp.zeros((rows, LANES), F32)
    inner = []
    for start, end in pairs(wide):
        both_dy = dy_low[:, start:end]
        both_x = x_low[:, start:end]
        side = iota((rows, end - start), 1) // HD
        parts = []
        for head in range(start // HD, end // HD):
            gap = cum_t[head : head + 1, :] - cum[:, head : head + 1]
            fade = jnp.where(upper, jnp.exp(gap), 0.0)
            own = jnp.where(side == head - start // HD, both_x, jnp.zeros_like(both_x))
            faded = fade * mm_nt(own, both_dy)
            stepped = faded * step[:, head : head + 1]
            d_scores = d_scores + stepped
            parts.append(mm((scores_t * fade).astype(BF16), both_dy))
            column = jnp.where(
                lane == head, jnp.sum(scores_t * faded, axis=1, keepdims=True), column
            )
            rows_ref[head : head + 1, :] = jnp.sum(scores_t * stepped, axis=0, keepdims=True)
        if len(parts) == 2:
            inner.append(jnp.where(side == 0, parts[0], parts[1]))
        else:
            inner.append(parts[0])
    inner = jnp.concatenate(inner, axis=1)

    enter = enter_ref[0]
    enter_low = enter.astype(BF16)
    dstate = dstate_ref[...]
    dstate_low = dstate.astype(BF16)
    outer = to_end * mm(b_low, dstate_low)
    g_x = step_wide * (inner + outer) + wide_ref[0:1, :] * dy
    dy_grown = dy * grown
    dy_grown_low = dy_grown.astype(BF16)
    carried_sum = mm_low(dy_grown * mm(c_low, enter_low), fold)
    outer_sum = mm_low(x * outer, fold)
    state_sum = mm_exact(
        jnp.broadcast_to(jnp.sum(enter * dstate, axis=0, keepdims=True), (8, wide)), fold
    )[0:1, :]
    step_outer = step * outer_sum
    g_cum = jnp.transpose(rows_ref[...]) + carried_sum - step * column - step_outer
    g_total = (
        jnp.sum(step_outer, axis=0, keepdims=True)
        + jnp.exp(total) * state_sum
    )
    g_decay = mm_thirds(upper.astype(F32), g_cum) + g_total
    scaled_decay = rate * g_decay
    g_raw = (column + outer_sum - scaled_decay) * jax.nn.sigmoid(shifted)
    head_grad_ref[0:1, :] += jnp.sum(g_raw, axis=0, keepdims=True)
    head_grad_ref[1:2, :] -= jnp.sum(step * scaled_decay, axis=0, keepdims=True)
    g_raw = pltpu.roll(g_raw, lax.rem(LANES - turned, LANES), 1)
    put(out_ref, core, g_raw.astype(BF16), wide + chans, wide + chans + LANES)
    for copy_ref in copies[1:]:
        put(copy_ref, core, g_raw.astype(BF16), chans, chans + LANES)

    d_low = d_scores.astype(BF16)
    ending = (x * (step_wide * to_end)).astype(BF16)
    g_b = mm(d_low, c_low) + mm_nt(ending, dstate_low)
    g_c = mm_tn(d_low, b_low) + mm_nt(dy_grown_low, enter_low)
    dstate_ref[...] = dstate * kept + mm_tn(c_low, dy_grown_low)

    gext_ref[0:rows, :wide] = g_x * slope[:, :wide]
    gext_ref[0:rows, wide : wide + NSTATE] = g_b * slope[:, wide : wide + NSTATE]
    gext_ref[0:rows, wide + NSTATE :] = g_c * slope[:, wide + NSTATE :]
    g_pre = gext_ref[0:rows, :]
    g_in = conv_ref[CONV - 1 : CONV, :] * g_pre
    for lag in range(CONV - 1):
        g_in = g_in + conv_ref[lag : lag + 1, :] * gext_ref[3 - lag : 3 - lag + rows, :]
    put(out_ref, core, g_in.astype(BF16), wide, wide + chans)
    for copy_ref in copies[1:]:
        put(copy_ref, core, g_in.astype(BF16), 0, chans)
    for lag in range(CONV):
        conv_grad_ref[lag : lag + 1, :] += jnp.sum(
            ext_ref[5 + lag : 5 + lag + rows, :] * g_pre, axis=0, keepdims=True
        )
    conv_grad_ref[CONV : CONV + 1, :] += jnp.sum(g_pre, axis=0, keepdims=True)
    gext_ref[rows : rows + 8, :] = gext_ref[0:8, :]


def mix_backward(place, proj, y, pulled, kappa, enter, conv_rows, head_rows, wide_rows, as_rows):
    length, width = proj.shape
    wide = wide_rows.shape[1]
    count = length // STRETCH
    whole = lambda shape: pl.BlockSpec(shape, lambda i, at: (0,) * len(shape))
    part = lambda cols: pl.BlockSpec((STRETCH, cols), lambda i, at: ((count - 1 - i) ^ (at[0] >> 1), 0))
    half = STRETCH // 2

    def last_rows(i, at):
        pair = jnp.maximum(count - 2 - i, 0) ^ (at[0] >> 1)
        block = 2 * pair + 1 - (at[0] & 1)
        return block * (half // 16) + half // 16 - 1, 0

    before = pl.BlockSpec((16, width), last_rows)
    turn = lambda i, at: (count - 1 - i) ^ (at[0] >> 1)
    if as_rows:
        scales = pl.BlockSpec((8, STRETCH), lambda i, at: (0, count - 1 - i))
    else:
        last = kappa.shape[1] // LANES - 1
        scales = pl.BlockSpec((STRETCH, LANES), lambda i, at: (turn(i, at), last))
    return pl.pallas_call(
        functools.partial(mix_backward_kernel, as_rows=as_rows),
        grid_spec=pltpu.PrefetchScalarGridSpec(
            num_scalar_prefetch=1,
            grid=(count,),
            in_specs=[
                part(width),
                before,
                part(wide),
                part(wide),
                scales,
                pl.BlockSpec((1, NSTATE, wide), lambda i, at: (count - 1 - i, 0, 0)),
                whole(conv_rows.shape),
                whole(head_rows.shape),
                whole(wide_rows.shape),
            ],
            out_specs=[
                part(width),
                whole((8, wide + BC)),
                whole((8, LANES)),
                whole((8, wide)),
            ]
            + ([part(wide)] if as_rows else [part(wide), part(width - wide)]),
            scratch_shapes=[
                pltpu.VMEM((NSTATE, wide), F32),
                pltpu.VMEM((STRETCH + 8, wide + BC), F32),
                pltpu.VMEM((STRETCH + 8, wide + BC), F32),
                pltpu.VMEM((LANES, STRETCH), F32),
            ],
        ),
        out_shape=[
            jax.ShapeDtypeStruct((length, width), BF16),
            jax.ShapeDtypeStruct((8, wide + BC), F32),
            jax.ShapeDtypeStruct((8, LANES), F32),
            jax.ShapeDtypeStruct((8, wide), F32),
        ]
        + [jax.ShapeDtypeStruct((length, wide), BF16)]
        + [jax.ShapeDtypeStruct((length, width - wide), BF16)] * (not as_rows),
        compiler_params=pltpu.CompilerParams(
            dimension_semantics=("arbitrary",), vmem_limit_bytes=CAP
        ),
        cost_estimate=pl.CostEstimate(
            flops=length * wide * 40000, bytes_accessed=length * 9000, transcendentals=0
        ),
        name="mix_backward",
    )(place, proj, proj, y, pulled, kappa, enter, conv_rows, head_rows, wide_rows)


def add_low(*terms):
    total = terms[0].astype(F32)
    for term in terms[1:]:
        total = total + term.astype(F32)
    return total.astype(BF16)


def rms(values):
    return lax.rsqrt(jnp.mean(values * values, axis=-1, keepdims=True) + eps)


def after(values, *others):
    return lax.optimization_barrier((values, others))[0]


def flip(values, axis):
    return lax.ppermute(values, axis, [(0, 1), (1, 0)])


def flip_both(values, names):
    return lax.ppermute(values, names, [(0, 3), (1, 2), (2, 1), (3, 0)])


def turn_back(own, near, far, residual, rho, grad, gate_rho, branch):
    rows, model = own.shape

    def kernel(own_ref, near_ref, far_ref, res_ref, rho_ref, grad_ref, gate_ref, br_ref, *refs):
        grad_out, sent_out = refs
        weighed = own_ref[...].astype(F32) + near_ref[...].astype(F32) + far_ref[...].astype(F32)
        res, rho, gate = res_ref[...], rho_ref[...], gate_ref[...]
        mean = jnp.sum(weighed * res, axis=1, keepdims=True) / model
        total = grad_ref[...].astype(F32) + rho * weighed - res * (rho * rho * rho * mean)
        grad_out[...] = total
        pulled = total * gate
        kappa = gate * gate * jnp.sum(pulled * br_ref[...], axis=1, keepdims=True) / DI
        sent_out[:, :model] = pulled.astype(BF16)
        sent_out[:, model:] = jnp.broadcast_to(kappa, (rows, LANES)).astype(BF16)

    return pl.pallas_call(
        kernel,
        in_specs=all_vmem(8),
        out_specs=all_vmem(2),
        out_shape=[
            jax.ShapeDtypeStruct((rows, model), F32),
            jax.ShapeDtypeStruct((rows, model + LANES), BF16),
        ],
        compiler_params=pltpu.CompilerParams(vmem_limit_bytes=CAP),
        name="turn_back",
    )(own, near, far, residual, rho, grad, gate_rho, branch)


class Axes:
    def __init__(self, seq, fsdp):
        between = tuple(f"b{i}" for i in range((seq // 4).bit_length() - 1))
        before = tuple(f"p{i}" for i in range((fsdp // 2).bit_length() - 1))
        self.seq = ("a",) + between + ("c",)
        self.fsdp = before + ("q",)
        self.every = self.seq + self.fsdp
        self.links = ("a",) + between
        self.team = self.seq
        self.copies = self.fsdp

    def bits(self, names, at):
        value = 0
        for spot, name in enumerate(names):
            if at >> (len(names) - 1 - spot) & 1:
                value |= 1 << (len(self.every) - 1 - self.every.index(name))
        return value

    def at(self, me, r, k, relative):
        if relative:
            me = me ^ self.bits(self.copies, r)
        else:
            me = me & ~self.bits(self.copies, -1) | self.bits(self.copies, r)
        return me & ~self.bits(self.team, -1) | self.bits(self.team, k)


def all_vmem(count):
    return [pl.BlockSpec(memory_space=pltpu.VMEM)] * count


SMEM = pl.BlockSpec(memory_space=pltpu.SMEM)


def split_in(axes, weights, gain, spare, layer):
    team = 2 ** len(axes.team)
    depth, columns = weights.shape[1:]
    wide = DI // team
    parts = 2 + 3 * LANES // wide

    def kernel(weight_ref, gain_ref, spare_ref, out_ref):
        scale = gain_ref[...].astype(F32)
        tail = (weight_ref[0, :, 2 * DI :].astype(F32) * scale).astype(BF16)
        tail = jnp.concatenate([tail, spare_ref[...]], axis=1)
        for k in range(team):
            for part in range(2):
                base = (1 - part) * DI + k * wide
                cut = weight_ref[0, :, base : base + wide].astype(F32)
                out_ref[k, part] = (cut * scale).astype(BF16)
            for part in range(2, parts):
                out_ref[k, part] = tail[:, (part - 2) * wide : (part - 1) * wide]

    whole = lambda shape: pl.BlockSpec(shape, lambda i: (0,) * len(shape))
    return pl.pallas_call(
        kernel,
        grid=(1,),
        in_specs=[
            pl.BlockSpec((1, depth, columns), lambda i: (layer, 0, 0)),
            whole((depth, 1)),
            whole(spare.shape),
        ],
        out_specs=whole((team, parts, depth, wide)),
        out_shape=jax.ShapeDtypeStruct((team, parts, depth, wide), BF16),
        compiler_params=pltpu.CompilerParams(vmem_limit_bytes=CAP),
        name="split_in",
    )(weights, gain[:, None], spare)


def columns_of(part, wide):
    return (1 - part if part < 2 else part) * wide


def join_in(axes, place, lists, relative):
    copies, team = len(lists), 2 ** len(axes.team)
    parts = len(lists[0]) // team
    depth, wide = lists[0][0][0].shape[-2:]
    rows = copies * team * depth
    extra = min(depth, 32)
    if depth % 16:
        flat = jnp.stack([jnp.stack([array[index] for array, index in row]) for row in lists])
        flat = flat.reshape(copies * team, parts, depth, wide)
        flat = jnp.concatenate(
            [flat[:, 1], flat[:, 0]] + [flat[:, part] for part in range(2, parts)], axis=-1
        )
        at = [axes.at(place[2], r, k, relative) for r in range(copies) for k in range(team)]
        flat = jnp.zeros_like(flat).at[jnp.stack(at)].set(flat)
        return flat.reshape(rows, -1), flat[:, :extra, -LANES:]

    arrays = []
    for row in lists:
        for array, _ in row:
            if not any(array is known for known in arrays):
                arrays.append(array)
    which = lambda array: next(i for i, known in enumerate(arrays) if known is array)

    def kernel(place_ref, *refs):
        out_ref, spare_ref = refs[-2:]
        for r in range(copies):
            for k in range(team):
                spot = axes.at(place_ref[2], r, k, relative)
                at = pl.ds(pl.multiple_of(spot * depth, 16), depth)
                for part in range(parts):
                    array, index = lists[r][parts * k + part]
                    base = columns_of(part, wide)
                    out_ref[at, base : base + wide] = refs[which(array)][index]
                index = index if isinstance(index, tuple) else (index,)
                index += (slice(0, extra), slice(wide - LANES, wide))
                spare_ref[spot] = refs[which(array)][index]

    return pl.pallas_call(
        kernel,
        in_specs=[SMEM] + all_vmem(len(arrays)),
        out_specs=all_vmem(2),
        out_shape=[
            jax.ShapeDtypeStruct((rows, parts * wide), BF16),
            jax.ShapeDtypeStruct((copies * team, extra, LANES), BF16),
        ],
        compiler_params=pltpu.CompilerParams(vmem_limit_bytes=CAP),
        name="join_in",
    )(place, *arrays)


def cut_in(axes, place, grad, spare, depth, wide, relative):
    copies, team = 2 ** len(axes.copies), 2 ** len(axes.team)
    parts = grad.shape[1] // wide
    pairs_at = [(r, k) for r in range(copies) for k in range(team)]
    if spare is not None:
        extra, room = spare.shape[1:]
    if depth % 16:
        flat = grad.reshape(copies * team, depth, -1)
        if spare is not None:
            flat = flat.at[:, :extra, -room:].set(spare)
        at = jnp.stack([axes.at(place[2], r, k, relative) for r, k in pairs_at])
        flat = jnp.take(flat, at, axis=0).reshape(copies, team, depth, parts, wide)
        flat = flat.transpose(0, 1, 3, 2, 4).reshape(copies, team * parts, depth, wide)
        return [flat[r] for r in range(copies)]

    def kernel(place_ref, grad_ref, *refs):
        out_refs = refs[-copies:]
        for r, k in pairs_at:
            spot = axes.at(place_ref[2], r, k, relative)
            rows = pl.ds(pl.multiple_of(spot * depth, 16), depth)
            for part in range(parts):
                out_refs[r][parts * k + part] = grad_ref[rows, part * wide : (part + 1) * wide]
            if spare is not None:
                out_refs[r][parts * k + parts - 1, 0:extra, wide - room :] = refs[0][spot]

    given = [] if spare is None else [spare]
    return pl.pallas_call(
        kernel,
        in_specs=[SMEM] + all_vmem(1 + len(given)),
        out_specs=all_vmem(copies),
        out_shape=[jax.ShapeDtypeStruct((team * parts, depth, wide), BF16)] * copies,
        compiler_params=pltpu.CompilerParams(vmem_limit_bytes=CAP),
        name="cut_in",
    )(place, grad, *given)


def join_out(axes, place, blocks, grad):
    copies = len(blocks)
    count, depth, wide = blocks[0].shape
    each, model = grad.shape[0] // copies, grad.shape[1]
    more = (each // depth) * (model // wide)

    def kernel(place_ref, grad_ref, *refs):
        block_refs, out_refs = refs[:copies], refs[copies:]
        for r in range(copies):
            out_refs[r][0:count] = block_refs[r][...]
            copy = (place_ref[2] & axes.bits(axes.copies, -1)) ^ axes.bits(axes.copies, r)
            for at in range(more):
                row, column = at // (model // wide), at % (model // wide)
                first = copy * each + row * depth
                out_refs[r][count + at] = grad_ref[
                    pl.ds(pl.multiple_of(first, 16), depth), column * wide : (column + 1) * wide
                ]

    return pl.pallas_call(
        kernel,
        in_specs=[SMEM] + all_vmem(1 + copies),
        out_specs=all_vmem(copies),
        out_shape=[jax.ShapeDtypeStruct((count + more, depth, wide), BF16)] * copies,
        compiler_params=pltpu.CompilerParams(vmem_limit_bytes=CAP),
        name="join_out",
    )(place, grad, *blocks)


def finish_in(axes, grads, weight, gain):
    layers, depth, columns = weight.shape
    team = 2 ** len(axes.team)
    wide = DI // team
    parts = grads[0][1].shape[1]
    room = (parts - 1) * wide - (columns - 2 * DI)

    def kernel(weight_ref, gain_ref, *refs):
        grad_ref, sum_ref, spare_ref = refs[-3:]
        for layer in range(layers):
            gate_ref, rest_ref = refs[2 * layer : 2 * layer + 2]
            scale = gain_ref[layer].astype(F32)
            tails = []
            for part in range(1, parts):
                tail = rest_ref[0, part].astype(F32)
                for k in range(1, team):
                    tail = tail + rest_ref[k, part].astype(F32)
                tails.append(tail)
            tail = jnp.concatenate(tails, axis=1)
            spare_ref[layer] = tail[:, columns - 2 * DI :]
            tail = tail[:, : columns - 2 * DI]
            grad_ref[layer, :, 2 * DI :] = tail * scale
            total = jnp.sum(tail * weight_ref[layer, :, 2 * DI :].astype(F32), 1, keepdims=True)
            for k in range(team):
                for base, values in ((0, gate_ref[k, 0]), (DI, rest_ref[k, 0])):
                    values = values.astype(F32)
                    spot = slice(base + k * wide, base + (k + 1) * wide)
                    grad_ref[layer, :, spot] = values * scale
                    total = total + jnp.sum(
                        values * weight_ref[layer, :, spot].astype(F32), 1, keepdims=True
                    )
            sum_ref[layer] = jnp.broadcast_to(total, (depth, LANES))

    grads, sums, spares = pl.pallas_call(
        kernel,
        in_specs=all_vmem(2 + 2 * layers),
        out_specs=all_vmem(3),
        out_shape=[
            jax.ShapeDtypeStruct((layers, depth, columns), F32),
            jax.ShapeDtypeStruct((layers, depth, LANES), F32),
            jax.ShapeDtypeStruct((layers, depth, room), F32),
        ],
        compiler_params=pltpu.CompilerParams(vmem_limit_bytes=CAP),
        name="finish_in",
    )(weight, gain[..., None], *[part for pair in grads for part in pair])
    return grads, sums[:, :, 0], spares


def together(*values):
    return lax.optimization_barrier(values)


def copies_start(axes, whole):
    slow, fast = axes.copies
    return whole, flip(whole, fast), flip(whole, slow)


def copies_corner(axes, parts):
    slow, fast = axes.copies
    whole, one, two = parts
    half = whole.shape[0] // 2
    return flip(one[:half], slow), flip(two[half:], fast)


def copies_whole_corner(axes, parts):
    return (flip(parts[1], axes.copies[0]),)


def copies_lists(parts, corner):
    count = parts[0].shape[0]
    each = count // len(corner)
    lists = [[(array, at) for at in range(count)] for array in parts]
    return lists + [[(corner[at // each], at % each) for at in range(count)]]


def sum_corner(axes, pieces):
    slow, fast = axes.copies
    half = pieces[3].shape[0] // 2
    return flip(pieces[3][:half], slow), flip(pieces[3][half:], fast)


def sum_sides(axes, pieces, corner):
    slow, fast = axes.copies
    half = pieces[0].shape[0] // 2
    to_fast = jnp.concatenate([add_low(pieces[1][:half], corner[0]), pieces[1][half:]], axis=0)
    to_slow = jnp.concatenate([pieces[2][:half], add_low(pieces[2][half:], corner[1])], axis=0)
    return flip(to_fast, fast), flip(to_slow, slow)


def sum_direct(axes, pieces):
    slow, fast = axes.copies
    return flip(pieces[1], fast), flip(pieces[2], slow), flip_both(pieces[3], axes.copies)


def gather_start(axes, rows):
    if len(axes.links) != 2:
        return (rows,)
    far, near = axes.links
    return rows, flip(rows, "c"), flip(rows, far), flip(rows, near)


def gather_corner(axes, parts):
    if len(axes.links) != 2:
        return parts, []
    rows, other, from_far, from_near = parts
    sides = jnp.stack([from_near, from_far])
    sides = jnp.stack([sides, flip(sides, "c")], axis=1).reshape(-1, rows.shape[1])
    corner = (flip(from_far, axes.links[1]),)
    return corner, [jnp.concatenate([rows, other], axis=0), sides]


def gather_end(axes, corner):
    if len(axes.links) != 2:
        whole = corner[0][None]
        for name in reversed(axes.links):
            whole = jnp.concatenate([whole, flip(whole, name)], axis=0)
        whole = jnp.stack([whole, flip(whole, "c")], axis=1)
        return whole.reshape(-1, corner[0].shape[1])
    return jnp.concatenate([corner[0], flip(corner[0], "c")], axis=0)


def core_sum(values, rows):
    both = values.reshape(-1, 2, rows, values.shape[-1])
    return add_low(both[:, 0], flip(both[:, 1], "c"))


def scatter_corner(axes, rows_of, rows):
    team = 2 ** len(axes.team)
    if len(axes.links) != 2:
        return (core_sum(rows_of(0, team * rows, ()), rows),)
    corner = core_sum(rows_of(6 * rows, 8 * rows, ()), rows)[0]
    hop = flip(corner, axes.links[1])
    sides = core_sum(rows_of(2 * rows, 6 * rows, corner), rows)
    return hop, sides, core_sum(rows_of(0, 2 * rows, corner), rows)[0]


def scatter_sides(axes, parts):
    if len(axes.links) != 2:
        whole = parts[0]
        for name in axes.links:
            half = whole.shape[0] // 2
            whole = add_low(whole[:half], flip(whole[half:], name))
        return (whole[0],)
    far, near = axes.links
    hop, sides, own = parts
    return own, flip(sides[0], near), flip(add_low(sides[1], hop), far)


def add_all(parts):
    total = parts[0].astype(F32)
    for part in parts[1:]:
        total = total + part.astype(F32)
    return total


def local(
    axes,
    tokens,
    cotangent,
    norm_gain,
    in_weight,
    conv_kernel,
    conv_shift,
    dt_bias,
    a_log,
    skip_gain,
    gate_gain,
    out_weight,
):
    layers, depth, columns = in_weight.shape
    rows = tokens.shape[1]
    model = tokens.shape[2]
    heads = dt_bias.shape[1]
    wide = heads * HD
    team = 2 ** len(axes.team)
    copies = 2 ** len(axes.copies)
    me = lax.axis_index(axes.team)
    all_at = lax.axis_index(axes.every)
    place = jnp.stack([me, lax.rem(LANES - me * heads, LANES), all_at]).astype(jnp.int32)

    n_conv = conv_shift.shape[1]
    room = 3 * LANES - (columns - 2 * DI)
    cuts = [(at, min(at + room, n_conv)) for at in range(0, n_conv, room)]
    taps = CONV + 1
    conv = jnp.concatenate([conv_kernel, conv_shift[:, None]], axis=1).reshape(-1, n_conv)
    conv = [jnp.pad(conv[:, at:end], ((0, 0), (0, room - end + at))) for at, end in cuts]
    conv = jnp.concatenate(conv, axis=0)
    spare = jnp.pad(conv, ((0, depth - conv.shape[0]), (0, 0)))

    def team_swap(blocks):
        return lax.all_to_all(blocks, axes.team, split_axis=0, concat_axis=0)

    def in_blocks(layer, start):
        blocks = split_in(axes, in_weight, after(norm_gain[layer], start), spare, layer)
        return team_swap(blocks).reshape(-1, depth, wide)

    def in_columns(blocks):
        got = lax.all_gather(blocks, axes.copies)
        lists = [[(got, (r, k)) for k in range(blocks.shape[0])] for r in range(copies)]
        return join_in(axes, place, lists, False)

    def out_rows(layer, start):
        gain = after(gate_gain[layer], start)
        mine = out_weight[layer].astype(F32) * gain.astype(F32)[:, None]
        return lax.all_gather(mine.astype(BF16), axes.copies, axis=0, tiled=True)

    paired = len(axes.copies) == 2
    assert layers == 2

    weight_out_0 = out_rows(0, tokens)
    blocks = in_blocks(0, tokens)
    parts = blocks.shape[0] // team
    residual_0 = tokens[0].astype(F32)
    rho_0 = rms(residual_0)
    blocks, sent = together(blocks, (residual_0 * rho_0).astype(BF16))
    gathered = gather_start(axes, sent)
    if paired:
        copied, gathered = together(copies_start(axes, blocks), gathered)
    hops, pieces_0 = gather_corner(axes, gathered)
    cot = gather_start(axes, after(cotangent[0], gathered))
    if paired:
        corner = copies_corner(axes, copied)
        corner, hops, weight_out_0 = together(corner, hops, weight_out_0)
        weight_in_0, beside = join_in(axes, place, copies_lists(copied, corner), True)
    else:
        weight_in_0, beside = in_columns(blocks)
    last = gather_end(axes, hops)
    last, cot = together(last, cot)
    pieces_0 = pieces_0 + [last]
    proj_0 = [mm(piece, weight_in_0).astype(BF16) for piece in pieces_0]
    proj_0 = jnp.concatenate(proj_0, axis=0)

    conv = beside[:, : conv.shape[0], LANES - room :]
    conv = conv.reshape(-1, len(cuts), layers * taps, room).transpose(0, 2, 1, 3)
    conv = conv.reshape(-1, layers * taps, len(cuts) * room)[:, :, :n_conv]
    conv = conv.reshape(-1, layers, taps, n_conv)
    conv = conv.transpose(1, 2, 0, 3).reshape(layers, CONV + 1, -1).astype(F32)
    conv = jnp.pad(conv, ((0, 0), (0, 7 - CONV), (0, 0)))
    conv = jnp.concatenate(
        [lax.dynamic_slice_in_dim(conv, me * wide, wide, 2), conv[:, :, DI:]], axis=2
    )
    head = jnp.stack([dt_bias, a_log, skip_gain], axis=1)
    skip = jnp.pad(jnp.repeat(head[:, 2:], HD, axis=2), ((0, 0), (0, 7), (0, 0)))
    head = jnp.stack([head[:, 0], jnp.exp(head[:, 1])], axis=1)
    head = jnp.pad(head, ((0, 0), (0, 6), (0, LANES - heads)))

    blocks = in_blocks(1, last)
    gated_0, y_0, enter_0 = mix_forward(place, proj_0, conv[0], head[0], skip[0])
    cot_hops, cot = gather_corner(axes, cot)
    (gated_0, y_0, enter_0), blocks, cot_hops = together((gated_0, y_0, enter_0), blocks, cot_hops)
    cot = cot + [gather_end(axes, cot_hops)]
    weight_out_1 = out_rows(1, gated_0)

    def branch_rows(begin, end, others):
        cut = after(gated_0, others)[begin:end]
        squares = jnp.sum(jnp.square(cut.astype(F32)), axis=1, keepdims=True)
        squares = jnp.broadcast_to(squares, (end - begin, LANES))
        return jnp.concatenate([mm(cut, weight_out_0), squares], axis=1).astype(BF16)

    got = together(*scatter_corner(axes, branch_rows, rows))
    got = scatter_sides(axes, got)
    if paired:
        got, copied = together(got, copies_start(axes, blocks))
    got = add_all(got)
    branch_0 = got[:, :model]
    gate_rho_0 = lax.rsqrt(got[:, model : model + 1] / DI + eps)

    residual_1 = residual_0 + gate_rho_0 * branch_0
    rho_1 = rms(residual_1)
    gathered = gather_start(axes, (residual_1 * rho_1).astype(BF16))
    g_scaled = jnp.concatenate([mm_nt(piece, weight_out_1).astype(BF16) for piece in cot], axis=0)
    if paired:
        gathered, corner, g_scaled = together(
            gathered, copies_whole_corner(axes, copied), g_scaled
        )
        weight_in_1 = join_in(axes, place, copies_lists(copied, corner), True)[0]
    else:
        weight_in_1 = in_columns(blocks)[0]
    hops, pieces_1 = gather_corner(axes, gathered)
    proj_1 = [mm(piece, weight_in_1).astype(BF16) for piece in pieces_1]
    hops, proj_1 = together(hops, proj_1)
    last = gather_end(axes, hops)
    pieces_1 = pieces_1 + [last]
    proj_1 = jnp.concatenate(proj_1 + [mm(last, weight_in_1).astype(BF16)], axis=0)
    gated_1, y_1, enter_1, sums = mix_forward(
        place, proj_1, conv[1], head[1], skip[1], g_scaled
    )

    sums = sums + flip(sums, "c")
    if len(axes.links) == 2:
        far, near = axes.links
        sums = sums + flip(sums, far) + flip(sums, near) + flip_both(sums, axes.links)
    else:
        for name in axes.links:
            sums = sums + flip(sums, name)

    def last_rows(begin, end, others):
        return mm(after(gated_1, others)[begin:end], weight_out_1).astype(BF16)

    sums, branch_1 = together(sums, scatter_corner(axes, last_rows, rows))
    branch_1 = scatter_sides(axes, branch_1)
    outs = mix_backward(
        place, proj_1, y_1, g_scaled, sums, enter_1, conv[1], head[1], skip[1], True
    )
    (g_proj, g_conv, g_head, g_skip, scaled_1), branch_1 = together(outs, branch_1)
    got_1 = jnp.concatenate(after(cot, g_proj), axis=0)
    normed = jnp.concatenate(after(pieces_1, g_proj), axis=0)

    def spare_rows(g_conv, g_head, g_skip):
        g_conv = jnp.concatenate(
            [
                lax.dynamic_update_slice_in_dim(
                    jnp.zeros((taps, DI), F32), g_conv[:taps, :wide], me * wide, 1
                ),
                g_conv[:taps, wide:],
            ],
            axis=1,
        )
        g_conv = g_conv.reshape(taps, -1, n_conv).transpose(1, 0, 2)
        g_conv = [
            jnp.pad(g_conv[..., at:end], ((0, 0), (0, 0), (0, room - end + at)))
            for at, end in cuts
        ]
        g_head = jnp.stack(
            [g_head[0, :heads], g_head[1, :heads], jnp.sum(g_skip[0].reshape(heads, HD), 1)]
        )
        g_head = jnp.pad(g_head, ((0, 0), (0, room - heads)))
        sharers = team * copies // team
        owner = jnp.arange(team * copies) // sharers == me
        g_head = jnp.where(owner[:, None, None], g_head, 0.0)
        spare = jnp.concatenate(g_conv + [g_head], axis=1)
        more = -spare.shape[1] % 16 if depth % 16 == 0 else 0
        return jnp.pad(spare, ((0, 0), (0, more), (0, 0))).astype(BF16)

    def in_gradient(normed, g_proj, beside, quick):
        spare = None if beside is None else spare_rows(*beside)
        g_in = mm_tn(normed, g_proj).astype(BF16)
        return cut_in(axes, place, g_in, spare, depth, wide, quick)

    def copies_scatter(values):
        return lax.psum_scatter(jnp.stack(values), axes.copies, scatter_dimension=0)

    def owned(summed):
        return team_swap(summed.reshape(team, -1, depth, wide))

    def weighed_rows(g_proj, weight_in):
        def make(begin, end, others):
            return mm_nt(after(g_proj, others)[begin:end], weight_in).astype(BF16)

        return make

    weighed = together(*scatter_corner(axes, weighed_rows(g_proj, weight_in_1), rows))
    weighed = scatter_sides(axes, weighed)
    g_late = after(g_proj, weighed[0])
    blocks = in_gradient(normed, g_late, (g_conv, g_head, g_skip), False)
    weighed, blocks = together(weighed, blocks)
    summed = copies_scatter(blocks)
    squares = lax.dynamic_slice_in_dim(sums, me * rows, rows, 1)[0][:, None]
    out = (residual_1 + lax.rsqrt(squares / DI + eps) * add_all(branch_1)).astype(BF16)
    if len(weighed) == 1:
        weighed = weighed + (jnp.zeros_like(weighed[0]),) * 2

    grad, sent = turn_back(
        *weighed, residual_1, rho_1, cotangent[0], gate_rho_0, branch_0
    )
    gathered = gather_start(axes, sent)
    g_out = mm_tn(scaled_1, got_1).astype(BF16)
    gathered, g_out = together(gathered, g_out)
    g_out_1 = lax.psum_scatter(g_out, axes.copies, scatter_dimension=0, tiled=True)
    hops, pieces = gather_corner(axes, gathered)
    g_scaled = [mm_nt(piece[:, :model], weight_out_0).astype(BF16) for piece in pieces]
    normed = jnp.concatenate(after(pieces_0, gathered), axis=0)
    hops, g_scaled, normed = together(hops, g_scaled, normed)
    last = gather_end(axes, hops)
    pieces = pieces + [last]
    g_scaled = g_scaled + [mm_nt(last[:, :model], weight_out_0).astype(BF16)]
    g_scaled = jnp.concatenate(g_scaled, axis=0)
    kappa = jnp.concatenate([piece[:, model:] for piece in pieces], axis=0)
    kappa = after(kappa, summed)
    outs = mix_backward(
        place, proj_0, y_0, g_scaled, kappa, enter_0, conv[0], head[0], skip[0], False
    )
    outs, owned_1 = together(outs, owned(summed))
    g_proj, g_conv, g_head, g_skip, g_gate, g_rest = outs
    owned_1 = owned_1[:, :1], owned_1[:, 1:]
    got = jnp.concatenate([piece[:, :model] for piece in after(pieces, g_proj)], axis=0)
    beside = g_conv, g_head, g_skip
    g_out = mm_tn(gated_0, got).astype(BF16)
    if paired:
        gates = in_gradient(normed, g_gate, None, True)
        gates = join_out(axes, place, gates, g_out)
        g_proj = after(g_proj, gates)
    weighed = scatter_corner(axes, weighed_rows(g_proj, weight_in_0), rows)
    if paired:
        weighed, gate_parts = together(weighed, sum_direct(axes, gates))
        weighed = scatter_sides(axes, weighed)
        rests = in_gradient(normed, after(g_rest, gate_parts), beside, True)
        corner = sum_corner(axes, rests)
        weighed, corner = together(weighed, corner)
        gates = add_low(gates[0], *gate_parts)
        g_out_0 = gates[team:].reshape(-1, model // wide, depth, wide)
        g_out_0 = g_out_0.transpose(0, 2, 1, 3).reshape(-1, model)
        gates = owned(gates[:team])
        sides, gates = together(sum_sides(axes, rests, corner), gates)
        rests = owned(add_low(rests[0], *sides))
    else:
        weighed = scatter_sides(axes, weighed)
        gates = owned(copies_scatter(in_gradient(normed, g_gate, None, False)))
        rests = owned(copies_scatter(in_gradient(normed, g_rest, beside, False)))
        g_out_0 = lax.psum_scatter(g_out, axes.copies, scatter_dimension=0, tiled=True)
    owned_0 = gates, rests
    weighed = add_all(weighed)
    mean = jnp.mean(weighed * residual_0, axis=1, keepdims=True)
    grad = grad + rho_0 * weighed - residual_0 * (rho_0 * rho_0 * rho_0 * mean)

    grad_in, grad_norm, spare = finish_in(axes, [owned_0, owned_1], in_weight, norm_gain)
    grad_out = jnp.stack([g_out_0, g_out_1]).astype(F32)
    grad_gate = jnp.sum(grad_out * out_weight.astype(F32), axis=2)
    grad_out = grad_out * gate_gain.astype(F32)[:, :, None]

    conv_grad = [
        spare[:, at * taps : (at + 1) * taps, : end - start] for at, (start, end) in enumerate(cuts)
    ]
    conv_grad = jnp.concatenate(conv_grad, axis=2)
    head_grad = spare[:, len(cuts) * taps : len(cuts) * taps + 3, :heads]
    return (
        out[None],
        grad[None],
        grad_norm,
        grad_in,
        conv_grad[:, :CONV],
        conv_grad[:, CONV],
        head_grad[:, 0],
        head_grad[:, 1],
        head_grad[:, 2],
        grad_gate,
        grad_out,
    )


def solution(mesh):
    axes = Axes(mesh.shape["seq"], mesh.shape["fsdp"])
    fine = Mesh(mesh.devices.reshape((2,) * len(axes.every)), axes.every)
    acts = P(axes.fsdp, axes.seq, None)
    flat = P(None, axes.every)
    rows = P(None, axes.every, None)
    taps = P(None, None, axes.every)
    head = P(None, axes.seq)
    return jax.shard_map(
        functools.partial(local, axes),
        mesh=fine,
        in_specs=(acts, acts, flat, rows, taps, flat, head, head, head, flat, rows),
        out_specs=(acts, acts, flat, rows, taps, flat, head, head, head, flat, rows),
        check_vma=False,
    )
```

```python
import functools

import jax
import jax.numpy as jnp
from jax import lax
from jax.experimental import pallas as pl
from jax.experimental.pallas import tpu as pltpu
from jax.sharding import Mesh
from jax.sharding import PartitionSpec as P

HD = 64
NSTATE = 128
STRETCH = 256
DI = 3072
CONV = 4
LANES = 128
BC = 2 * NSTATE

eps = 1e-05

F32 = jnp.float32
BF16 = jnp.bfloat16
EXACT = lax.Precision.HIGHEST
CAP = 48 * 1024 * 1024


def mm(left, right):
    return jnp.dot(left, right, preferred_element_type=F32)


def mm_nt(left, right):
    return lax.dot_general(left, right, (((1,), (1,)), ((), ())), preferred_element_type=F32)


def mm_tn(left, right):
    return lax.dot_general(left, right, (((0,), (0,)), ((), ())), preferred_element_type=F32)


def mm_exact(left, right):
    return jnp.dot(left, right, precision=EXACT, preferred_element_type=F32)


def mm_low(left, right):
    return mm(left.astype(BF16), right.astype(BF16))


def mm_thirds(ones, right):
    lane = iota(right.shape, 1)
    high = right.astype(BF16).astype(F32)
    left = right - high
    middle = left.astype(BF16).astype(F32)
    low = left - middle
    packed = jnp.where(lane < 64, pltpu.roll(middle, 32, 1), pltpu.roll(low, 64, 1))
    packed = jnp.where(lane < 32, high, jnp.where(lane < 96, packed, 0.0))
    total = mm_low(ones, packed)
    total = total + pltpu.roll(total, 96, 1) + pltpu.roll(total, 64, 1)
    return jnp.where(lane < 32, total, 0.0)


def sum_rows(values, ones):
    high = values.astype(BF16).astype(F32)
    left = values - high
    middle = left.astype(BF16).astype(F32)
    parts = jnp.concatenate([high, middle, left - middle], axis=0)
    total = mm_low(parts, ones)
    return total[0:8] + total[8:16] + total[16:24]


def as_columns(*rows):
    stacked = jnp.concatenate(rows, axis=0)
    rest = jnp.zeros((LANES - stacked.shape[0], stacked.shape[1]), F32)
    return jnp.transpose(jnp.concatenate([stacked, rest], axis=0))


def logistic(values):
    return 0.5 * jnp.tanh(0.5 * values) + 0.5


def iota(shape, dim):
    return lax.broadcasted_iota(jnp.int32, shape, dim)


def head_spread(width, first):
    return (iota((LANES, width), 0) == iota((LANES, width), 1) // HD + first).astype(BF16)


def head_fold(heads, width):
    return iota((heads, width), 0) == iota((heads, width), 1) // HD


def own_steps(raw, turned):
    return pltpu.roll(raw.astype(F32), turned, 1)


def steps_of(raw, head_ref):
    shifted = jnp.transpose(raw)[0:8] + head_ref[:, 0:1]
    return shifted, jnp.maximum(shifted, 0.0) + jnp.log1p(jnp.exp(-jnp.abs(shifted)))


def steps_beside(raw, head_rows):
    shifted = raw + head_rows[0:1]
    step = jnp.maximum(shifted, 0.0) + jnp.log1p(jnp.exp(-jnp.abs(shifted)))
    return shifted, step


def take(ref, core):
    half = ref.shape[0] // 2
    first = ref[pl.ds(pl.multiple_of(core * half, half), half), :]
    second = ref[pl.ds(pl.multiple_of((1 - core) * half, half), half), :]
    return jnp.concatenate([first, second], axis=0)


def put(ref, core, values, start, end):
    half = ref.shape[0] // 2
    ref[pl.ds(pl.multiple_of(core * half, half), half), start:end] = values[:half]
    ref[pl.ds(pl.multiple_of((1 - core) * half, half), half), start:end] = values[half:]


def pairs(width):
    return [(at, min(at + LANES, width)) for at in range(0, width, LANES)]


def mix_forward_kernel(
    place_ref, proj_ref, conv_ref, head_ref, skip_ref, *refs, with_sums
):
    gated_ref, y_ref, enter_ref = refs[with_sums : with_sums + 3]
    state_ref, ext_ref = refs[-2:]
    core, turned = place_ref[0] & 1, place_ref[1]
    rows = proj_ref.shape[0]
    wide = gated_ref.shape[1]
    chans = wide + BC

    @pl.when(pl.program_id(0) == 0)
    def _():
        state_ref[...] = jnp.zeros_like(state_ref)
        ext_ref[0:8, :] = jnp.zeros((8, chans), F32)

    proj = take(proj_ref, core)
    ext_ref[8 : 8 + rows, :] = proj[:, wide : wide + chans].astype(F32)
    pre = conv_ref[CONV : CONV + 1, :] + conv_ref[0:1, :] * ext_ref[5 : 5 + rows, :]
    for lag in range(1, CONV):
        pre = pre + conv_ref[lag : lag + 1, :] * ext_ref[5 + lag : 5 + lag + rows, :]
    ext_ref[0:8, :] = ext_ref[rows : rows + 8, :]
    act = pre * jax.nn.sigmoid(pre)
    x = act[:, :wide]
    b_low = act[:, wide : wide + NSTATE].astype(BF16)
    c_low = act[:, wide + NSTATE :].astype(BF16)

    _, step = steps_beside(own_steps(proj[:, wide + chans :], turned), head_ref)
    decay = -step * head_ref[1:2, :]
    lower = iota((rows, rows), 0) >= iota((rows, rows), 1)
    cum = mm_thirds(lower.astype(F32), decay)
    cum_t = jnp.transpose(cum)
    spread = head_spread(wide, 0)
    total = cum[rows - 1 : rows, :]
    step_wide = mm_low(step, spread)
    grown = mm_low(jnp.exp(cum), spread)
    ending_wide = mm_low(step * jnp.exp(total - cum), spread)
    kept = mm_exact(jnp.broadcast_to(jnp.exp(total), (8, LANES)), spread.astype(F32))[0:1, :]

    scores = mm_nt(c_low, b_low)
    weighted = x * step_wide
    weighted_low = weighted.astype(BF16)
    within = []
    for start, end in pairs(wide):
        both = weighted_low[:, start:end]
        parts = []
        for head in range(start // HD, end // HD):
            gap = cum[:, head : head + 1] - cum_t[head : head + 1, :]
            mixed = jnp.where(lower, jnp.exp(gap), 0.0) * scores
            parts.append(mm(mixed.astype(BF16), both))
        if len(parts) == 2:
            first = iota((rows, end - start), 1) < HD
            within.append(jnp.where(first, parts[0], parts[1]))
        else:
            within.append(parts[0])
    within = jnp.concatenate(within, axis=1)
    state = state_ref[...]
    enter_ref[0] = state
    carried = grown * mm(c_low, state.astype(BF16))
    y = within + carried + skip_ref[0:1, :] * x
    gate = proj[:, :wide].astype(F32)
    gated = (y * (gate * jax.nn.sigmoid(gate))).astype(BF16)
    if not with_sums:
        put(gated_ref, core, gated, 0, wide)
    else:
        gated_ref[...] = gated
        gated = gated.astype(F32)
        ones = jnp.ones((8, wide), BF16)
        product = gated * take(refs[0], core).astype(F32)
        squares = mm_nt(ones, (gated * gated).astype(BF16))
        product = mm_nt(ones, product.astype(BF16))
        refs[4][...] = jnp.where(iota((8, rows), 0) == 0, squares, product)
    put(y_ref, core, y.astype(BF16), 0, wide)
    state_ref[...] = state * kept + mm_tn(b_low, (x * ending_wide).astype(BF16))


def mix_forward(place, proj, conv_rows, head_rows, wide_rows, pulled=None):
    with_sums = pulled is not None
    length, width = proj.shape
    wide = wide_rows.shape[1]
    count = length // STRETCH
    whole = lambda shape: pl.BlockSpec(shape, lambda i, at: (0,) * len(shape))
    part = lambda cols: pl.BlockSpec((STRETCH, cols), lambda i, at: (i ^ (at[0] >> 1), 0))
    plain = pl.BlockSpec((STRETCH, wide), lambda i, at: (i, 0))
    return pl.pallas_call(
        functools.partial(mix_forward_kernel, with_sums=with_sums),
        grid_spec=pltpu.PrefetchScalarGridSpec(
            num_scalar_prefetch=1,
            grid=(count,),
            in_specs=[
                part(width),
                whole(conv_rows.shape),
                whole(head_rows.shape),
                whole(wide_rows.shape),
            ]
            + [part(wide)] * with_sums,
            out_specs=[
                plain if with_sums else part(wide),
                part(wide),
                pl.BlockSpec((1, NSTATE, wide), lambda i, at: (i, 0, 0)),
            ]
            + [pl.BlockSpec((8, STRETCH), lambda i, at: (0, i))] * with_sums,
            scratch_shapes=[
                pltpu.VMEM((NSTATE, wide), F32),
                pltpu.VMEM((STRETCH + 8, wide + BC), F32),
            ],
        ),
        out_shape=[
            jax.ShapeDtypeStruct((length, wide), BF16),
            jax.ShapeDtypeStruct((length, wide), BF16),
            jax.ShapeDtypeStruct((count, NSTATE, wide), F32),
        ]
        + [jax.ShapeDtypeStruct((8, length), F32)] * with_sums,
        compiler_params=pltpu.CompilerParams(
            dimension_semantics=("arbitrary",), vmem_limit_bytes=CAP
        ),
        cost_estimate=pl.CostEstimate(
            flops=length * wide * 18000, bytes_accessed=length * 6000, transcendentals=0
        ),
        name="mix_forward",
    )(place, proj, conv_rows, head_rows, wide_rows, *[pulled] * with_sums)


def mix_backward_kernel(
    place_ref,
    proj_ref,
    before_ref,
    y_ref,
    pulled_ref,
    kappa_ref,
    enter_ref,
    conv_ref,
    head_ref,
    wide_ref,
    *refs,
    as_rows,
):
    out_ref, conv_grad_ref, head_grad_ref, skip_grad_ref = refs[:4]
    dstate_ref, ext_ref, gext_ref, rows_ref = refs[-4:]
    core, turned = place_ref[0] & 1, place_ref[1]
    rows = proj_ref.shape[0]
    wide = y_ref.shape[1]
    chans = wide + BC
    turn = pl.program_id(0)

    @pl.when(turn == 0)
    def _():
        dstate_ref[...] = jnp.zeros_like(dstate_ref)
        gext_ref[rows : rows + 8, :] = jnp.zeros((8, chans), F32)
        conv_grad_ref[...] = jnp.zeros_like(conv_grad_ref)
        head_grad_ref[...] = jnp.zeros_like(head_grad_ref)
        skip_grad_ref[...] = jnp.zeros_like(skip_grad_ref)
        rows_ref[...] = jnp.zeros_like(rows_ref)

    before = before_ref[8:16, wide : wide + chans].astype(F32)
    ext_ref[0:8, :] = jnp.where(turn == pl.num_programs(0) - 1, 0.0, before)
    proj = take(proj_ref, core)
    ext_ref[8 : 8 + rows, :] = proj[:, wide : wide + chans].astype(F32)
    pre = conv_ref[CONV : CONV + 1, :] + conv_ref[0:1, :] * ext_ref[5 : 5 + rows, :]
    for lag in range(1, CONV):
        pre = pre + conv_ref[lag : lag + 1, :] * ext_ref[5 + lag : 5 + lag + rows, :]
    sig = logistic(pre)
    act = pre * sig
    slope = sig * (1.0 + pre * (1.0 - sig))
    x = act[:, :wide]
    x_low = x.astype(BF16)
    b_low = act[:, wide : wide + NSTATE].astype(BF16)
    c_low = act[:, wide + NSTATE :].astype(BF16)

    shifted, step = steps_of(own_steps(proj[:, wide + chans :], turned), head_ref)
    rate = head_ref[:, 1:2]
    decay = -step * rate
    lower = iota((rows, rows), 0) >= iota((rows, rows), 1)
    upper = iota((rows, rows), 0) <= iota((rows, rows), 1)
    cum_t = sum_rows(decay, upper)
    total = cum_t[:, rows - 1 : rows]
    cum = as_columns(cum_t, step, jnp.exp(cum_t), jnp.exp(total - cum_t))
    cum_low = cum.astype(BF16)
    step_wide = mm(cum_low, head_spread(wide, 8))
    grown = mm(cum_low, head_spread(wide, 16))
    to_end = mm(cum_low, head_spread(wide, 24))
    fold = head_fold(8, wide)
    fold_low = head_fold(16, wide).astype(BF16)
    kept = jnp.sum(jnp.where(fold, jnp.exp(total), 0.0), axis=0, keepdims=True)

    gate = proj[:, :wide].astype(F32)
    y = take(y_ref, core).astype(F32)
    gate_sig = logistic(gate)
    gate_act = gate * gate_sig
    gated = y * gate_act
    if as_rows:
        g_gated = take(pulled_ref, core).astype(F32)
        sums = jnp.transpose(kappa_ref[...])
        rho = lax.rsqrt(sums[:, 0:1] / DI + eps)
        kappa = rho * rho * rho * sums[:, 1:2] / DI
        g_gated = rho * g_gated - gated * kappa
        put(refs[4], core, (gated * rho).astype(BF16), 0, wide)
        copies = []
    else:
        copies = [refs[4], refs[5]]
        g_gated = take(pulled_ref, core).astype(F32)
        g_gated = g_gated - gated * take(kappa_ref, core)[:, 0:1].astype(F32)
    dy = g_gated * gate_act
    g_gate = g_gated * y * (gate_sig * (1.0 + gate * (1.0 - gate_sig)))
    put(out_ref, core, g_gate.astype(BF16), 0, wide)
    for copy_ref in copies[:1]:
        put(copy_ref, core, g_gate.astype(BF16), 0, wide)
    dy_low = dy.astype(BF16)
    skip_grad_ref[0:1, :] += jnp.sum(x * dy, axis=0, keepdims=True)

    scores_t = mm_nt(b_low, c_low)
    lane = iota((rows, LANES), 1)
    d_scores = jnp.zeros((rows, rows), F32)
    column = jnp.zeros((rows, LANES), F32)
    inner = []
    for start, end in pairs(wide):
        both_dy = dy_low[:, start:end]
        both_x = x_low[:, start:end]
        side = iota((rows, end - start), 1) // HD
        parts = []
        for head in range(start // HD, end // HD):
            gap = cum_t[head : head + 1, :] - cum[:, head : head + 1]
            fade = jnp.where(upper, jnp.exp(gap), 0.0)
            own = jnp.where(side == head - start // HD, both_x, jnp.zeros_like(both_x))
            faded = fade * mm_nt(own, both_dy)
            stepped = faded * cum[:, 8 + head : 9 + head]
            d_scores = d_scores + stepped
            parts.append(mm((scores_t * fade).astype(BF16), both_dy))
            column = jnp.where(
                lane == head, jnp.sum(scores_t * faded, axis=1, keepdims=True), column
            )
            rows_ref[head : head + 1, :] = jnp.sum(scores_t * stepped, axis=0, keepdims=True)
        if len(parts) == 2:
            inner.append(jnp.where(side == 0, parts[0], parts[1]))
        else:
            inner.append(parts[0])
    inner = jnp.concatenate(inner, axis=1)

    enter = enter_ref[0]
    enter_low = enter.astype(BF16)
    dstate = dstate_ref[...]
    dstate_low = dstate.astype(BF16)
    outer = to_end * mm(b_low, dstate_low)
    g_x = step_wide * (inner + outer) + wide_ref[0:1, :] * dy
    dy_grown = dy * grown
    dy_grown_low = dy_grown.astype(BF16)
    carried_sum = mm_nt(fold_low, (dy_grown * mm(c_low, enter_low)).astype(BF16))[0:8]
    outer_sum = mm_nt(fold_low, (x * outer).astype(BF16))[0:8]
    state_sum = jnp.sum(enter * dstate, axis=0, keepdims=True)
    state_sum = jnp.sum(jnp.where(fold, state_sum, 0.0), axis=1, keepdims=True)
    column = jnp.transpose(column)[0:8]
    step_outer = step * outer_sum
    g_cum = rows_ref[0:8, :] + carried_sum - step * column - step_outer
    g_total = jnp.sum(step_outer, axis=1, keepdims=True) + jnp.exp(total) * state_sum
    g_decay = sum_rows(g_cum, lower) + g_total
    scaled_decay = rate * g_decay
    g_raw = (column + outer_sum - scaled_decay) * jax.nn.sigmoid(shifted)
    head_grad_ref[:, 0:1] += jnp.sum(g_raw, axis=1, keepdims=True)
    head_grad_ref[:, 1:2] -= jnp.sum(step * scaled_decay, axis=1, keepdims=True)
    g_raw = pltpu.roll(as_columns(g_raw), lax.rem(LANES - turned, LANES), 1)
    put(out_ref, core, g_raw.astype(BF16), wide + chans, wide + chans + LANES)
    for copy_ref in copies[1:]:
        put(copy_ref, core, g_raw.astype(BF16), chans, chans + LANES)

    d_low = d_scores.astype(BF16)
    ending = (x * (step_wide * to_end)).astype(BF16)
    g_b = mm(d_low, c_low) + mm_nt(ending, dstate_low)
    g_c = mm_tn(d_low, b_low) + mm_nt(dy_grown_low, enter_low)
    dstate_ref[...] = dstate * kept + mm_tn(c_low, dy_grown_low)

    gext_ref[0:rows, :wide] = g_x * slope[:, :wide]
    gext_ref[0:rows, wide : wide + NSTATE] = g_b * slope[:, wide : wide + NSTATE]
    gext_ref[0:rows, wide + NSTATE :] = g_c * slope[:, wide + NSTATE :]
    g_pre = gext_ref[0:rows, :]
    current = ext_ref[8 : 8 + rows, :]
    g_in = jnp.zeros_like(g_pre)
    for lag in range(CONV):
        moved = gext_ref[3 - lag : 3 - lag + rows, :]
        g_in = g_in + conv_ref[lag : lag + 1, :] * moved
        conv_grad_ref[lag : lag + 1, :] += jnp.sum(current * moved, axis=0, keepdims=True)
    put(out_ref, core, g_in.astype(BF16), wide, wide + chans)
    for copy_ref in copies[1:]:
        put(copy_ref, core, g_in.astype(BF16), 0, chans)
    conv_grad_ref[CONV : CONV + 1, :] += jnp.sum(g_pre, axis=0, keepdims=True)
    gext_ref[rows : rows + 8, :] = gext_ref[0:8, :]


def mix_backward(place, proj, y, pulled, kappa, enter, conv_rows, head_rows, wide_rows, as_rows):
    length, width = proj.shape
    wide = wide_rows.shape[1]
    count = length // STRETCH
    whole = lambda shape: pl.BlockSpec(shape, lambda i, at: (0,) * len(shape))
    part = lambda cols: pl.BlockSpec((STRETCH, cols), lambda i, at: ((count - 1 - i) ^ (at[0] >> 1), 0))
    half = STRETCH // 2

    def last_rows(i, at):
        pair = jnp.maximum(count - 2 - i, 0) ^ (at[0] >> 1)
        block = 2 * pair + 1 - (at[0] & 1)
        return block * (half // 16) + half // 16 - 1, 0

    before = pl.BlockSpec((16, width), last_rows)
    turn = lambda i, at: (count - 1 - i) ^ (at[0] >> 1)
    if as_rows:
        scales = pl.BlockSpec((8, STRETCH), lambda i, at: (0, count - 1 - i))
    else:
        last = kappa.shape[1] // LANES - 1
        scales = pl.BlockSpec((STRETCH, LANES), lambda i, at: (turn(i, at), last))
    return pl.pallas_call(
        functools.partial(mix_backward_kernel, as_rows=as_rows),
        grid_spec=pltpu.PrefetchScalarGridSpec(
            num_scalar_prefetch=1,
            grid=(count,),
            in_specs=[
                part(width),
                before,
                part(wide),
                part(wide),
                scales,
                pl.BlockSpec((1, NSTATE, wide), lambda i, at: (count - 1 - i, 0, 0)),
                whole(conv_rows.shape),
                whole(head_rows.shape),
                whole(wide_rows.shape),
            ],
            out_specs=[
                part(width),
                whole((8, wide + BC)),
                whole((8, LANES)),
                whole((8, wide)),
            ]
            + ([part(wide)] if as_rows else [part(wide), part(width - wide)]),
            scratch_shapes=[
                pltpu.VMEM((NSTATE, wide), F32),
                pltpu.VMEM((STRETCH + 8, wide + BC), F32),
                pltpu.VMEM((STRETCH + 8, wide + BC), F32),
                pltpu.VMEM((8, STRETCH), F32),
            ],
        ),
        out_shape=[
            jax.ShapeDtypeStruct((length, width), BF16),
            jax.ShapeDtypeStruct((8, wide + BC), F32),
            jax.ShapeDtypeStruct((8, LANES), F32),
            jax.ShapeDtypeStruct((8, wide), F32),
        ]
        + [jax.ShapeDtypeStruct((length, wide), BF16)]
        + [jax.ShapeDtypeStruct((length, width - wide), BF16)] * (not as_rows),
        compiler_params=pltpu.CompilerParams(
            dimension_semantics=("arbitrary",), vmem_limit_bytes=CAP
        ),
        cost_estimate=pl.CostEstimate(
            flops=length * wide * 40000, bytes_accessed=length * 9000, transcendentals=0
        ),
        name="mix_backward",
    )(place, proj, proj, y, pulled, kappa, enter, conv_rows, head_rows, wide_rows)


def add_low(*terms):
    total = terms[0].astype(F32)
    for term in terms[1:]:
        total = total + term.astype(F32)
    return total.astype(BF16)


def rms(values):
    return lax.rsqrt(jnp.mean(values * values, axis=-1, keepdims=True) + eps)


def after(values, *others):
    return lax.optimization_barrier((values, others))[0]


def flip(values, axis):
    return lax.ppermute(values, axis, [(0, 1), (1, 0)])


def flip_both(values, names):
    return lax.ppermute(values, names, [(0, 3), (1, 2), (2, 1), (3, 0)])


def turn_back(own, near, far, residual, rho, grad, gate_rho, branch):
    rows, model = own.shape

    def kernel(own_ref, near_ref, far_ref, res_ref, rho_ref, grad_ref, gate_ref, br_ref, *refs):
        grad_out, sent_out = refs
        weighed = own_ref[...].astype(F32) + near_ref[...].astype(F32) + far_ref[...].astype(F32)
        res, rho, gate = res_ref[...], rho_ref[...], gate_ref[...]
        mean = jnp.sum(weighed * res, axis=1, keepdims=True) / model
        total = grad_ref[...].astype(F32) + rho * weighed - res * (rho * rho * rho * mean)
        grad_out[...] = total
        pulled = total * gate
        kappa = gate * gate * jnp.sum(pulled * br_ref[...], axis=1, keepdims=True) / DI
        sent_out[:, :model] = pulled.astype(BF16)
        sent_out[:, model:] = jnp.broadcast_to(kappa, (rows, LANES)).astype(BF16)

    return pl.pallas_call(
        kernel,
        in_specs=all_vmem(8),
        out_specs=all_vmem(2),
        out_shape=[
            jax.ShapeDtypeStruct((rows, model), F32),
            jax.ShapeDtypeStruct((rows, model + LANES), BF16),
        ],
        compiler_params=pltpu.CompilerParams(vmem_limit_bytes=CAP),
        name="turn_back",
    )(own, near, far, residual, rho, grad, gate_rho, branch)


class Axes:
    def __init__(self, seq, fsdp):
        between = tuple(f"b{i}" for i in range((seq // 4).bit_length() - 1))
        before = tuple(f"p{i}" for i in range((fsdp // 2).bit_length() - 1))
        self.seq = ("a",) + between + ("c",)
        self.fsdp = before + ("q",)
        self.every = self.seq + self.fsdp
        self.links = ("a",) + between
        self.team = self.seq
        self.copies = self.fsdp

    def bits(self, names, at):
        value = 0
        for spot, name in enumerate(names):
            if at >> (len(names) - 1 - spot) & 1:
                value |= 1 << (len(self.every) - 1 - self.every.index(name))
        return value

    def at(self, me, r, k, relative):
        if relative:
            me = me ^ self.bits(self.copies, r)
        else:
            me = me & ~self.bits(self.copies, -1) | self.bits(self.copies, r)
        return me & ~self.bits(self.team, -1) | self.bits(self.team, k)


def all_vmem(count):
    return [pl.BlockSpec(memory_space=pltpu.VMEM)] * count


SMEM = pl.BlockSpec(memory_space=pltpu.SMEM)


def split_in(axes, weights, gain, spare, layer):
    team = 2 ** len(axes.team)
    depth, columns = weights.shape[1:]
    wide = DI // team
    parts = 2 + 3 * LANES // wide

    def kernel(weight_ref, gain_ref, spare_ref, out_ref):
        scale = gain_ref[...].astype(F32)
        tail = (weight_ref[0, :, 2 * DI :].astype(F32) * scale).astype(BF16)
        tail = jnp.concatenate([tail, spare_ref[...]], axis=1)
        for k in range(team):
            for part in range(2):
                base = (1 - part) * DI + k * wide
                cut = weight_ref[0, :, base : base + wide].astype(F32)
                out_ref[k, part] = (cut * scale).astype(BF16)
            for part in range(2, parts):
                out_ref[k, part] = tail[:, (part - 2) * wide : (part - 1) * wide]

    whole = lambda shape: pl.BlockSpec(shape, lambda i: (0,) * len(shape))
    return pl.pallas_call(
        kernel,
        grid=(1,),
        in_specs=[
            pl.BlockSpec((1, depth, columns), lambda i: (layer, 0, 0)),
            whole((depth, 1)),
            whole(spare.shape),
        ],
        out_specs=whole((team, parts, depth, wide)),
        out_shape=jax.ShapeDtypeStruct((team, parts, depth, wide), BF16),
        compiler_params=pltpu.CompilerParams(vmem_limit_bytes=CAP),
        name="split_in",
    )(weights, gain[:, None], spare)


def columns_of(part, wide):
    return (1 - part if part < 2 else part) * wide


def join_in(axes, place, lists, relative):
    copies, team = len(lists), 2 ** len(axes.team)
    parts = len(lists[0]) // team
    depth, wide = lists[0][0][0].shape[-2:]
    rows = copies * team * depth
    extra = min(depth, 32)
    if depth % 16:
        flat = jnp.stack([jnp.stack([array[index] for array, index in row]) for row in lists])
        flat = flat.reshape(copies * team, parts, depth, wide)
        flat = jnp.concatenate(
            [flat[:, 1], flat[:, 0]] + [flat[:, part] for part in range(2, parts)], axis=-1
        )
        at = [axes.at(place[2], r, k, relative) for r in range(copies) for k in range(team)]
        flat = jnp.zeros_like(flat).at[jnp.stack(at)].set(flat)
        return flat.reshape(rows, -1), flat[:, :extra, -LANES:]

    arrays = []
    for row in lists:
        for array, _ in row:
            if not any(array is known for known in arrays):
                arrays.append(array)
    which = lambda array: next(i for i, known in enumerate(arrays) if known is array)

    def kernel(place_ref, *refs):
        out_ref, spare_ref = refs[-2:]
        for r in range(copies):
            for k in range(team):
                spot = axes.at(place_ref[2], r, k, relative)
                at = pl.ds(pl.multiple_of(spot * depth, 16), depth)
                for part in range(parts):
                    array, index = lists[r][parts * k + part]
                    base = columns_of(part, wide)
                    out_ref[at, base : base + wide] = refs[which(array)][index]
                index = index if isinstance(index, tuple) else (index,)
                index += (slice(0, extra), slice(wide - LANES, wide))
                spare_ref[spot] = refs[which(array)][index]

    return pl.pallas_call(
        kernel,
        in_specs=[SMEM] + all_vmem(len(arrays)),
        out_specs=all_vmem(2),
        out_shape=[
            jax.ShapeDtypeStruct((rows, parts * wide), BF16),
            jax.ShapeDtypeStruct((copies * team, extra, LANES), BF16),
        ],
        compiler_params=pltpu.CompilerParams(vmem_limit_bytes=CAP),
        name="join_in",
    )(place, *arrays)


def cut_in(axes, place, grad, spare, depth, wide, relative):
    copies, team = 2 ** len(axes.copies), 2 ** len(axes.team)
    parts = grad.shape[1] // wide
    pairs_at = [(r, k) for r in range(copies) for k in range(team)]
    if spare is not None:
        extra, room = spare.shape[1:]
    if depth % 16:
        flat = grad.reshape(copies * team, depth, -1)
        if spare is not None:
            flat = flat.at[:, :extra, -room:].set(spare)
        at = jnp.stack([axes.at(place[2], r, k, relative) for r, k in pairs_at])
        flat = jnp.take(flat, at, axis=0).reshape(copies, team, depth, parts, wide)
        flat = flat.transpose(0, 1, 3, 2, 4).reshape(copies, team * parts, depth, wide)
        return [flat[r] for r in range(copies)]

    def kernel(place_ref, grad_ref, *refs):
        out_refs = refs[-copies:]
        for r, k in pairs_at:
            spot = axes.at(place_ref[2], r, k, relative)
            rows = pl.ds(pl.multiple_of(spot * depth, 16), depth)
            for part in range(parts):
                out_refs[r][parts * k + part] = grad_ref[rows, part * wide : (part + 1) * wide]
            if spare is not None:
                out_refs[r][parts * k + parts - 1, 0:extra, wide - room :] = refs[0][spot]

    given = [] if spare is None else [spare]
    return pl.pallas_call(
        kernel,
        in_specs=[SMEM] + all_vmem(1 + len(given)),
        out_specs=all_vmem(copies),
        out_shape=[jax.ShapeDtypeStruct((team * parts, depth, wide), BF16)] * copies,
        compiler_params=pltpu.CompilerParams(vmem_limit_bytes=CAP),
        name="cut_in",
    )(place, grad, *given)


def join_out(axes, place, blocks, grad):
    copies = len(blocks)
    count, depth, wide = blocks[0].shape
    each, model = grad.shape[0] // copies, grad.shape[1]
    more = (each // depth) * (model // wide)

    def kernel(place_ref, grad_ref, *refs):
        block_refs, out_refs = refs[:copies], refs[copies:]
        for r in range(copies):
            out_refs[r][0:count] = block_refs[r][...]
            copy = (place_ref[2] & axes.bits(axes.copies, -1)) ^ axes.bits(axes.copies, r)
            for at in range(more):
                row, column = at // (model // wide), at % (model // wide)
                first = copy * each + row * depth
                out_refs[r][count + at] = grad_ref[
                    pl.ds(pl.multiple_of(first, 16), depth), column * wide : (column + 1) * wide
                ]

    return pl.pallas_call(
        kernel,
        in_specs=[SMEM] + all_vmem(1 + copies),
        out_specs=all_vmem(copies),
        out_shape=[jax.ShapeDtypeStruct((count + more, depth, wide), BF16)] * copies,
        compiler_params=pltpu.CompilerParams(vmem_limit_bytes=CAP),
        name="join_out",
    )(place, grad, *blocks)


def finish_in(axes, grads, weight, gain):
    layers, depth, columns = weight.shape
    team = 2 ** len(axes.team)
    wide = DI // team
    parts = grads[0][1].shape[1]
    room = (parts - 1) * wide - (columns - 2 * DI)

    def kernel(weight_ref, gain_ref, *refs):
        grad_ref, sum_ref, spare_ref = refs[-3:]
        for layer in range(layers):
            gate_ref, rest_ref = refs[2 * layer : 2 * layer + 2]
            scale = gain_ref[layer].astype(F32)
            tails = []
            for part in range(1, parts):
                tail = rest_ref[0, part].astype(F32)
                for k in range(1, team):
                    tail = tail + rest_ref[k, part].astype(F32)
                tails.append(tail)
            tail = jnp.concatenate(tails, axis=1)
            spare_ref[layer] = tail[:, columns - 2 * DI :]
            tail = tail[:, : columns - 2 * DI]
            grad_ref[layer, :, 2 * DI :] = tail * scale
            total = jnp.sum(tail * weight_ref[layer, :, 2 * DI :].astype(F32), 1, keepdims=True)
            for k in range(team):
                for base, values in ((0, gate_ref[k, 0]), (DI, rest_ref[k, 0])):
                    values = values.astype(F32)
                    spot = slice(base + k * wide, base + (k + 1) * wide)
                    grad_ref[layer, :, spot] = values * scale
                    total = total + jnp.sum(
                        values * weight_ref[layer, :, spot].astype(F32), 1, keepdims=True
                    )
            sum_ref[layer] = jnp.broadcast_to(total, (depth, LANES))

    grads, sums, spares = pl.pallas_call(
        kernel,
        in_specs=all_vmem(2 + 2 * layers),
        out_specs=all_vmem(3),
        out_shape=[
            jax.ShapeDtypeStruct((layers, depth, columns), F32),
            jax.ShapeDtypeStruct((layers, depth, LANES), F32),
            jax.ShapeDtypeStruct((layers, depth, room), F32),
        ],
        compiler_params=pltpu.CompilerParams(vmem_limit_bytes=CAP),
        name="finish_in",
    )(weight, gain[..., None], *[part for pair in grads for part in pair])
    return grads, sums[:, :, 0], spares


def together(*values):
    return lax.optimization_barrier(values)


def copies_start(axes, whole):
    slow, fast = axes.copies
    return whole, flip(whole, fast), flip(whole, slow)


def copies_corner(axes, parts):
    slow, fast = axes.copies
    whole, one, two = parts
    half = whole.shape[0] // 2
    return flip(one[:half], slow), flip(two[half:], fast)


def copies_whole_corner(axes, parts):
    return (flip(parts[1], axes.copies[0]),)


def copies_lists(parts, corner):
    count = parts[0].shape[0]
    each = count // len(corner)
    lists = [[(array, at) for at in range(count)] for array in parts]
    return lists + [[(corner[at // each], at % each) for at in range(count)]]


def sum_corner(axes, pieces):
    slow, fast = axes.copies
    half = pieces[3].shape[0] // 2
    return flip(pieces[3][:half], slow), flip(pieces[3][half:], fast)


def sum_sides(axes, pieces, corner):
    slow, fast = axes.copies
    half = pieces[0].shape[0] // 2
    to_fast = jnp.concatenate([add_low(pieces[1][:half], corner[0]), pieces[1][half:]], axis=0)
    to_slow = jnp.concatenate([pieces[2][:half], add_low(pieces[2][half:], corner[1])], axis=0)
    return flip(to_fast, fast), flip(to_slow, slow)


def sum_direct(axes, pieces):
    slow, fast = axes.copies
    return flip(pieces[1], fast), flip(pieces[2], slow), flip_both(pieces[3], axes.copies)


def gather_start(axes, rows):
    if len(axes.links) != 2:
        return (rows,)
    far, near = axes.links
    return rows, flip(rows, "c"), flip(rows, far), flip(rows, near)


def gather_corner(axes, parts):
    if len(axes.links) != 2:
        return parts, []
    rows, other, from_far, from_near = parts
    most = [rows, other, from_near, flip(from_near, "c"), from_far, flip(from_far, "c")]
    return (flip(from_far, axes.links[1]),), [jnp.concatenate(most, axis=0)]


def gather_end(axes, corner):
    if len(axes.links) != 2:
        whole = corner[0][None]
        for name in reversed(axes.links):
            whole = jnp.concatenate([whole, flip(whole, name)], axis=0)
        whole = jnp.stack([whole, flip(whole, "c")], axis=1)
        return whole.reshape(-1, corner[0].shape[1])
    return jnp.concatenate([corner[0], flip(corner[0], "c")], axis=0)


def core_sum(values, rows):
    both = values.reshape(-1, 2, rows, values.shape[-1])
    return add_low(both[:, 0], flip(both[:, 1], "c"))


def scatter_corner(axes, rows_of, rows):
    team = 2 ** len(axes.team)
    if len(axes.links) != 2:
        return (core_sum(rows_of(0, team * rows, ()), rows),)
    corner = core_sum(rows_of(6 * rows, 8 * rows, ()), rows)[0]
    hop = flip(corner, axes.links[1])
    sides = core_sum(rows_of(2 * rows, 6 * rows, corner), rows)
    return hop, sides, core_sum(rows_of(0, 2 * rows, corner), rows)[0]


def scatter_sides(axes, parts):
    if len(axes.links) != 2:
        whole = parts[0]
        for name in axes.links:
            half = whole.shape[0] // 2
            whole = add_low(whole[:half], flip(whole[half:], name))
        return (whole[0],)
    far, near = axes.links
    hop, sides, own = parts
    return own, flip(sides[0], near), flip(add_low(sides[1], hop), far)


def add_all(parts):
    total = parts[0].astype(F32)
    for part in parts[1:]:
        total = total + part.astype(F32)
    return total


def local(
    axes,
    tokens,
    cotangent,
    norm_gain,
    in_weight,
    conv_kernel,
    conv_shift,
    dt_bias,
    a_log,
    skip_gain,
    gate_gain,
    out_weight,
):
    layers, depth, columns = in_weight.shape
    rows = tokens.shape[1]
    model = tokens.shape[2]
    heads = dt_bias.shape[1]
    wide = heads * HD
    team = 2 ** len(axes.team)
    copies = 2 ** len(axes.copies)
    me = lax.axis_index(axes.team)
    all_at = lax.axis_index(axes.every)
    place = jnp.stack([me, lax.rem(LANES - me * heads, LANES), all_at]).astype(jnp.int32)

    n_conv = conv_shift.shape[1]
    room = 3 * LANES - (columns - 2 * DI)
    cuts = [(at, min(at + room, n_conv)) for at in range(0, n_conv, room)]
    taps = CONV + 1
    conv = jnp.concatenate([conv_kernel, conv_shift[:, None]], axis=1).reshape(-1, n_conv)
    conv = [jnp.pad(conv[:, at:end], ((0, 0), (0, room - end + at))) for at, end in cuts]
    conv = jnp.concatenate(conv, axis=0)
    spare = jnp.pad(conv, ((0, depth - conv.shape[0]), (0, 0)))

    def team_swap(blocks):
        return lax.all_to_all(blocks, axes.team, split_axis=0, concat_axis=0)

    def in_blocks(layer, start):
        blocks = split_in(axes, in_weight, after(norm_gain[layer], start), spare, layer)
        return team_swap(blocks).reshape(-1, depth, wide)

    def in_columns(blocks):
        got = lax.all_gather(blocks, axes.copies)
        lists = [[(got, (r, k)) for k in range(blocks.shape[0])] for r in range(copies)]
        return join_in(axes, place, lists, False)

    def out_rows(layer, start):
        gain = after(gate_gain[layer], start)
        mine = out_weight[layer].astype(F32) * gain.astype(F32)[:, None]
        return lax.all_gather(mine.astype(BF16), axes.copies, axis=0, tiled=True)

    paired = len(axes.copies) == 2
    assert layers == 2

    weight_out_0 = out_rows(0, tokens)
    blocks = in_blocks(0, tokens)
    parts = blocks.shape[0] // team
    residual_0 = tokens[0].astype(F32)
    rho_0 = rms(residual_0)
    blocks, sent = together(blocks, (residual_0 * rho_0).astype(BF16))
    gathered = gather_start(axes, sent)
    if paired:
        copied, gathered = together(copies_start(axes, blocks), gathered)
    hops, pieces_0 = gather_corner(axes, gathered)
    cot = gather_start(axes, after(cotangent[0], gathered))
    if paired:
        corner = copies_corner(axes, copied)
        corner, hops, weight_out_0 = together(corner, hops, weight_out_0)
        weight_in_0, beside = join_in(axes, place, copies_lists(copied, corner), True)
    else:
        weight_in_0, beside = in_columns(blocks)
    last = gather_end(axes, hops)
    last, cot = together(last, cot)
    pieces_0 = pieces_0 + [last]
    proj_0 = [mm(piece, weight_in_0).astype(BF16) for piece in pieces_0]
    proj_0 = jnp.concatenate(proj_0, axis=0)

    conv = beside[:, : conv.shape[0], LANES - room :]
    conv = conv.reshape(-1, len(cuts), layers * taps, room).transpose(0, 2, 1, 3)
    conv = conv.reshape(-1, layers * taps, len(cuts) * room)[:, :, :n_conv]
    conv = conv.reshape(-1, layers, taps, n_conv)
    conv = conv.transpose(1, 2, 0, 3).reshape(layers, CONV + 1, -1).astype(F32)
    conv = jnp.pad(conv, ((0, 0), (0, 7 - CONV), (0, 0)))
    conv = jnp.concatenate(
        [lax.dynamic_slice_in_dim(conv, me * wide, wide, 2), conv[:, :, DI:]], axis=2
    )
    head = jnp.stack([dt_bias, a_log, skip_gain], axis=1)
    skip = jnp.pad(jnp.repeat(head[:, 2:], HD, axis=2), ((0, 0), (0, 7), (0, 0)))
    head = jnp.stack([head[:, 0], jnp.exp(head[:, 1])], axis=1)
    head_rows = jnp.pad(head, ((0, 0), (0, 6), (0, LANES - heads)))
    head = jnp.pad(head.transpose(0, 2, 1), ((0, 0), (0, 8 - heads), (0, LANES - 2)))

    blocks = in_blocks(1, last)
    gated_0, y_0, enter_0 = mix_forward(place, proj_0, conv[0], head_rows[0], skip[0])
    cot_hops, cot = gather_corner(axes, cot)
    (gated_0, y_0, enter_0), blocks, cot_hops = together((gated_0, y_0, enter_0), blocks, cot_hops)
    cot = cot + [gather_end(axes, cot_hops)]
    weight_out_1 = out_rows(1, gated_0)

    def branch_rows(begin, end, others):
        cut = after(gated_0, others)[begin:end]
        squares = jnp.sum(jnp.square(cut.astype(F32)), axis=1, keepdims=True)
        squares = jnp.broadcast_to(squares, (end - begin, LANES))
        return jnp.concatenate([mm(cut, weight_out_0), squares], axis=1).astype(BF16)

    got = together(*scatter_corner(axes, branch_rows, rows))
    got = scatter_sides(axes, got)
    if paired:
        got, copied = together(got, copies_start(axes, blocks))
    got = add_all(got)
    branch_0 = got[:, :model]
    gate_rho_0 = lax.rsqrt(got[:, model : model + 1] / DI + eps)

    residual_1 = residual_0 + gate_rho_0 * branch_0
    rho_1 = rms(residual_1)
    gathered = gather_start(axes, (residual_1 * rho_1).astype(BF16))
    g_scaled = jnp.concatenate([mm_nt(piece, weight_out_1).astype(BF16) for piece in cot], axis=0)
    if paired:
        gathered, corner, g_scaled = together(
            gathered, copies_whole_corner(axes, copied), g_scaled
        )
        weight_in_1 = join_in(axes, place, copies_lists(copied, corner), True)[0]
    else:
        weight_in_1 = in_columns(blocks)[0]
    hops, pieces_1 = gather_corner(axes, gathered)
    proj_1 = [mm(piece, weight_in_1).astype(BF16) for piece in pieces_1]
    hops, proj_1 = together(hops, proj_1)
    last = gather_end(axes, hops)
    pieces_1 = pieces_1 + [last]
    proj_1 = jnp.concatenate(proj_1 + [mm(last, weight_in_1).astype(BF16)], axis=0)
    gated_1, y_1, enter_1, sums = mix_forward(
        place, proj_1, conv[1], head_rows[1], skip[1], g_scaled
    )

    sums = sums + flip(sums, "c")
    if len(axes.links) == 2:
        far, near = axes.links
        sums = sums + flip(sums, far) + flip(sums, near) + flip_both(sums, axes.links)
    else:
        for name in axes.links:
            sums = sums + flip(sums, name)

    branch_1 = mm(gated_1, weight_out_1).astype(BF16)
    sums, branch_1 = together(sums, branch_1)
    branch_1 = lax.psum_scatter(branch_1, axes.team, scatter_dimension=0, tiled=True)
    outs = mix_backward(
        place, proj_1, y_1, g_scaled, sums, enter_1, conv[1], head[1], skip[1], True
    )
    g_proj, g_conv, g_head, g_skip, scaled_1 = outs
    got_1 = jnp.concatenate(after(cot, g_proj), axis=0)
    normed = jnp.concatenate(after(pieces_1, g_proj), axis=0)

    def spare_rows(g_conv, g_head, g_skip):
        g_conv = jnp.concatenate(
            [
                lax.dynamic_update_slice_in_dim(
                    jnp.zeros((taps, DI), F32), g_conv[:taps, :wide], me * wide, 1
                ),
                g_conv[:taps, wide:],
            ],
            axis=1,
        )
        g_conv = g_conv.reshape(taps, -1, n_conv).transpose(1, 0, 2)
        g_conv = [
            jnp.pad(g_conv[..., at:end], ((0, 0), (0, 0), (0, room - end + at)))
            for at, end in cuts
        ]
        g_head = jnp.stack(
            [g_head[:heads, 0], g_head[:heads, 1], jnp.sum(g_skip[0].reshape(heads, HD), 1)]
        )
        g_head = jnp.pad(g_head, ((0, 0), (0, room - heads)))
        sharers = team * copies // team
        owner = jnp.arange(team * copies) // sharers == me
        g_head = jnp.where(owner[:, None, None], g_head, 0.0)
        spare = jnp.concatenate(g_conv + [g_head], axis=1)
        more = -spare.shape[1] % 16 if depth % 16 == 0 else 0
        return jnp.pad(spare, ((0, 0), (0, more), (0, 0))).astype(BF16)

    def in_gradient(normed, g_proj, beside, quick):
        spare = None if beside is None else spare_rows(*beside)
        g_in = mm_tn(normed, g_proj).astype(BF16)
        return cut_in(axes, place, g_in, spare, depth, wide, quick)

    def copies_scatter(values):
        return lax.psum_scatter(jnp.stack(values), axes.copies, scatter_dimension=0)

    def owned(summed):
        return team_swap(summed.reshape(team, -1, depth, wide))

    def weighed_rows(g_proj, weight_in):
        def make(begin, end, others):
            return mm_nt(after(g_proj, others)[begin:end], weight_in).astype(BF16)

        return make

    weighed = scatter_corner(axes, weighed_rows(g_proj, weight_in_1), rows)
    weighed, branch_1 = together(weighed, branch_1)
    weighed = scatter_sides(axes, weighed)
    g_late = after(g_proj, weighed[0])
    blocks = in_gradient(normed, g_late, (g_conv, g_head, g_skip), False)
    weighed, blocks = together(weighed, blocks)
    summed = copies_scatter(blocks)
    squares = lax.dynamic_slice_in_dim(sums, me * rows, rows, 1)[0][:, None]
    out = (residual_1 + lax.rsqrt(squares / DI + eps) * branch_1.astype(F32)).astype(BF16)
    if len(weighed) == 1:
        weighed = weighed + (jnp.zeros_like(weighed[0]),) * 2

    grad, sent = turn_back(
        *weighed, residual_1, rho_1, cotangent[0], gate_rho_0, branch_0
    )
    gathered = gather_start(axes, sent)
    g_out = mm_tn(scaled_1, got_1).astype(BF16)
    gathered, g_out = together(gathered, g_out)
    g_out_1 = lax.psum_scatter(g_out, axes.copies, scatter_dimension=0, tiled=True)
    hops, pieces = gather_corner(axes, gathered)
    g_scaled = [mm_nt(piece[:, :model], weight_out_0).astype(BF16) for piece in pieces]
    normed = jnp.concatenate(after(pieces_0, gathered), axis=0)
    hops, g_scaled, normed = together(hops, g_scaled, normed)
    last = gather_end(axes, hops)
    pieces = pieces + [last]
    g_scaled = g_scaled + [mm_nt(last[:, :model], weight_out_0).astype(BF16)]
    g_scaled = jnp.concatenate(g_scaled, axis=0)
    kappa = jnp.concatenate([piece[:, model:] for piece in pieces], axis=0)
    kappa = after(kappa, summed)
    outs = mix_backward(
        place, proj_0, y_0, g_scaled, kappa, enter_0, conv[0], head[0], skip[0], False
    )
    outs, owned_1 = together(outs, owned(summed))
    g_proj, g_conv, g_head, g_skip, g_gate, g_rest = outs
    owned_1 = owned_1[:, :1], owned_1[:, 1:]
    got = jnp.concatenate([piece[:, :model] for piece in after(pieces, g_proj)], axis=0)
    beside = g_conv, g_head, g_skip
    g_out = mm_tn(gated_0, got).astype(BF16)
    if paired:
        gates = in_gradient(normed, g_gate, None, True)
        gates = join_out(axes, place, gates, g_out)
        g_proj = after(g_proj, gates)
    weighed = scatter_corner(axes, weighed_rows(g_proj, weight_in_0), rows)
    if paired:
        weighed, gate_parts = together(weighed, sum_direct(axes, gates))
        weighed = scatter_sides(axes, weighed)
        rests = in_gradient(normed, after(g_rest, gate_parts), beside, True)
        corner = sum_corner(axes, rests)
        weighed, corner = together(weighed, corner)
        gates = add_low(gates[0], *gate_parts)
        g_out_0 = gates[team:].reshape(-1, model // wide, depth, wide)
        g_out_0 = g_out_0.transpose(0, 2, 1, 3).reshape(-1, model)
        gates = owned(gates[:team])
        sides, gates = together(sum_sides(axes, rests, corner), gates)
        rests = owned(add_low(rests[0], *sides))
    else:
        weighed = scatter_sides(axes, weighed)
        gates = owned(copies_scatter(in_gradient(normed, g_gate, None, False)))
        rests = owned(copies_scatter(in_gradient(normed, g_rest, beside, False)))
        g_out_0 = lax.psum_scatter(g_out, axes.copies, scatter_dimension=0, tiled=True)
    owned_0 = gates, rests
    weighed = add_all(weighed)
    mean = jnp.mean(weighed * residual_0, axis=1, keepdims=True)
    grad = grad + rho_0 * weighed - residual_0 * (rho_0 * rho_0 * rho_0 * mean)

    grad_in, grad_norm, spare = finish_in(axes, [owned_0, owned_1], in_weight, norm_gain)
    grad_out = jnp.stack([g_out_0, g_out_1]).astype(F32)
    grad_gate = jnp.sum(grad_out * out_weight.astype(F32), axis=2)
    grad_out = grad_out * gate_gain.astype(F32)[:, :, None]

    conv_grad = [
        spare[:, at * taps : (at + 1) * taps, : end - start] for at, (start, end) in enumerate(cuts)
    ]
    conv_grad = jnp.concatenate(conv_grad, axis=2)
    head_grad = spare[:, len(cuts) * taps : len(cuts) * taps + 3, :heads]
    return (
        out[None],
        grad[None],
        grad_norm,
        grad_in,
        conv_grad[:, :CONV],
        conv_grad[:, CONV],
        head_grad[:, 0],
        head_grad[:, 1],
        head_grad[:, 2],
        grad_gate,
        grad_out,
    )


def solution(mesh):
    axes = Axes(mesh.shape["seq"], mesh.shape["fsdp"])
    fine = Mesh(mesh.devices.reshape((2,) * len(axes.every)), axes.every)
    acts = P(axes.fsdp, axes.seq, None)
    flat = P(None, axes.every)
    rows = P(None, axes.every, None)
    taps = P(None, None, axes.every)
    head = P(None, axes.seq)
    return jax.shard_map(
        functools.partial(local, axes),
        mesh=fine,
        in_specs=(acts, acts, flat, rows, taps, flat, head, head, head, flat, rows),
        out_specs=(acts, acts, flat, rows, taps, flat, head, head, head, flat, rows),
        check_vma=False,
    )
```

```python
import functools

import jax
import jax.numpy as jnp
from jax import lax
from jax.experimental import pallas as pl
from jax.experimental.pallas import tpu as pltpu
from jax.sharding import Mesh
from jax.sharding import PartitionSpec as P

HD = 64
NSTATE = 128
STRETCH = 256
DI = 3072
CONV = 4
LANES = 128
BC = 2 * NSTATE

eps = 1e-05

F32 = jnp.float32
BF16 = jnp.bfloat16
EXACT = lax.Precision.HIGHEST
CAP = 48 * 1024 * 1024


def mm(left, right):
    return jnp.dot(left, right, preferred_element_type=F32)


def mm_nt(left, right):
    return lax.dot_general(left, right, (((1,), (1,)), ((), ())), preferred_element_type=F32)


def mm_tn(left, right):
    return lax.dot_general(left, right, (((0,), (0,)), ((), ())), preferred_element_type=F32)


def mm_exact(left, right):
    return jnp.dot(left, right, precision=EXACT, preferred_element_type=F32)


def mm_low(left, right):
    return mm(left.astype(BF16), right.astype(BF16))


def mm_thirds(ones, right):
    lane = iota(right.shape, 1)
    high = right.astype(BF16).astype(F32)
    left = right - high
    middle = left.astype(BF16).astype(F32)
    low = left - middle
    packed = jnp.where(lane < 64, pltpu.roll(middle, 32, 1), pltpu.roll(low, 64, 1))
    packed = jnp.where(lane < 32, high, jnp.where(lane < 96, packed, 0.0))
    total = mm_low(ones, packed)
    total = total + pltpu.roll(total, 96, 1) + pltpu.roll(total, 64, 1)
    return jnp.where(lane < 32, total, 0.0)


def sum_rows(values, ones):
    high = values.astype(BF16).astype(F32)
    left = values - high
    middle = left.astype(BF16).astype(F32)
    parts = jnp.concatenate([high, middle, left - middle], axis=0)
    total = mm_low(parts, ones)
    return total[0:8] + total[8:16] + total[16:24]


def as_columns(*rows):
    stacked = jnp.concatenate(rows, axis=0)
    rest = jnp.zeros((LANES - stacked.shape[0], stacked.shape[1]), F32)
    return jnp.transpose(jnp.concatenate([stacked, rest], axis=0))


def logistic(values):
    return 0.5 * jnp.tanh(0.5 * values) + 0.5


def iota(shape, dim):
    return lax.broadcasted_iota(jnp.int32, shape, dim)


def head_spread(width, first):
    return (iota((LANES, width), 0) == iota((LANES, width), 1) // HD + first).astype(BF16)


def head_fold(heads, width):
    return iota((heads, width), 0) == iota((heads, width), 1) // HD


def own_steps(raw, turned):
    return pltpu.roll(raw.astype(F32), turned, 1)


def steps_of(raw, head_ref):
    shifted = jnp.transpose(raw)[0:8] + head_ref[:, 0:1]
    return shifted, jnp.maximum(shifted, 0.0) + jnp.log1p(jnp.exp(-jnp.abs(shifted)))


def steps_beside(raw, head_rows):
    shifted = raw + head_rows[0:1]
    step = jnp.maximum(shifted, 0.0) + jnp.log1p(jnp.exp(-jnp.abs(shifted)))
    return shifted, step


def take(ref, core):
    half = ref.shape[0] // 2
    first = ref[pl.ds(pl.multiple_of(core * half, half), half), :]
    second = ref[pl.ds(pl.multiple_of((1 - core) * half, half), half), :]
    return jnp.concatenate([first, second], axis=0)


def put(ref, core, values, start, end):
    half = ref.shape[0] // 2
    ref[pl.ds(pl.multiple_of(core * half, half), half), start:end] = values[:half]
    ref[pl.ds(pl.multiple_of((1 - core) * half, half), half), start:end] = values[half:]


def pairs(width):
    return [(at, min(at + LANES, width)) for at in range(0, width, LANES)]


def mix_forward_kernel(
    place_ref, proj_ref, conv_ref, head_ref, skip_ref, *refs, with_sums
):
    gated_ref, y_ref, enter_ref = refs[with_sums : with_sums + 3]
    state_ref, ext_ref = refs[-2:]
    core, turned = place_ref[0] & 1, place_ref[1]
    rows = proj_ref.shape[0]
    wide = gated_ref.shape[1]
    chans = wide + BC

    @pl.when(pl.program_id(0) == 0)
    def _():
        state_ref[...] = jnp.zeros_like(state_ref)
        ext_ref[0:8, :] = jnp.zeros((8, chans), F32)

    proj = take(proj_ref, core)
    ext_ref[8 : 8 + rows, :] = proj[:, wide : wide + chans].astype(F32)
    pre = conv_ref[CONV : CONV + 1, :] + conv_ref[0:1, :] * ext_ref[5 : 5 + rows, :]
    for lag in range(1, CONV):
        pre = pre + conv_ref[lag : lag + 1, :] * ext_ref[5 + lag : 5 + lag + rows, :]
    ext_ref[0:8, :] = ext_ref[rows : rows + 8, :]
    act = pre * jax.nn.sigmoid(pre)
    x = act[:, :wide]
    b_low = act[:, wide : wide + NSTATE].astype(BF16)
    c_low = act[:, wide + NSTATE :].astype(BF16)

    _, step = steps_beside(own_steps(proj[:, wide + chans :], turned), head_ref)
    decay = -step * head_ref[1:2, :]
    lower = iota((rows, rows), 0) >= iota((rows, rows), 1)
    cum = mm_thirds(lower.astype(F32), decay)
    cum_t = jnp.transpose(cum)
    spread = head_spread(wide, 0)
    total = cum[rows - 1 : rows, :]
    step_wide = mm_low(step, spread)
    grown = mm_low(jnp.exp(cum), spread)
    ending_wide = mm_low(step * jnp.exp(total - cum), spread)
    kept = mm_exact(jnp.broadcast_to(jnp.exp(total), (8, LANES)), spread.astype(F32))[0:1, :]

    scores = mm_nt(c_low, b_low)
    weighted = x * step_wide
    weighted_low = weighted.astype(BF16)
    within = []
    for start, end in pairs(wide):
        both = weighted_low[:, start:end]
        parts = []
        for head in range(start // HD, end // HD):
            gap = cum[:, head : head + 1] - cum_t[head : head + 1, :]
            mixed = jnp.where(lower, jnp.exp(gap), 0.0) * scores
            parts.append(mm(mixed.astype(BF16), both))
        if len(parts) == 2:
            first = iota((rows, end - start), 1) < HD
            within.append(jnp.where(first, parts[0], parts[1]))
        else:
            within.append(parts[0])
    within = jnp.concatenate(within, axis=1)
    state = state_ref[...]
    enter_ref[0] = state
    carried = grown * mm(c_low, state.astype(BF16))
    y = within + carried + skip_ref[0:1, :] * x
    gate = proj[:, :wide].astype(F32)
    gated = (y * (gate * jax.nn.sigmoid(gate))).astype(BF16)
    if not with_sums:
        put(gated_ref, core, gated, 0, wide)
    else:
        gated_ref[...] = gated
        gated = gated.astype(F32)
        ones = jnp.ones((8, wide), BF16)
        product = gated * take(refs[0], core).astype(F32)
        squares = mm_nt(ones, (gated * gated).astype(BF16))
        product = mm_nt(ones, product.astype(BF16))
        refs[4][...] = jnp.where(iota((8, rows), 0) == 0, squares, product)
    put(y_ref, core, y.astype(BF16), 0, wide)
    state_ref[...] = state * kept + mm_tn(b_low, (x * ending_wide).astype(BF16))


def mix_forward(place, proj, conv_rows, head_rows, wide_rows, pulled=None):
    with_sums = pulled is not None
    length, width = proj.shape
    wide = wide_rows.shape[1]
    count = length // STRETCH
    whole = lambda shape: pl.BlockSpec(shape, lambda i, at: (0,) * len(shape))
    part = lambda cols: pl.BlockSpec((STRETCH, cols), lambda i, at: (i ^ (at[0] >> 1), 0))
    plain = pl.BlockSpec((STRETCH, wide), lambda i, at: (i, 0))
    return pl.pallas_call(
        functools.partial(mix_forward_kernel, with_sums=with_sums),
        grid_spec=pltpu.PrefetchScalarGridSpec(
            num_scalar_prefetch=1,
            grid=(count,),
            in_specs=[
                part(width),
                whole(conv_rows.shape),
                whole(head_rows.shape),
                whole(wide_rows.shape),
            ]
            + [part(wide)] * with_sums,
            out_specs=[
                plain if with_sums else part(wide),
                part(wide),
                pl.BlockSpec((1, NSTATE, wide), lambda i, at: (i, 0, 0)),
            ]
            + [pl.BlockSpec((8, STRETCH), lambda i, at: (0, i))] * with_sums,
            scratch_shapes=[
                pltpu.VMEM((NSTATE, wide), F32),
                pltpu.VMEM((STRETCH + 8, wide + BC), F32),
            ],
        ),
        out_shape=[
            jax.ShapeDtypeStruct((length, wide), BF16),
            jax.ShapeDtypeStruct((length, wide), BF16),
            jax.ShapeDtypeStruct((count, NSTATE, wide), F32),
        ]
        + [jax.ShapeDtypeStruct((8, length), F32)] * with_sums,
        compiler_params=pltpu.CompilerParams(
            dimension_semantics=("arbitrary",), vmem_limit_bytes=CAP
        ),
        cost_estimate=pl.CostEstimate(
            flops=length * wide * 18000, bytes_accessed=length * 6000, transcendentals=0
        ),
        name="mix_forward",
    )(place, proj, conv_rows, head_rows, wide_rows, *[pulled] * with_sums)


def mix_backward_kernel(
    place_ref,
    proj_ref,
    before_ref,
    y_ref,
    pulled_ref,
    kappa_ref,
    enter_ref,
    conv_ref,
    head_ref,
    wide_ref,
    *refs,
    as_rows,
):
    out_ref, conv_grad_ref, head_grad_ref, skip_grad_ref = refs[:4]
    dstate_ref, ext_ref, gext_ref, rows_ref = refs[-4:]
    core, turned = place_ref[0] & 1, place_ref[1]
    rows = proj_ref.shape[0]
    wide = y_ref.shape[1]
    chans = wide + BC
    turn = pl.program_id(0)

    @pl.when(turn == 0)
    def _():
        dstate_ref[...] = jnp.zeros_like(dstate_ref)
        gext_ref[rows : rows + 8, :] = jnp.zeros((8, chans), F32)
        conv_grad_ref[...] = jnp.zeros_like(conv_grad_ref)
        head_grad_ref[...] = jnp.zeros_like(head_grad_ref)
        skip_grad_ref[...] = jnp.zeros_like(skip_grad_ref)
        rows_ref[...] = jnp.zeros_like(rows_ref)

    before = before_ref[8:16, wide : wide + chans].astype(F32)
    ext_ref[0:8, :] = jnp.where(turn == pl.num_programs(0) - 1, 0.0, before)
    proj = take(proj_ref, core)
    ext_ref[8 : 8 + rows, :] = proj[:, wide : wide + chans].astype(F32)
    pre = conv_ref[CONV : CONV + 1, :] + conv_ref[0:1, :] * ext_ref[5 : 5 + rows, :]
    for lag in range(1, CONV):
        pre = pre + conv_ref[lag : lag + 1, :] * ext_ref[5 + lag : 5 + lag + rows, :]
    sig = logistic(pre)
    act = pre * sig
    slope = sig * (1.0 + pre * (1.0 - sig))
    x = act[:, :wide]
    x_low = x.astype(BF16)
    b_low = act[:, wide : wide + NSTATE].astype(BF16)
    c_low = act[:, wide + NSTATE :].astype(BF16)

    shifted, step = steps_of(own_steps(proj[:, wide + chans :], turned), head_ref)
    rate = head_ref[:, 1:2]
    decay = -step * rate
    lower = iota((rows, rows), 0) >= iota((rows, rows), 1)
    upper = iota((rows, rows), 0) <= iota((rows, rows), 1)
    cum_t = sum_rows(decay, upper)
    total = cum_t[:, rows - 1 : rows]
    cum = as_columns(cum_t, step, jnp.exp(cum_t), jnp.exp(total - cum_t))
    cum_low = cum.astype(BF16)
    step_wide = mm(cum_low, head_spread(wide, 8))
    grown = mm(cum_low, head_spread(wide, 16))
    to_end = mm(cum_low, head_spread(wide, 24))
    fold = head_fold(8, wide)
    fold_low = head_fold(16, wide).astype(BF16)
    kept = jnp.sum(jnp.where(fold, jnp.exp(total), 0.0), axis=0, keepdims=True)

    gate = proj[:, :wide].astype(F32)
    y = take(y_ref, core).astype(F32)
    gate_sig = logistic(gate)
    gate_act = gate * gate_sig
    gated = y * gate_act
    if as_rows:
        g_gated = take(pulled_ref, core).astype(F32)
        sums = jnp.transpose(kappa_ref[...])
        rho = lax.rsqrt(sums[:, 0:1] / DI + eps)
        kappa = rho * rho * rho * sums[:, 1:2] / DI
        g_gated = rho * g_gated - gated * kappa
        put(refs[4], core, (gated * rho).astype(BF16), 0, wide)
        copies = []
    else:
        copies = [refs[4], refs[5]]
        g_gated = take(pulled_ref, core).astype(F32)
        g_gated = g_gated - gated * take(kappa_ref, core)[:, 0:1].astype(F32)
    dy = g_gated * gate_act
    g_gate = g_gated * y * (gate_sig * (1.0 + gate * (1.0 - gate_sig)))
    put(out_ref, core, g_gate.astype(BF16), 0, wide)
    for copy_ref in copies[:1]:
        put(copy_ref, core, g_gate.astype(BF16), 0, wide)
    dy_low = dy.astype(BF16)
    skip_grad_ref[0:1, :] += jnp.sum(x * dy, axis=0, keepdims=True)

    scores_t = mm_nt(b_low, c_low)
    lane = iota((rows, LANES), 1)
    d_scores = jnp.zeros((rows, rows), F32)
    column = jnp.zeros((rows, LANES), F32)
    inner = []
    for start, end in pairs(wide):
        both_dy = dy_low[:, start:end]
        both_x = x_low[:, start:end]
        side = iota((rows, end - start), 1) // HD
        parts = []
        for head in range(start // HD, end // HD):
            gap = cum_t[head : head + 1, :] - cum[:, head : head + 1]
            fade = jnp.where(upper, jnp.exp(gap), 0.0)
            own = jnp.where(side == head - start // HD, both_x, jnp.zeros_like(both_x))
            faded = fade * mm_nt(own, both_dy)
            stepped = faded * cum[:, 8 + head : 9 + head]
            d_scores = d_scores + stepped
            parts.append(mm((scores_t * fade).astype(BF16), both_dy))
            column = jnp.where(
                lane == head, jnp.sum(scores_t * faded, axis=1, keepdims=True), column
            )
            rows_ref[head : head + 1, :] = jnp.sum(scores_t * stepped, axis=0, keepdims=True)
        if len(parts) == 2:
            inner.append(jnp.where(side == 0, parts[0], parts[1]))
        else:
            inner.append(parts[0])
    inner = jnp.concatenate(inner, axis=1)

    enter = enter_ref[0]
    enter_low = enter.astype(BF16)
    dstate = dstate_ref[...]
    dstate_low = dstate.astype(BF16)
    outer = to_end * mm(b_low, dstate_low)
    g_x = step_wide * (inner + outer) + wide_ref[0:1, :] * dy
    dy_grown = dy * grown
    dy_grown_low = dy_grown.astype(BF16)
    carried_sum = mm_nt(fold_low, (dy_grown * mm(c_low, enter_low)).astype(BF16))[0:8]
    outer_sum = mm_nt(fold_low, (x * outer).astype(BF16))[0:8]
    state_sum = jnp.sum(enter * dstate, axis=0, keepdims=True)
    state_sum = jnp.sum(jnp.where(fold, state_sum, 0.0), axis=1, keepdims=True)
    column = jnp.transpose(column)[0:8]
    step_outer = step * outer_sum
    g_cum = rows_ref[0:8, :] + carried_sum - step * column - step_outer
    g_total = jnp.sum(step_outer, axis=1, keepdims=True) + jnp.exp(total) * state_sum
    g_decay = sum_rows(g_cum, lower) + g_total
    scaled_decay = rate * g_decay
    g_raw = (column + outer_sum - scaled_decay) * jax.nn.sigmoid(shifted)
    head_grad_ref[:, 0:1] += jnp.sum(g_raw, axis=1, keepdims=True)
    head_grad_ref[:, 1:2] -= jnp.sum(step * scaled_decay, axis=1, keepdims=True)
    g_raw = pltpu.roll(as_columns(g_raw), lax.rem(LANES - turned, LANES), 1)
    put(out_ref, core, g_raw.astype(BF16), wide + chans, wide + chans + LANES)
    for copy_ref in copies[1:]:
        put(copy_ref, core, g_raw.astype(BF16), chans, chans + LANES)

    d_low = d_scores.astype(BF16)
    ending = (x * (step_wide * to_end)).astype(BF16)
    g_b = mm(d_low, c_low) + mm_nt(ending, dstate_low)
    g_c = mm_tn(d_low, b_low) + mm_nt(dy_grown_low, enter_low)
    dstate_ref[...] = dstate * kept + mm_tn(c_low, dy_grown_low)

    gext_ref[0:rows, :wide] = g_x * slope[:, :wide]
    gext_ref[0:rows, wide : wide + NSTATE] = g_b * slope[:, wide : wide + NSTATE]
    gext_ref[0:rows, wide + NSTATE :] = g_c * slope[:, wide + NSTATE :]
    g_pre = gext_ref[0:rows, :]
    current = ext_ref[8 : 8 + rows, :]
    g_in = jnp.zeros_like(g_pre)
    for lag in range(CONV):
        moved = gext_ref[3 - lag : 3 - lag + rows, :]
        g_in = g_in + conv_ref[lag : lag + 1, :] * moved
        conv_grad_ref[lag : lag + 1, :] += jnp.sum(current * moved, axis=0, keepdims=True)
    put(out_ref, core, g_in.astype(BF16), wide, wide + chans)
    for copy_ref in copies[1:]:
        put(copy_ref, core, g_in.astype(BF16), 0, chans)
    conv_grad_ref[CONV : CONV + 1, :] += jnp.sum(g_pre, axis=0, keepdims=True)
    gext_ref[rows : rows + 8, :] = gext_ref[0:8, :]


def mix_backward(place, proj, y, pulled, kappa, enter, conv_rows, head_rows, wide_rows, as_rows):
    length, width = proj.shape
    wide = wide_rows.shape[1]
    count = length // STRETCH
    whole = lambda shape: pl.BlockSpec(shape, lambda i, at: (0,) * len(shape))
    part = lambda cols: pl.BlockSpec((STRETCH, cols), lambda i, at: ((count - 1 - i) ^ (at[0] >> 1), 0))
    half = STRETCH // 2

    def last_rows(i, at):
        pair = jnp.maximum(count - 2 - i, 0) ^ (at[0] >> 1)
        block = 2 * pair + 1 - (at[0] & 1)
        return block * (half // 16) + half // 16 - 1, 0

    before = pl.BlockSpec((16, width), last_rows)
    turn = lambda i, at: (count - 1 - i) ^ (at[0] >> 1)
    if as_rows:
        scales = pl.BlockSpec((8, STRETCH), lambda i, at: (0, count - 1 - i))
    else:
        last = kappa.shape[1] // LANES - 1
        scales = pl.BlockSpec((STRETCH, LANES), lambda i, at: (turn(i, at), last))
    return pl.pallas_call(
        functools.partial(mix_backward_kernel, as_rows=as_rows),
        grid_spec=pltpu.PrefetchScalarGridSpec(
            num_scalar_prefetch=1,
            grid=(count,),
            in_specs=[
                part(width),
                before,
                part(wide),
                part(wide),
                scales,
                pl.BlockSpec((1, NSTATE, wide), lambda i, at: (count - 1 - i, 0, 0)),
                whole(conv_rows.shape),
                whole(head_rows.shape),
                whole(wide_rows.shape),
            ],
            out_specs=[
                part(width),
                whole((8, wide + BC)),
                whole((8, LANES)),
                whole((8, wide)),
            ]
            + ([part(wide)] if as_rows else [part(wide), part(width - wide)]),
            scratch_shapes=[
                pltpu.VMEM((NSTATE, wide), F32),
                pltpu.VMEM((STRETCH + 8, wide + BC), F32),
                pltpu.VMEM((STRETCH + 8, wide + BC), F32),
                pltpu.VMEM((8, STRETCH), F32),
            ],
        ),
        out_shape=[
            jax.ShapeDtypeStruct((length, width), BF16),
            jax.ShapeDtypeStruct((8, wide + BC), F32),
            jax.ShapeDtypeStruct((8, LANES), F32),
            jax.ShapeDtypeStruct((8, wide), F32),
        ]
        + [jax.ShapeDtypeStruct((length, wide), BF16)]
        + [jax.ShapeDtypeStruct((length, width - wide), BF16)] * (not as_rows),
        compiler_params=pltpu.CompilerParams(
            dimension_semantics=("arbitrary",), vmem_limit_bytes=CAP
        ),
        cost_estimate=pl.CostEstimate(
            flops=length * wide * 40000, bytes_accessed=length * 9000, transcendentals=0
        ),
        name="mix_backward",
    )(place, proj, proj, y, pulled, kappa, enter, conv_rows, head_rows, wide_rows)


def add_low(*terms):
    total = terms[0].astype(F32)
    for term in terms[1:]:
        total = total + term.astype(F32)
    return total.astype(BF16)


def rms(values):
    return lax.rsqrt(jnp.mean(values * values, axis=-1, keepdims=True) + eps)


def after(values, *others):
    return lax.optimization_barrier((values, others))[0]


def flip(values, axis):
    return lax.ppermute(values, axis, [(0, 1), (1, 0)])


def flip_both(values, names):
    return lax.ppermute(values, names, [(0, 3), (1, 2), (2, 1), (3, 0)])


def turn_back(own, near, far, residual, rho, grad, gate_rho, branch):
    rows, model = own.shape

    def kernel(own_ref, near_ref, far_ref, res_ref, rho_ref, grad_ref, gate_ref, br_ref, *refs):
        grad_out, sent_out = refs
        weighed = own_ref[...].astype(F32) + near_ref[...].astype(F32) + far_ref[...].astype(F32)
        res, rho, gate = res_ref[...], rho_ref[...], gate_ref[...]
        mean = jnp.sum(weighed * res, axis=1, keepdims=True) / model
        total = grad_ref[...].astype(F32) + rho * weighed - res * (rho * rho * rho * mean)
        grad_out[...] = total
        pulled = total * gate
        kappa = gate * gate * jnp.sum(pulled * br_ref[...], axis=1, keepdims=True) / DI
        sent_out[:, :model] = pulled.astype(BF16)
        sent_out[:, model:] = jnp.broadcast_to(kappa, (rows, LANES)).astype(BF16)

    return pl.pallas_call(
        kernel,
        in_specs=all_vmem(8),
        out_specs=all_vmem(2),
        out_shape=[
            jax.ShapeDtypeStruct((rows, model), F32),
            jax.ShapeDtypeStruct((rows, model + LANES), BF16),
        ],
        compiler_params=pltpu.CompilerParams(vmem_limit_bytes=CAP),
        name="turn_back",
    )(own, near, far, residual, rho, grad, gate_rho, branch)


class Axes:
    def __init__(self, seq, fsdp):
        between = tuple(f"b{i}" for i in range((seq // 4).bit_length() - 1))
        before = tuple(f"p{i}" for i in range((fsdp // 2).bit_length() - 1))
        self.seq = ("a",) + between + ("c",)
        self.fsdp = before + ("q",)
        self.every = self.seq + self.fsdp
        self.links = ("a",) + between
        self.team = self.seq
        self.copies = self.fsdp

    def bits(self, names, at):
        value = 0
        for spot, name in enumerate(names):
            if at >> (len(names) - 1 - spot) & 1:
                value |= 1 << (len(self.every) - 1 - self.every.index(name))
        return value

    def at(self, me, r, k, relative):
        if relative:
            me = me ^ self.bits(self.copies, r)
        else:
            me = me & ~self.bits(self.copies, -1) | self.bits(self.copies, r)
        return me & ~self.bits(self.team, -1) | self.bits(self.team, k)


def all_vmem(count):
    return [pl.BlockSpec(memory_space=pltpu.VMEM)] * count


SMEM = pl.BlockSpec(memory_space=pltpu.SMEM)


def split_in(axes, weights, gain, spare, layer):
    team = 2 ** len(axes.team)
    depth, columns = weights.shape[1:]
    wide = DI // team
    parts = 2 + 3 * LANES // wide

    def kernel(weight_ref, gain_ref, spare_ref, out_ref):
        scale = gain_ref[...].astype(F32)
        tail = (weight_ref[0, :, 2 * DI :].astype(F32) * scale).astype(BF16)
        tail = jnp.concatenate([tail, spare_ref[...]], axis=1)
        for k in range(team):
            for part in range(2):
                base = (1 - part) * DI + k * wide
                cut = weight_ref[0, :, base : base + wide].astype(F32)
                out_ref[k, part] = (cut * scale).astype(BF16)
            for part in range(2, parts):
                out_ref[k, part] = tail[:, (part - 2) * wide : (part - 1) * wide]

    whole = lambda shape: pl.BlockSpec(shape, lambda i: (0,) * len(shape))
    return pl.pallas_call(
        kernel,
        grid=(1,),
        in_specs=[
            pl.BlockSpec((1, depth, columns), lambda i: (layer, 0, 0)),
            whole((depth, 1)),
            whole(spare.shape),
        ],
        out_specs=whole((team, parts, depth, wide)),
        out_shape=jax.ShapeDtypeStruct((team, parts, depth, wide), BF16),
        compiler_params=pltpu.CompilerParams(vmem_limit_bytes=CAP),
        name="split_in",
    )(weights, gain[:, None], spare)


def columns_of(part, wide):
    return (1 - part if part < 2 else part) * wide


def join_in(axes, place, lists, relative):
    copies, team = len(lists), 2 ** len(axes.team)
    parts = len(lists[0]) // team
    depth, wide = lists[0][0][0].shape[-2:]
    rows = copies * team * depth
    extra = min(depth, 32)
    if depth % 16:
        flat = jnp.stack([jnp.stack([array[index] for array, index in row]) for row in lists])
        flat = flat.reshape(copies * team, parts, depth, wide)
        flat = jnp.concatenate(
            [flat[:, 1], flat[:, 0]] + [flat[:, part] for part in range(2, parts)], axis=-1
        )
        at = [axes.at(place[2], r, k, relative) for r in range(copies) for k in range(team)]
        flat = jnp.zeros_like(flat).at[jnp.stack(at)].set(flat)
        return flat.reshape(rows, -1), flat[:, :extra, -LANES:]

    arrays = []
    for row in lists:
        for array, _ in row:
            if not any(array is known for known in arrays):
                arrays.append(array)
    which = lambda array: next(i for i, known in enumerate(arrays) if known is array)

    def kernel(place_ref, *refs):
        out_ref, spare_ref = refs[-2:]
        for r in range(copies):
            for k in range(team):
                spot = axes.at(place_ref[2], r, k, relative)
                at = pl.ds(pl.multiple_of(spot * depth, 16), depth)
                for part in range(parts):
                    array, index = lists[r][parts * k + part]
                    base = columns_of(part, wide)
                    out_ref[at, base : base + wide] = refs[which(array)][index]
                index = index if isinstance(index, tuple) else (index,)
                index += (slice(0, extra), slice(wide - LANES, wide))
                spare_ref[spot] = refs[which(array)][index]

    return pl.pallas_call(
        kernel,
        in_specs=[SMEM] + all_vmem(len(arrays)),
        out_specs=all_vmem(2),
        out_shape=[
            jax.ShapeDtypeStruct((rows, parts * wide), BF16),
            jax.ShapeDtypeStruct((copies * team, extra, LANES), BF16),
        ],
        compiler_params=pltpu.CompilerParams(vmem_limit_bytes=CAP),
        name="join_in",
    )(place, *arrays)


def cut_in(axes, place, grad, spare, depth, wide, relative):
    copies, team = 2 ** len(axes.copies), 2 ** len(axes.team)
    parts = grad.shape[1] // wide
    pairs_at = [(r, k) for r in range(copies) for k in range(team)]
    if spare is not None:
        extra, room = spare.shape[1:]
    if depth % 16:
        flat = grad.reshape(copies * team, depth, -1)
        if spare is not None:
            flat = flat.at[:, :extra, -room:].set(spare)
        at = jnp.stack([axes.at(place[2], r, k, relative) for r, k in pairs_at])
        flat = jnp.take(flat, at, axis=0).reshape(copies, team, depth, parts, wide)
        flat = flat.transpose(0, 1, 3, 2, 4).reshape(copies, team * parts, depth, wide)
        return [flat[r] for r in range(copies)]

    def kernel(place_ref, grad_ref, *refs):
        out_refs = refs[-copies:]
        for r, k in pairs_at:
            spot = axes.at(place_ref[2], r, k, relative)
            rows = pl.ds(pl.multiple_of(spot * depth, 16), depth)
            for part in range(parts):
                out_refs[r][parts * k + part] = grad_ref[rows, part * wide : (part + 1) * wide]
            if spare is not None:
                out_refs[r][parts * k + parts - 1, 0:extra, wide - room :] = refs[0][spot]

    given = [] if spare is None else [spare]
    return pl.pallas_call(
        kernel,
        in_specs=[SMEM] + all_vmem(1 + len(given)),
        out_specs=all_vmem(copies),
        out_shape=[jax.ShapeDtypeStruct((team * parts, depth, wide), BF16)] * copies,
        compiler_params=pltpu.CompilerParams(vmem_limit_bytes=CAP),
        name="cut_in",
    )(place, grad, *given)


def join_out(axes, place, blocks, grad):
    copies = len(blocks)
    count, depth, wide = blocks[0].shape
    each, model = grad.shape[0] // copies, grad.shape[1]
    more = (each // depth) * (model // wide)

    def kernel(place_ref, grad_ref, *refs):
        block_refs, out_refs = refs[:copies], refs[copies:]
        for r in range(copies):
            out_refs[r][0:count] = block_refs[r][...]
            copy = (place_ref[2] & axes.bits(axes.copies, -1)) ^ axes.bits(axes.copies, r)
            for at in range(more):
                row, column = at // (model // wide), at % (model // wide)
                first = copy * each + row * depth
                out_refs[r][count + at] = grad_ref[
                    pl.ds(pl.multiple_of(first, 16), depth), column * wide : (column + 1) * wide
                ]

    return pl.pallas_call(
        kernel,
        in_specs=[SMEM] + all_vmem(1 + copies),
        out_specs=all_vmem(copies),
        out_shape=[jax.ShapeDtypeStruct((count + more, depth, wide), BF16)] * copies,
        compiler_params=pltpu.CompilerParams(vmem_limit_bytes=CAP),
        name="join_out",
    )(place, grad, *blocks)


def finish_in(axes, grads, weight, gain):
    layers, depth, columns = weight.shape
    team = 2 ** len(axes.team)
    wide = DI // team
    parts = grads[0][1].shape[1]
    room = (parts - 1) * wide - (columns - 2 * DI)

    def kernel(weight_ref, gain_ref, *refs):
        grad_ref, sum_ref, spare_ref = refs[-3:]
        for layer in range(layers):
            gate_ref, rest_ref = refs[2 * layer : 2 * layer + 2]
            scale = gain_ref[layer].astype(F32)
            tails = []
            for part in range(1, parts):
                tail = rest_ref[0, part].astype(F32)
                for k in range(1, team):
                    tail = tail + rest_ref[k, part].astype(F32)
                tails.append(tail)
            tail = jnp.concatenate(tails, axis=1)
            spare_ref[layer] = tail[:, columns - 2 * DI :]
            tail = tail[:, : columns - 2 * DI]
            grad_ref[layer, :, 2 * DI :] = tail * scale
            total = jnp.sum(tail * weight_ref[layer, :, 2 * DI :].astype(F32), 1, keepdims=True)
            for k in range(team):
                for base, values in ((0, gate_ref[k, 0]), (DI, rest_ref[k, 0])):
                    values = values.astype(F32)
                    spot = slice(base + k * wide, base + (k + 1) * wide)
                    grad_ref[layer, :, spot] = values * scale
                    total = total + jnp.sum(
                        values * weight_ref[layer, :, spot].astype(F32), 1, keepdims=True
                    )
            sum_ref[layer] = jnp.broadcast_to(total, (depth, LANES))

    grads, sums, spares = pl.pallas_call(
        kernel,
        in_specs=all_vmem(2 + 2 * layers),
        out_specs=all_vmem(3),
        out_shape=[
            jax.ShapeDtypeStruct((layers, depth, columns), F32),
            jax.ShapeDtypeStruct((layers, depth, LANES), F32),
            jax.ShapeDtypeStruct((layers, depth, room), F32),
        ],
        compiler_params=pltpu.CompilerParams(vmem_limit_bytes=CAP),
        name="finish_in",
    )(weight, gain[..., None], *[part for pair in grads for part in pair])
    return grads, sums[:, :, 0], spares


def together(*values):
    return lax.optimization_barrier(values)


def copies_start(axes, whole):
    slow, fast = axes.copies
    return whole, flip(whole, fast), flip(whole, slow)


def copies_corner(axes, parts):
    slow, fast = axes.copies
    whole, one, two = parts
    half = whole.shape[0] // 2
    return flip(one[:half], slow), flip(two[half:], fast)


def copies_whole_corner(axes, parts):
    return (flip(parts[1], axes.copies[0]),)


def copies_lists(parts, corner):
    count = parts[0].shape[0]
    each = count // len(corner)
    lists = [[(array, at) for at in range(count)] for array in parts]
    return lists + [[(corner[at // each], at % each) for at in range(count)]]


def sum_corner(axes, pieces):
    slow, fast = axes.copies
    half = pieces[3].shape[0] // 2
    return flip(pieces[3][:half], slow), flip(pieces[3][half:], fast)


def sum_sides(axes, pieces, corner):
    slow, fast = axes.copies
    half = pieces[0].shape[0] // 2
    to_fast = jnp.concatenate([add_low(pieces[1][:half], corner[0]), pieces[1][half:]], axis=0)
    to_slow = jnp.concatenate([pieces[2][:half], add_low(pieces[2][half:], corner[1])], axis=0)
    return flip(to_fast, fast), flip(to_slow, slow)


def sum_direct(axes, pieces):
    slow, fast = axes.copies
    return flip(pieces[1], fast), flip(pieces[2], slow), flip_both(pieces[3], axes.copies)


def gather_start(axes, rows):
    if len(axes.links) != 2:
        return (rows,)
    far, near = axes.links
    return rows, flip(rows, "c"), flip(rows, far), flip(rows, near)


def gather_corner(axes, parts):
    if len(axes.links) != 2:
        return parts, []
    rows, other, from_far, from_near = parts
    most = [rows, other, from_near, flip(from_near, "c"), from_far, flip(from_far, "c")]
    return (flip(from_far, axes.links[1]),), [jnp.concatenate(most, axis=0)]


def gather_end(axes, corner):
    if len(axes.links) != 2:
        whole = corner[0][None]
        for name in reversed(axes.links):
            whole = jnp.concatenate([whole, flip(whole, name)], axis=0)
        whole = jnp.stack([whole, flip(whole, "c")], axis=1)
        return whole.reshape(-1, corner[0].shape[1])
    return jnp.concatenate([corner[0], flip(corner[0], "c")], axis=0)


def core_sum(values, rows):
    both = values.reshape(-1, 2, rows, values.shape[-1])
    return both[:, 0] + flip(both[:, 1].astype(BF16), "c").astype(F32)


def scatter_corner(axes, rows_of, rows):
    team = 2 ** len(axes.team)
    if len(axes.links) != 2:
        return (core_sum(rows_of(0, team * rows, ()), rows),)
    corner = core_sum(rows_of(6 * rows, 8 * rows, ()), rows)[0]
    hop = flip(corner.astype(BF16), axes.links[1])
    sides = core_sum(rows_of(2 * rows, 6 * rows, corner), rows)
    return hop, sides, core_sum(rows_of(0, 2 * rows, corner), rows)[0]


def scatter_sides(axes, parts):
    if len(axes.links) != 2:
        whole = parts[0]
        for name in axes.links:
            half = whole.shape[0] // 2
            whole = add_low(whole[:half], flip(whole[half:], name))
        return (whole[0],)
    far, near = axes.links
    hop, sides, own = parts
    return own, flip(sides[0].astype(BF16), near), flip(add_low(sides[1], hop), far)


def add_all(parts):
    total = parts[0].astype(F32)
    for part in parts[1:]:
        total = total + part.astype(F32)
    return total


def local(
    axes,
    tokens,
    cotangent,
    norm_gain,
    in_weight,
    conv_kernel,
    conv_shift,
    dt_bias,
    a_log,
    skip_gain,
    gate_gain,
    out_weight,
):
    layers, depth, columns = in_weight.shape
    rows = tokens.shape[1]
    model = tokens.shape[2]
    heads = dt_bias.shape[1]
    wide = heads * HD
    team = 2 ** len(axes.team)
    copies = 2 ** len(axes.copies)
    me = lax.axis_index(axes.team)
    all_at = lax.axis_index(axes.every)
    place = jnp.stack([me, lax.rem(LANES - me * heads, LANES), all_at]).astype(jnp.int32)

    n_conv = conv_shift.shape[1]
    room = 3 * LANES - (columns - 2 * DI)
    cuts = [(at, min(at + room, n_conv)) for at in range(0, n_conv, room)]
    taps = CONV + 1
    conv = jnp.concatenate([conv_kernel, conv_shift[:, None]], axis=1).reshape(-1, n_conv)
    conv = [jnp.pad(conv[:, at:end], ((0, 0), (0, room - end + at))) for at, end in cuts]
    conv = jnp.concatenate(conv, axis=0)
    spare = jnp.pad(conv, ((0, depth - conv.shape[0]), (0, 0)))

    def team_swap(blocks):
        return lax.all_to_all(blocks, axes.team, split_axis=0, concat_axis=0)

    def in_blocks(layer, start):
        blocks = split_in(axes, in_weight, after(norm_gain[layer], start), spare, layer)
        return team_swap(blocks).reshape(-1, depth, wide)

    def in_columns(blocks):
        got = lax.all_gather(blocks, axes.copies)
        lists = [[(got, (r, k)) for k in range(blocks.shape[0])] for r in range(copies)]
        return join_in(axes, place, lists, False)

    def out_rows(layer, start):
        gain = after(gate_gain[layer], start)
        mine = out_weight[layer].astype(F32) * gain.astype(F32)[:, None]
        return lax.all_gather(mine.astype(BF16), axes.copies, axis=0, tiled=True)

    paired = len(axes.copies) == 2
    assert layers == 2

    weight_out_0 = out_rows(0, tokens)
    blocks = in_blocks(0, tokens)
    parts = blocks.shape[0] // team
    residual_0 = tokens[0].astype(F32)
    rho_0 = rms(residual_0)
    blocks, sent = together(blocks, (residual_0 * rho_0).astype(BF16))
    gathered = gather_start(axes, sent)
    if paired:
        copied, gathered = together(copies_start(axes, blocks), gathered)
    hops, pieces_0 = gather_corner(axes, gathered)
    cot = gather_start(axes, after(cotangent[0], gathered))
    if paired:
        corner = copies_corner(axes, copied)
        corner, hops, weight_out_0 = together(corner, hops, weight_out_0)
        weight_in_0, beside = join_in(axes, place, copies_lists(copied, corner), True)
    else:
        weight_in_0, beside = in_columns(blocks)
    last = gather_end(axes, hops)
    last, cot = together(last, cot)
    pieces_0 = pieces_0 + [last]
    proj_0 = [mm(piece, weight_in_0).astype(BF16) for piece in pieces_0]
    proj_0 = jnp.concatenate(proj_0, axis=0)

    conv = beside[:, : conv.shape[0], LANES - room :]
    conv = conv.reshape(-1, len(cuts), layers * taps, room).transpose(0, 2, 1, 3)
    conv = conv.reshape(-1, layers * taps, len(cuts) * room)[:, :, :n_conv]
    conv = conv.reshape(-1, layers, taps, n_conv)
    conv = conv.transpose(1, 2, 0, 3).reshape(layers, CONV + 1, -1).astype(F32)
    conv = jnp.pad(conv, ((0, 0), (0, 7 - CONV), (0, 0)))
    conv = jnp.concatenate(
        [lax.dynamic_slice_in_dim(conv, me * wide, wide, 2), conv[:, :, DI:]], axis=2
    )
    head = jnp.stack([dt_bias, a_log, skip_gain], axis=1)
    skip = jnp.pad(jnp.repeat(head[:, 2:], HD, axis=2), ((0, 0), (0, 7), (0, 0)))
    head = jnp.stack([head[:, 0], jnp.exp(head[:, 1])], axis=1)
    head_rows = jnp.pad(head, ((0, 0), (0, 6), (0, LANES - heads)))
    head = jnp.pad(head.transpose(0, 2, 1), ((0, 0), (0, 8 - heads), (0, LANES - 2)))

    blocks = in_blocks(1, hops)
    gated_0, y_0, enter_0 = mix_forward(place, proj_0, conv[0], head_rows[0], skip[0])
    cot_hops, cot = gather_corner(axes, cot)
    (gated_0, y_0, enter_0), blocks, cot_hops = together((gated_0, y_0, enter_0), blocks, cot_hops)
    cot = cot + [gather_end(axes, cot_hops)]
    weight_out_1 = out_rows(1, gated_0)

    def branch_rows(begin, end, others):
        cut = after(gated_0, others)[begin:end]
        squares = jnp.sum(jnp.square(cut.astype(F32)), axis=1, keepdims=True)
        squares = jnp.broadcast_to(squares, (end - begin, LANES))
        return jnp.concatenate([mm(cut, weight_out_0), squares], axis=1)

    got = together(*scatter_corner(axes, branch_rows, rows))
    got = scatter_sides(axes, got)
    if paired:
        got, copied = together(got, copies_start(axes, blocks))
    got = add_all(got)
    branch_0 = got[:, :model]
    gate_rho_0 = lax.rsqrt(got[:, model : model + 1] / DI + eps)

    residual_1 = residual_0 + gate_rho_0 * branch_0
    rho_1 = rms(residual_1)
    gathered = gather_start(axes, (residual_1 * rho_1).astype(BF16))
    g_scaled = jnp.concatenate([mm_nt(piece, weight_out_1).astype(BF16) for piece in cot], axis=0)
    if paired:
        gathered, corner, g_scaled = together(
            gathered, copies_whole_corner(axes, copied), g_scaled
        )
        weight_in_1 = join_in(axes, place, copies_lists(copied, corner), True)[0]
    else:
        weight_in_1 = in_columns(blocks)[0]
    hops, pieces_1 = gather_corner(axes, gathered)
    proj_1 = [mm(piece, weight_in_1).astype(BF16) for piece in pieces_1]
    hops, proj_1 = together(hops, proj_1)
    last = gather_end(axes, hops)
    pieces_1 = pieces_1 + [last]
    proj_1 = jnp.concatenate(proj_1 + [mm(last, weight_in_1).astype(BF16)], axis=0)
    gated_1, y_1, enter_1, sums = mix_forward(
        place, proj_1, conv[1], head_rows[1], skip[1], g_scaled
    )

    sums = sums + flip(sums, "c")
    if len(axes.links) == 2:
        far, near = axes.links
        sums = sums + flip(sums, far) + flip(sums, near) + flip_both(sums, axes.links)
    else:
        for name in axes.links:
            sums = sums + flip(sums, name)

    branch_1 = mm(gated_1, weight_out_1).astype(BF16)
    sums, branch_1 = together(sums, branch_1)
    branch_1 = lax.psum_scatter(branch_1, axes.team, scatter_dimension=0, tiled=True)
    outs = mix_backward(
        place, proj_1, y_1, g_scaled, sums, enter_1, conv[1], head[1], skip[1], True
    )
    g_proj, g_conv, g_head, g_skip, scaled_1 = outs
    got_1 = jnp.concatenate(after(cot, g_proj), axis=0)
    normed = jnp.concatenate(after(pieces_1, g_proj), axis=0)

    def spare_rows(g_conv, g_head, g_skip):
        g_conv = jnp.concatenate(
            [
                lax.dynamic_update_slice_in_dim(
                    jnp.zeros((taps, DI), F32), g_conv[:taps, :wide], me * wide, 1
                ),
                g_conv[:taps, wide:],
            ],
            axis=1,
        )
        g_conv = g_conv.reshape(taps, -1, n_conv).transpose(1, 0, 2)
        g_conv = [
            jnp.pad(g_conv[..., at:end], ((0, 0), (0, 0), (0, room - end + at)))
            for at, end in cuts
        ]
        g_head = jnp.stack(
            [g_head[:heads, 0], g_head[:heads, 1], jnp.sum(g_skip[0].reshape(heads, HD), 1)]
        )
        g_head = jnp.pad(g_head, ((0, 0), (0, room - heads)))
        sharers = team * copies // team
        owner = jnp.arange(team * copies) // sharers == me
        g_head = jnp.where(owner[:, None, None], g_head, 0.0)
        spare = jnp.concatenate(g_conv + [g_head], axis=1)
        more = -spare.shape[1] % 16 if depth % 16 == 0 else 0
        return jnp.pad(spare, ((0, 0), (0, more), (0, 0))).astype(BF16)

    def head_sums(g_head, g_skip):
        skips = jnp.sum(g_skip[0].reshape(heads, HD), 1)
        return jnp.stack([g_head[:heads, 0], g_head[:heads, 1], skips])

    head_1 = head_sums(g_head, g_skip)

    def in_gradient(normed, g_proj, beside, quick):
        spare = None if beside is None else spare_rows(*beside)
        g_in = mm_tn(normed, g_proj).astype(BF16)
        return cut_in(axes, place, g_in, spare, depth, wide, quick)

    def copies_scatter(values):
        return lax.psum_scatter(jnp.stack(values), axes.copies, scatter_dimension=0)

    def owned(summed):
        return team_swap(summed.reshape(team, -1, depth, wide))

    def weighed_rows(g_proj, weight_in):
        def make(begin, end, others):
            return mm_nt(after(g_proj, others)[begin:end], weight_in)

        return make

    weighed = scatter_corner(axes, weighed_rows(g_proj, weight_in_1), rows)
    weighed, branch_1 = together(weighed, branch_1)
    weighed = scatter_sides(axes, weighed)
    g_late = after(g_proj, weighed[0])
    blocks = in_gradient(normed, g_late, (g_conv, g_head, g_skip), False)
    weighed, blocks = together(weighed, blocks)
    summed = copies_scatter(blocks)
    squares = lax.dynamic_slice_in_dim(sums, me * rows, rows, 1)[0][:, None]
    out = (residual_1 + lax.rsqrt(squares / DI + eps) * branch_1.astype(F32)).astype(BF16)
    if len(weighed) == 1:
        weighed = weighed + (jnp.zeros_like(weighed[0]),) * 2

    grad, sent = turn_back(
        *weighed, residual_1, rho_1, cotangent[0], gate_rho_0, branch_0
    )
    gathered = gather_start(axes, sent)
    g_out = mm_tn(scaled_1, got_1).astype(BF16)
    gathered, g_out = together(gathered, g_out)
    g_out_1 = lax.psum_scatter(g_out, axes.copies, scatter_dimension=0, tiled=True)
    hops, pieces = gather_corner(axes, gathered)
    g_scaled = [mm_nt(piece[:, :model], weight_out_0).astype(BF16) for piece in pieces]
    normed = jnp.concatenate(after(pieces_0, gathered), axis=0)
    hops, g_scaled, normed = together(hops, g_scaled, normed)
    last = gather_end(axes, hops)
    pieces = pieces + [last]
    g_scaled = g_scaled + [mm_nt(last[:, :model], weight_out_0).astype(BF16)]
    g_scaled = jnp.concatenate(g_scaled, axis=0)
    kappa = jnp.concatenate([piece[:, model:] for piece in pieces], axis=0)
    kappa = after(kappa, summed)
    outs = mix_backward(
        place, proj_0, y_0, g_scaled, kappa, enter_0, conv[0], head[0], skip[0], False
    )
    outs, owned_1 = together(outs, owned(summed))
    g_proj, g_conv, g_head, g_skip, g_gate, g_rest = outs
    owned_1 = owned_1[:, :1], owned_1[:, 1:]
    got = jnp.concatenate([piece[:, :model] for piece in after(pieces, g_proj)], axis=0)
    beside = g_conv, g_head, g_skip
    head_grad = lax.psum(jnp.stack([head_sums(g_head, g_skip), head_1]), axes.copies)
    g_out = mm_tn(gated_0, got).astype(BF16)
    if paired:
        gates = in_gradient(normed, g_gate, None, True)
        gates = join_out(axes, place, gates, g_out)
        g_proj = after(g_proj, gates)
    weighed = scatter_corner(axes, weighed_rows(g_proj, weight_in_0), rows)
    if paired:
        weighed, gate_parts = together(weighed, sum_direct(axes, gates))
        weighed = scatter_sides(axes, weighed)
        rests = in_gradient(normed, after(g_rest, gate_parts), beside, True)
        corner = sum_corner(axes, rests)
        gates = add_low(gates[0], *gate_parts)
        g_out_0 = gates[team:].reshape(-1, model // wide, depth, wide)
        g_out_0 = g_out_0.transpose(0, 2, 1, 3).reshape(-1, model)
        gates = owned(gates[:team])
        sides = sum_sides(axes, rests, corner)
        rests = owned(add_low(rests[0], *sides))
    else:
        weighed = scatter_sides(axes, weighed)
        gates = owned(copies_scatter(in_gradient(normed, g_gate, None, False)))
        rests = owned(copies_scatter(in_gradient(normed, g_rest, beside, False)))
        g_out_0 = lax.psum_scatter(g_out, axes.copies, scatter_dimension=0, tiled=True)
    owned_0 = gates, rests
    weighed = add_all(weighed)
    mean = jnp.mean(weighed * residual_0, axis=1, keepdims=True)
    grad = grad + rho_0 * weighed - residual_0 * (rho_0 * rho_0 * rho_0 * mean)

    grad_in, grad_norm, spare = finish_in(axes, [owned_0, owned_1], in_weight, norm_gain)
    grad_out = jnp.stack([g_out_0, g_out_1]).astype(F32)
    grad_gate = jnp.sum(grad_out * out_weight.astype(F32), axis=2)
    grad_out = grad_out * gate_gain.astype(F32)[:, :, None]

    conv_grad = [
        spare[:, at * taps : (at + 1) * taps, : end - start] for at, (start, end) in enumerate(cuts)
    ]
    conv_grad = jnp.concatenate(conv_grad, axis=2)
    return (
        out[None],
        grad[None],
        grad_norm,
        grad_in,
        conv_grad[:, :CONV],
        conv_grad[:, CONV],
        head_grad[:, 0],
        head_grad[:, 1],
        head_grad[:, 2],
        grad_gate,
        grad_out,
    )


def solution(mesh):
    axes = Axes(mesh.shape["seq"], mesh.shape["fsdp"])
    fine = Mesh(mesh.devices.reshape((2,) * len(axes.every)), axes.every)
    acts = P(axes.fsdp, axes.seq, None)
    flat = P(None, axes.every)
    rows = P(None, axes.every, None)
    taps = P(None, None, axes.every)
    head = P(None, axes.seq)
    return jax.shard_map(
        functools.partial(local, axes),
        mesh=fine,
        in_specs=(acts, acts, flat, rows, taps, flat, head, head, head, flat, rows),
        out_specs=(acts, acts, flat, rows, taps, flat, head, head, head, flat, rows),
        check_vma=False,
    )
```
